128 devices in a mesh: fsdp: 32 (over x, y, core), tp: 4 (over z).
Axes of the slice: x: 4, y: 4, z: 4, core: 2. Of those that a mesh axis runs over, the one named last changes fastest.
Arguments:
- tokens: bfloat16 [16384, 1024], P(('fsdp', 'tp')), may hold values from -6 to 6
- doc_start: int32 [16384], P('fsdp'), may hold values from 0 to 16383, as said below
- norm_gains: float32 [2, 1024], P(None, ('fsdp', 'tp')), may hold values from 0.1 to 1.9
- norm_biases: float32 [2, 1024], P(None, ('fsdp', 'tp')), may hold values from -1.8 to 1.8
- out_biases: float32 [2, 1024], P(None, ('fsdp', 'tp')), may hold values from -1.8 to 1.8
- w_qkv: bfloat16 [3, 1024, 1024], P(None, 'fsdp', 'tp'), may hold values from -0.1875 to 0.1875
- b_qv: bfloat16 [2, 4, 256], P(None, 'tp', 'fsdp'), may hold values from -1.796875 to 1.796875
- w_out: bfloat16 [1024, 1024], P('tp', 'fsdp'), may hold values from -4 to 4
- w_up: bfloat16 [1024, 4096], P('fsdp', 'tp'), may hold values from -0.1875 to 0.1875
- b_up: bfloat16 [4, 1024], P('tp', 'fsdp'), may hold values from -1.796875 to 1.796875
- w_down: bfloat16 [4096, 1024], P('tp', 'fsdp'), may hold values from -0.09375 to 0.09375
- out_grad: bfloat16 [16384, 1024], P(('fsdp', 'tp')), may hold values from -6 to 6
Outputs:
- output: float32 [16384, 1024], P(('fsdp', 'tp'))
- grad_tokens: float32 [16384, 1024], P(('fsdp', 'tp'))
- grad_norm_gains: float32 [2, 1024], P(None, ('fsdp', 'tp'))
- grad_norm_biases: float32 [2, 1024], P(None, ('fsdp', 'tp'))
- grad_out_biases: float32 [2, 1024], P(None, ('fsdp', 'tp'))
- grad_w_qkv: float32 [3, 1024, 1024], P(None, 'fsdp', 'tp')
- grad_b_qv: float32 [2, 4, 256], P(None, 'tp', 'fsdp')
- grad_w_out: float32 [1024, 1024], P('tp', 'fsdp')
- grad_w_up: float32 [1024, 4096], P('fsdp', 'tp')
- grad_b_up: float32 [4, 1024], P('tp', 'fsdp')
- grad_w_down: float32 [4096, 1024], P('tp', 'fsdp')
The draws below stay inside these ranges and needn't reach their ends.
Inputs may be any that keep to these rules, and one draw needn't show every extreme that they name: doc_start[i] is the first position of the document of token i: documents are runs of consecutive tokens, doc_start never falls, i - 2000 < doc_start[i] <= i, and no document crosses a multiple of 4096. The last token of every sequence is a document of its own; every other document has 200 to 2000 tokens, except the one just before that last token, which may be shorter; every sequence holds a document of exactly 2000 tokens.
All inputs are finite; a program needn't handle non-finite values.
Results may differ from the reference program's by a relative error of at most 0.035.
Values may be sent and summed in bfloat16 or wider, within the bound.
No kernel may reach another device: no remote copies, remote signals or barrier semaphores. Data moves between devices by JAX's collectives and lax.ppermute only.
A program may use at most 128 MiB of HBM per device.

```python
from functools import partial
import jax
import jax.numpy as jnp
from jax import lax

D = 1024
HEADS = 16
HEAD_DIM = 64
FF = 4096
DOC_MIN = 200
DOC_MAX = 2000
SEQ = 4096
TOKENS = 16384
N_TP = 4


def draw_doc_start(key, part):
    key = jax.random.fold_in(key, 7)
    seq_count = TOKENS // SEQ
    doc_count = SEQ // DOC_MIN + 2
    subkeys = jax.random.split(key, 2)
    doc_lengths = jax.random.randint(subkeys[0], (seq_count, doc_count), DOC_MIN, DOC_MAX + 1).astype(jnp.int32)
    longest_at = jax.random.randint(subkeys[1], (seq_count,), 0, 2).astype(jnp.int32)
    slots = jnp.arange(doc_count, dtype=jnp.int32)
    doc_lengths = jnp.where(slots[None, :] == longest_at[:, None], DOC_MAX, doc_lengths).astype(jnp.int32)
    doc_ends = jnp.cumsum(doc_lengths, axis=1).astype(jnp.int32)
    doc_firsts = (doc_ends - doc_lengths).astype(jnp.int32)
    places = jnp.arange(SEQ, dtype=jnp.int32)
    local_start = jnp.max(jnp.where(doc_firsts[:, None, :] <= places[None, :, None], doc_firsts[:, None, :], 0), axis=-1)
    local_start = jnp.where(places[None, :] == SEQ - 1, SEQ - 1, local_start).astype(jnp.int32)
    offsets = jnp.arange(seq_count, dtype=jnp.int32)[:, None] * SEQ
    return (local_start + offsets).reshape(TOKENS).astype(jnp.int32)


def levels(key, extent, shards, smallest, top_value):
    level, own = 1.0, jax.random.fold_in(key, 6)
    for axis_at, blocks in shards:
        heights = jnp.exp(jax.random.uniform(jax.random.fold_in(own, axis_at), (blocks,), jnp.float32, smallest / len(shards), top_value / len(shards)))
        level = level * jnp.repeat(heights, extent[axis_at] // blocks).reshape([-1 if axis == axis_at else 1 for axis in range(len(extent))])
    return level


def normal_values(rng, dims, scale, bound, shards=(), kind=jnp.bfloat16):
    entries = jax.random.normal(rng, dims, jnp.float32) * scale
    if len(shards) > 0:
        entries = levels(rng, dims, shards, -0.22, 0.18) * entries
    return jnp.clip(entries, min=-bound, max=bound).astype(kind)


def setup_inputs(seed: int = 0) -> dict:
    splits = jax.random.split(jax.random.key(seed), 13)
    tokens = normal_values(splits[0], (TOKENS, D), 1.0, 6.0, ((0, 128),))
    doc_start = draw_doc_start(jax.random.fold_in(splits[12], 71), 0)
    norm_gains = jnp.clip(1.0 + 0.18 * jax.random.normal(splits[2], (2, D), jnp.float32), 0.1, 1.9)
    norm_biases = normal_values(splits[3], (2, D), 0.3, 1.8, ((1, 128),), jnp.float32)
    out_biases = normal_values(splits[4], (2, D), 0.3, 1.8, ((1, 128),), jnp.float32)
    w_qkv = normal_values(splits[5], (3, D, D), D ** -0.5, 0.1875, ((1, 32), (2, 4)))
    b_qv = normal_values(splits[6], (2, N_TP, D // N_TP), 0.3, 1.796875, ((1, 4), (2, 32)))
    w_out = normal_values(splits[7], (D, D), 2 ** -0.5, 4.0, ((0, 4), (1, 32)))
    w_up = normal_values(splits[8], (D, FF), D ** -0.5, 0.1875, ((0, 32), (1, 4)))
    b_up = normal_values(splits[9], (N_TP, FF // N_TP), 0.3, 1.796875, ((0, 4), (1, 32)))
    w_down = normal_values(splits[10], (FF, D), FF ** -0.5, 0.09375, ((0, 4), (1, 32)))
    out_grad = normal_values(splits[11], (TOKENS, D), 1.0, 6.0, ((0, 128),))
    return {"tokens": tokens, "doc_start": doc_start, "norm_gains": norm_gains, "norm_biases": norm_biases, "out_biases": out_biases, "w_qkv": w_qkv, "b_qv": b_qv, "w_out": w_out, "w_up": w_up, "b_up": b_up, "w_down": w_down, "out_grad": out_grad}


@jax.custom_vjp
def low(v):
    return lax.optimization_barrier(v.astype(jnp.bfloat16)).astype(jnp.float32)

@jax.custom_vjp
def low_back(v):
    return v

def low_keep(v):
    return (low(v), None)

def low_pass(kept, grad):
    return (grad,)

def back_keep(v):
    return (v, None)

def back_low(kept, grad):
    return (low(grad),)
low.defvjp(low_keep, low_pass)
low_back.defvjp(back_keep, back_low)
EPSILON = 1e-05
HIGH = lax.Precision.HIGHEST

def layer_norm(values, gain, shift):
    centred = values - lax.optimization_barrier(jnp.mean(values, axis=-1, keepdims=True))
    spread = lax.optimization_barrier(jnp.mean(centred * centred, axis=-1, keepdims=True))
    return centred * lax.rsqrt(spread + EPSILON) * gain + shift

def attend(queries, key_rows, value_rows, starts, first):
    length = queries.shape[0]
    block_rows = min(512, length)
    score_scale = HEAD_DIM ** (-0.5)
    key_pos = first + jnp.arange(length, dtype=jnp.int32)

    def one_block(block_index):
        row_first = block_index * block_rows
        query_block = lax.dynamic_slice_in_dim(queries, row_first, block_rows, 0)
        start_block = lax.dynamic_slice_in_dim(starts, row_first, block_rows, 0)
        query_pos = first + row_first + jnp.arange(block_rows, dtype=jnp.int32)
        scores = jnp.einsum('qhd,khd->hqk', query_block, key_rows, precision=HIGH) * score_scale
        scores = low_back(scores)
        allowed = (key_pos[None, :] <= query_pos[:, None]) & (key_pos[None, :] >= start_block[:, None])
        scores = jnp.where(allowed[None], scores, -1e+30)
        peak_score = lax.optimization_barrier(jnp.max(scores, axis=-1, keepdims=True))
        exponents = jnp.exp(scores - peak_score)
        prob_rows = low(exponents / lax.optimization_barrier(jnp.sum(exponents, axis=-1, keepdims=True)))
        return jnp.einsum('hqk,khd->qhd', prob_rows, value_rows, precision=HIGH)
    blocks = lax.map(jax.checkpoint(one_block), jnp.arange(length // block_rows, dtype=jnp.int32))
    return blocks.reshape(length, queries.shape[1], queries.shape[2])

def attention(queries, key_rows, value_rows, starts):
    seq_count = TOKENS // SEQ
    shaped = (seq_count, SEQ, HEADS, HEAD_DIM)
    firsts = jnp.arange(seq_count, dtype=jnp.int32) * SEQ

    def one_sequence(packed):
        return attend(packed[0], packed[1], packed[2], packed[3], packed[4])
    mixed = lax.map(one_sequence, (queries.reshape(shaped), key_rows.reshape(shaped), value_rows.reshape(shaped), starts.reshape(seq_count, SEQ), firsts))
    return mixed.reshape(TOKENS, HEADS * HEAD_DIM)

def layer(starts, inputs, gain_rows, shift_rows, bias_rows, w_qkv, b_qv, w_out, w_up, b_up, w_down):
    normed = low(layer_norm(inputs, gain_rows[0], shift_rows[0]))
    qv_bias = b_qv.reshape(2, D)
    queries = low(low_back(jnp.dot(normed, w_qkv[0], precision=HIGH) + qv_bias[0]))
    key_rows = low(low_back(jnp.dot(normed, w_qkv[1], precision=HIGH)))
    value_rows = low(low_back(jnp.dot(normed, w_qkv[2], precision=HIGH) + qv_bias[1]))
    mixed = low(low_back(attention(queries, key_rows, value_rows, starts)))
    middle = inputs + low_back(jnp.dot(mixed, w_out, precision=HIGH)) + bias_rows[0]
    normed_two = low(layer_norm(middle, gain_rows[1], shift_rows[1]))
    pre_act = low_back(jnp.dot(normed_two, w_up, precision=HIGH) + b_up.reshape(FF))
    active = low(jax.nn.gelu(pre_act, approximate=True))
    return middle + low_back(jnp.dot(active, w_down, precision=HIGH)) + bias_rows[1]

def reference(tokens, doc_start, norm_gains, norm_biases, out_biases, w_qkv, b_qv, w_out, w_up, b_up, w_down, out_grad):
    primals = (tokens.astype(jnp.float32), norm_gains.astype(jnp.float32), norm_biases.astype(jnp.float32), out_biases.astype(jnp.float32), w_qkv.astype(jnp.float32), b_qv.astype(jnp.float32), w_out.astype(jnp.float32), w_up.astype(jnp.float32), b_up.astype(jnp.float32), w_down.astype(jnp.float32))
    output, backward = jax.vjp(partial(layer, doc_start), *primals)
    grads = backward(out_grad.astype(jnp.float32))
    return (output, grads[0], grads[1], grads[2], grads[3], grads[4], grads[5], grads[6], grads[7], grads[8], grads[9])
```

```python
import jax
import jax.numpy as jnp
from jax import lax
from jax.experimental import pallas as pl
from jax.experimental.pallas import tpu as pltpu
from jax.sharding import PartitionSpec as P

HEAD_DIM = 64
BLOCK = 512
MSG = 208
EPSILON = 1e-05
MASKED = -1e30
BF = jnp.bfloat16
F32 = jnp.float32


def along_y(a, d):
    pairs = [
        ((x * 4 + y) * 2 + c, (x * 4 + (y + d) % 4) * 2 + c)
        for x in range(4)
        for y in range(4)
        for c in range(2)
    ]
    return lax.ppermute(a, "fsdp", pairs)


def along_x(a, d):
    pairs = [
        ((x * 4 + y) * 2 + c, (((x + d) % 4) * 4 + y) * 2 + c)
        for x in range(4)
        for y in range(4)
        for c in range(2)
    ]
    return lax.ppermute(a, "fsdp", pairs)


def other_core(a):
    return lax.ppermute(a, "fsdp", [(i, i ^ 1) for i in range(32)])


def along_z(a, d):
    return lax.ppermute(a, "tp", [(i, (i + d) % 4) for i in range(4)])


def from_all(a, move):
    return [a, move(a, 1), move(a, 2), move(a, 3)]


def in_order(rel, me):
    n = rel[0].shape[0]
    turned = [rel[0], rel[3], rel[2], rel[1]]
    twice = jnp.concatenate(turned + turned[:3], axis=0)
    return lax.dynamic_slice_in_dim(twice, ((4 - me) % 4) * n, 4 * n, axis=0)


def placed_in_order(rel, me):
    n = rel[0].shape[0]
    out = jnp.zeros((4 * n, *rel[0].shape[1:]), rel[0].dtype)
    for d, a in enumerate(rel):
        out = lax.dynamic_update_slice_in_dim(out, a, ((me - d) % 4) * n, axis=0)
    return out


def gather_rows(a, x, y, c):
    rows, width = a.shape
    by_y = placed_in_order(from_all(a, along_y), y)
    by_x = placed_in_order(from_all(by_y, along_x), x)
    theirs = other_core(by_x)
    mine = by_x.reshape(16, 1, rows, width)
    theirs = theirs.reshape(16, 1, rows, width)
    both = jnp.where(
        c == 0,
        jnp.concatenate([mine, theirs], axis=1),
        jnp.concatenate([theirs, mine], axis=1),
    )
    return both.reshape(32 * rows, width)


def piece(a, at, n):
    return lax.dynamic_slice_in_dim(a, at * n, n, axis=0)


def scatter_rows(a, x, y, c):
    width = a.shape[1]
    a = a.reshape(16, 2, 32, width)
    away = lax.dynamic_index_in_dim(a, 1 - c, 1, keepdims=False)
    mine = lax.dynamic_index_in_dim(a, c, 1, keepdims=False)
    a = (mine.astype(F32) + other_core(away).astype(F32)).astype(BF).reshape(16 * 32, width)
    for move, me, n in ((along_x, x, 128), (along_y, y, 32)):
        total = piece(a, me, n).astype(F32)
        for d in (2, 1, 3):
            total = total + move(piece(a, (me + d) % 4, n), d).astype(F32)
        a = total.astype(BF)
    return total


def halves(v):
    high = lax.reduce_precision(v, 8, 7)
    return high.astype(BF), (v - high).astype(BF)


def normalized(values):
    centred = values - jnp.mean(values, axis=-1, keepdims=True)
    spread = jnp.mean(centred * centred, axis=-1, keepdims=True)
    scale = lax.rsqrt(spread + EPSILON)
    return centred * scale, scale


def norm_back(grad, normed, scale, gain):
    e = grad * gain
    return scale * (
        e
        - jnp.mean(e, axis=-1, keepdims=True)
        - normed * jnp.mean(e * normed, axis=-1, keepdims=True)
    )


def dot(a, b, ca, cb):
    return lax.dot_general(a, b, (((ca,), (cb,)), ((), ())), preferred_element_type=F32)


def unpack(place, msgs, sib, q_s, kt_s, vt_s, start_s, k_s, v_s):
    y, c = place[0], place[1]
    for d in range(4):
        block = lax.rem(y - d + 4, 4) * 2
        msg = msgs[d]
        q_s[d] = msg[0:64, :] * BF(0.125)
        first = msg[192:208, :].astype(F32)
        start_s[d] = first[0:1] * 64.0 + first[1:2]
        k, v = msg[64:128, :], msg[128:192, :]
        kt_s[block + c] = k.T
        vt_s[block + c] = v.T
        k_s[block + c] = k
        v_s[block + c] = v
        k, v = sib[d, 0:64, :], sib[d, 64:128, :]
        kt_s[block + 1 - c] = k.T
        vt_s[block + 1 - c] = v.T
        k_s[block + 1 - c] = k
        v_s[block + 1 - c] = v


def positions(place, axis):
    shape = (BLOCK, 1) if axis == 0 else (1, BLOCK)
    at = lax.broadcasted_iota(jnp.int32, shape, axis)
    chunk = (place[2] - (at >> 7)) & 3
    return ((chunk << 7) + (at & 127)).astype(F32)


def allowed_in(place, start, query_block, key_block, diagonal):
    key_pos = positions(place, 0)
    allowed = key_pos >= start - (key_block * BLOCK).astype(F32)
    if diagonal:
        allowed = allowed & (key_pos <= positions(place, 1))
    return allowed


def forward_kernel(
    place, m0, m1, m2, m3, sib, mixed, mixed_low, logs,
    q_s, kt_s, vt_s, start_s, k_s, v_s, peak_s, total_s, acc_s,
):
    unpack(place, (m0, m1, m2, m3), sib, q_s, kt_s, vt_s, start_s, k_s, v_s)

    def queries(d, carry):
        block = lax.rem(place[0] - d + 4, 4) * 2 + place[1]
        start = start_s[d]
        peak_s[...] = jnp.full((1, BLOCK), MASKED, F32)
        total_s[...] = jnp.zeros((1, BLOCK), F32)
        acc_s[...] = jnp.zeros((HEAD_DIM, BLOCK), F32)

        def step(key_block, diagonal):
            s = dot(kt_s[key_block], q_s[d], 1, 0)
            s = jnp.where(allowed_in(place, start, block, key_block, diagonal), s, MASKED)
            old = peak_s[...]
            peak = jnp.maximum(old, jnp.max(s, axis=0, keepdims=True))
            p = jnp.exp(s - peak)
            shrink = jnp.exp(old - peak)
            peak_s[...] = peak
            total_s[...] = total_s[...] * shrink + jnp.sum(p, axis=0, keepdims=True)
            acc_s[...] = acc_s[...] * shrink + dot(v_s[key_block], p.astype(BF), 1, 0)

        def body(key_block, carry):
            step(key_block, False)
            return carry

        low = jnp.min(start).astype(jnp.int32) // BLOCK
        lax.fori_loop(low, block, body, 0)
        step(block, True)
        out = acc_s[...] / total_s[...]
        mixed[d] = out
        mixed_low[d] = out.astype(BF)
        logs[d] = peak_s[...] + jnp.log(total_s[...])
        return carry

    lax.fori_loop(0, 4, queries, 0)


def backward_kernel(
    place, m0, m1, m2, m3, sib, mixed, logs, g0, g1, g2, g3, dq, own, away,
    q_s, kt_s, vt_s, start_s, k_s, v_s, g_s, dk_s, dv_s, acc_s,
):
    unpack(place, (m0, m1, m2, m3), sib, q_s, kt_s, vt_s, start_s, k_s, v_s)
    for d, g in enumerate((g0, g1, g2, g3)):
        g_s[d] = g[...]
    dk_s[...] = jnp.zeros(dk_s.shape, F32)
    dv_s[...] = jnp.zeros(dv_s.shape, F32)

    def queries(d, carry):
        block = lax.rem(place[0] - d + 4, 4) * 2 + place[1]
        start = start_s[d]
        log = logs[d]
        grad = g_s[d]
        q = q_s[d]
        delta = jnp.sum(grad.astype(F32) * mixed[d], axis=0, keepdims=True)
        qt = q.T
        gt = grad.T
        acc_s[...] = jnp.zeros((HEAD_DIM, BLOCK), F32)

        def step(key_block, diagonal):
            s = dot(kt_s[key_block], q, 1, 0)
            p = jnp.where(
                allowed_in(place, start, block, key_block, diagonal), jnp.exp(s - log), 0.0
            )
            dp = dot(vt_s[key_block], grad, 1, 0)
            ds = (p * (dp - delta)).astype(BF)
            dv_s[key_block] += dot(p.astype(BF), gt, 1, 0)
            dk_s[key_block] += dot(ds, qt, 1, 0)
            acc_s[...] += dot(k_s[key_block], ds, 1, 0)

        def body(key_block, carry):
            step(key_block, False)
            return carry

        low = jnp.min(start).astype(jnp.int32) // BLOCK
        lax.fori_loop(low, block, body, 0)
        step(block, True)
        dq[d] = (acc_s[...] * 0.125).astype(BF)
        return carry

    lax.fori_loop(0, 4, queries, 0)
    for d in range(4):
        block = lax.rem(place[0] - d + 4, 4) * 2
        own[d, 0:64, :] = dk_s[block + place[1]].T
        own[d, 64:128, :] = dv_s[block + place[1]].T
        away[d, 0:64, :] = dk_s[block + 1 - place[1]].T.astype(BF)
        away[d, 64:128, :] = dv_s[block + 1 - place[1]].T.astype(BF)


KV_SCRATCH = [
    pltpu.VMEM((4, HEAD_DIM, BLOCK), BF),
    pltpu.VMEM((8, BLOCK, HEAD_DIM), BF),
    pltpu.VMEM((8, BLOCK, HEAD_DIM), BF),
    pltpu.VMEM((4, 1, BLOCK), F32),
    pltpu.VMEM((8, HEAD_DIM, BLOCK), BF),
    pltpu.VMEM((8, HEAD_DIM, BLOCK), BF),
]
PARAMS = pltpu.CompilerParams(vmem_limit_bytes=48 * 1024 * 1024)


def in_vmem(n):
    return [pl.BlockSpec(memory_space=pltpu.SMEM)] + [pl.BlockSpec(memory_space=pltpu.VMEM)] * n


def attend(place, msgs, sib):
    return pl.pallas_call(
        forward_kernel,
        out_shape=(
            jax.ShapeDtypeStruct((4, HEAD_DIM, BLOCK), F32),
            jax.ShapeDtypeStruct((4, HEAD_DIM, BLOCK), BF),
            jax.ShapeDtypeStruct((4, 1, BLOCK), F32),
        ),
        in_specs=in_vmem(5),
        out_specs=[pl.BlockSpec(memory_space=pltpu.VMEM)] * 3,
        scratch_shapes=KV_SCRATCH
        + [
            pltpu.VMEM((1, BLOCK), F32),
            pltpu.VMEM((1, BLOCK), F32),
            pltpu.VMEM((HEAD_DIM, BLOCK), F32),
        ],
        compiler_params=PARAMS,
        cost_estimate=pl.CostEstimate(flops=10**10, bytes_accessed=10**7, transcendentals=0),
    )(place, *msgs, sib)


def attend_back(place, msgs, sib, mixed, logs, grads):
    return pl.pallas_call(
        backward_kernel,
        out_shape=(
            jax.ShapeDtypeStruct((4, HEAD_DIM, BLOCK), BF),
            jax.ShapeDtypeStruct((4, 2 * HEAD_DIM, BLOCK), F32),
            jax.ShapeDtypeStruct((4, 2 * HEAD_DIM, BLOCK), BF),
        ),
        in_specs=in_vmem(11),
        out_specs=[pl.BlockSpec(memory_space=pltpu.VMEM)] * 3,
        scratch_shapes=KV_SCRATCH
        + [
            pltpu.VMEM((4, HEAD_DIM, BLOCK), BF),
            pltpu.VMEM((8, BLOCK, HEAD_DIM), F32),
            pltpu.VMEM((8, BLOCK, HEAD_DIM), F32),
            pltpu.VMEM((HEAD_DIM, BLOCK), F32),
        ],
        compiler_params=PARAMS,
        cost_estimate=pl.CostEstimate(flops=2 * 10**10, bytes_accessed=10**7, transcendentals=0),
    )(place, *msgs, sib, mixed, logs, *grads)


def gelu_pair(v):
    root = 0.7978845608028654
    square = v * v
    t = jnp.tanh(root * v * (1.0 + 0.044715 * square))
    half = 0.5 * (1.0 + t)
    slope = half + 0.5 * v * (1.0 - t * t) * (root * (1.0 + 3 * 0.044715 * square))
    return v * half, slope


def summed(own, sent):
    total = own
    for d in (2, 1, 3):
        total = total + along_z(sent[d], -d).astype(F32)
    return total


def local(
    tokens, doc_start, norm_gains, norm_biases, out_biases, w_qkv, b_qv, w_out, w_up, b_up,
    w_down, out_grad,
):
    f = lax.axis_index("fsdp")
    x, y, c = f // 8, (f // 2) % 4, f % 2
    t = lax.axis_index("tp")
    place = jnp.stack([y, c, t]).astype(jnp.int32)

    both_ff = jnp.concatenate([w_up, w_down.T], axis=1)
    ff_all = lax.all_gather(both_ff, "fsdp", axis=0, tiled=True)
    up_all, down_all = ff_all[:, :1024], ff_all[:, 1024:]

    vectors = jnp.concatenate([norm_gains, norm_biases, out_biases], axis=0)
    vectors = in_order([v[None] for v in from_all(vectors, along_z)], t)
    vectors = jnp.moveaxis(vectors, 0, 1).reshape(6, 32)
    high, low = halves(vectors)
    small = jnp.concatenate([high.reshape(-1), low.reshape(-1), b_qv.reshape(-1), b_up.reshape(-1)])
    small = jnp.pad(small, (0, 32 * 128 - small.shape[0])).reshape(32, 128)
    qkv_local = w_qkv.reshape(3, 32, 4, 64).transpose(1, 2, 0, 3).reshape(32, 768)
    attn_all = gather_rows(jnp.concatenate([qkv_local, w_out.T, small], axis=1), x, y, c)
    qkv_all = attn_all[:, :768]
    out_own = attn_all[:, 768:1024]
    small = attn_all[:, 1024:].reshape(32, 32 * 128).astype(F32)
    vectors = (small[:, :192] + small[:, 192:384]).reshape(32, 6, 32)
    vectors = vectors.transpose(1, 0, 2).reshape(6, 1024)
    gain_one, gain_two, shift_one, shift_two, bias_one, bias_two = (vectors[i] for i in range(6))
    qv_bias = small[:, 384:400].reshape(32, 2, 8).transpose(1, 0, 2).reshape(2, 4, 64)
    up_bias = small[:, 400:432].reshape(1024)
    bias_columns = jnp.stack([qv_bias[0], jnp.zeros_like(qv_bias[0]), qv_bias[1]], axis=1)

    rows = jnp.concatenate(from_all(tokens, along_z), axis=0)
    full_grad = jnp.concatenate(from_all(out_grad, along_z), axis=0)
    out_rel = from_all(out_own, along_z)

    n_one, scale_one = normalized(rows.astype(F32))
    normed_one = (n_one * gain_one + shift_one).astype(BF)
    qkv = dot(qkv_all, normed_one, 0, 1) + bias_columns.reshape(768, 1)
    qkv = qkv.astype(BF)

    first = doc_start - x * 4096
    turned = first.reshape(4, 128)
    first = jnp.concatenate(
        [lax.dynamic_slice_in_dim(turned, (t - d) % 4, 1, axis=0) for d in range(4)], axis=0
    ).reshape(1, BLOCK)
    first = jnp.concatenate([first // 64, first % 64, jnp.zeros((14, BLOCK), jnp.int32)], axis=0)
    first = first.astype(BF)

    def message(d):
        return jnp.concatenate([piece(qkv, (y + d) % 4, 192), first], axis=0)

    msgs = [message(0)] + [along_y(message(d), d) for d in (1, 2, 3)]
    sib = other_core(jnp.stack([m[64:192] for m in msgs]))
    mixed, mixed_low, logs = attend(place, msgs, sib)

    back = [mixed_low[0]] + [along_y(mixed_low[d], -d) for d in (1, 2, 3)]
    mixed_own = in_order([back[0], back[3], back[2], back[1]], y)
    by_z = [mixed_own.reshape(256, 4, 128)[:, d] for d in range(4)]
    mixed_rel = [by_z[0]] + [along_z(by_z[d], -d) for d in (1, 2, 3)]
    out_after = [out_rel[0], out_rel[3], out_rel[2], out_rel[1]]
    attn = dot(jnp.concatenate(mixed_rel, axis=0), jnp.concatenate(out_after, axis=1), 0, 1)
    middle = tokens.astype(F32) + attn + bias_one
    n_two, scale_two = normalized(middle)
    normed_two = (n_two * gain_two + shift_two).astype(BF)
    full_two = jnp.concatenate(from_all(normed_two, along_z), axis=0)

    pre_act = dot(full_two, up_all, 1, 0) + up_bias
    active, slope = gelu_pair(pre_act)
    active = active.astype(BF)
    grad_active = dot(full_grad, down_all, 1, 0)
    grad_pre = (grad_active * slope).astype(BF)
    part = dot(grad_pre, up_all, 1, 1)
    sent = part.astype(BF)
    grad_two = summed(part[:128], [sent[128 * d : 128 * (d + 1)] for d in range(4)])
    part = dot(active, down_all, 1, 1)
    sent = part.astype(BF)
    mlp = summed(part[:128], [sent[128 * d : 128 * (d + 1)] for d in range(4)])
    output = middle + mlp + bias_two

    grad_up = dot(full_two, grad_pre, 0, 0).astype(BF)
    grad_down = dot(full_grad, active, 0, 0).astype(BF)
    ff_grads = lax.psum_scatter(
        jnp.concatenate([grad_up, grad_down], axis=1), "fsdp", scatter_dimension=0, tiled=True
    ).astype(F32)
    out_wup, out_wdown = ff_grads[:, :1024], ff_grads[:, 1024:].T
    grad_bup = jnp.sum(grad_pre.astype(F32), axis=0)

    upstream = out_grad.astype(F32)
    grad_middle = upstream + norm_back(grad_two, n_two, scale_two, gain_two)
    middle_low = grad_middle.astype(BF)
    sums_two = [
        jnp.sum(grad_two * n_two, axis=0),
        jnp.sum(grad_two, axis=0),
        jnp.sum(grad_middle, axis=0),
        jnp.sum(upstream, axis=0),
    ]
    grad_mixed = [dot(w, middle_low, 0, 1).astype(BF) for w in out_after]
    by_z = [grad_mixed[0]] + [along_z(grad_mixed[d], d) for d in (1, 2, 3)]
    grad_heads = jnp.concatenate(by_z, axis=1)
    grads = [piece(grad_heads, y, 64)] + [
        along_y(piece(grad_heads, (y + d) % 4, 64), d) for d in (1, 2, 3)
    ]
    full_middle = jnp.concatenate(from_all(middle_low, along_z), axis=0)
    grad_out = dot(full_middle, mixed_own, 0, 1).astype(BF)

    dq, own, away = attend_back(place, msgs, sib, mixed, logs, grads)
    pair = (own + other_core(away).astype(F32)).astype(BF)
    dqkv = jnp.concatenate([dq, pair], axis=1)
    back = [dqkv[0]] + [along_y(dqkv[d], -d) for d in (1, 2, 3)]
    grad_qkv = in_order([back[0], back[3], back[2], back[1]], y)

    part = dot(grad_qkv, qkv_all, 0, 1)
    sent = part.astype(BF)
    grad_one = summed(part[:128], [sent[128 * d : 128 * (d + 1)] for d in range(4)])
    grad_tokens = grad_middle + norm_back(grad_one, n_one[:128], scale_one[:128], gain_one)

    sums = jnp.stack(
        [jnp.sum(part * n_one, axis=0), sums_two[0], jnp.sum(part, axis=0), *sums_two[1:]]
    )
    sums = sums.reshape(6, 32, 32).transpose(1, 0, 2).reshape(32, 192)
    grad_bqv = jnp.sum(grad_qkv.astype(F32).reshape(4, 3, 64, BLOCK), axis=-1)
    grad_bqv = jnp.stack([grad_bqv[:, 0].reshape(256), grad_bqv[:, 2].reshape(256)])
    grad_bqv = grad_bqv.reshape(2, 32, 8).transpose(1, 0, 2).reshape(32, 16)
    small = jnp.concatenate([sums, grad_bqv, grad_bup.reshape(32, 32)], axis=1).astype(BF)
    small = jnp.pad(small, ((0, 0), (0, 32 * 128 - 240))).reshape(1024, 128)
    grad_wqkv = dot(normed_one, grad_qkv, 0, 1).astype(BF)
    got = scatter_rows(jnp.concatenate([grad_wqkv, grad_out, small], axis=1), x, y, c)
    out_qkv = got[:, :768].reshape(32, 4, 3, 64).transpose(2, 0, 1, 3).reshape(3, 32, 256)
    out_wout = got[:, 768:1024].T
    small = got[:2, 1024:].reshape(256)
    out_bqv = small[192:208].reshape(2, 1, 8)
    out_bup = small[208:240].reshape(1, 32)
    vectors = small[:192].reshape(6, 4, 8)
    vectors = lax.dynamic_index_in_dim(vectors, t, 1, keepdims=False) + sum(
        along_z(lax.dynamic_index_in_dim(vectors, (t + d) % 4, 1, keepdims=False), d)
        for d in (1, 2, 3)
    )
    return (
        output,
        grad_tokens,
        vectors[0:2],
        vectors[2:4],
        vectors[4:6],
        out_qkv,
        out_bqv,
        out_wout,
        out_wup,
        out_bup,
        out_wdown,
    )


def solution(mesh):
    by_rows = P(("fsdp", "tp"), None)
    by_features = P(None, ("fsdp", "tp"))
    weights = (
        P(None, "fsdp", "tp"),
        P(None, "tp", "fsdp"),
        P("tp", "fsdp"),
        P("fsdp", "tp"),
        P("tp", "fsdp"),
        P("tp", "fsdp"),
    )
    return jax.shard_map(
        local,
        mesh=mesh,
        in_specs=(by_rows, P("fsdp"), by_features, by_features, by_features, *weights, by_rows),
        out_specs=(by_rows, by_rows, by_features, by_features, by_features, *weights),
        check_vma=False,
    )
```

```python
import jax
import jax.numpy as jnp
from jax import lax
from jax.experimental import pallas as pl
from jax.experimental.pallas import tpu as pltpu
from jax.sharding import PartitionSpec as P

HEAD_DIM = 64
BLOCK = 512
MSG = 208
EPSILON = 1e-05
MASKED = -1e30
BF = jnp.bfloat16
F32 = jnp.float32


def along_y(a, d):
    pairs = [
        ((x * 4 + y) * 2 + c, (x * 4 + (y + d) % 4) * 2 + c)
        for x in range(4)
        for y in range(4)
        for c in range(2)
    ]
    return lax.ppermute(a, "fsdp", pairs)


def along_x(a, d):
    pairs = [
        ((x * 4 + y) * 2 + c, (((x + d) % 4) * 4 + y) * 2 + c)
        for x in range(4)
        for y in range(4)
        for c in range(2)
    ]
    return lax.ppermute(a, "fsdp", pairs)


def other_core(a):
    return lax.ppermute(a, "fsdp", [(i, i ^ 1) for i in range(32)])


def along_z(a, d):
    return lax.ppermute(a, "tp", [(i, (i + d) % 4) for i in range(4)])


def from_all(a, move):
    return [a, move(a, 1), move(a, 2), move(a, 3)]


def in_order(rel, me):
    n = rel[0].shape[0]
    turned = [rel[0], rel[3], rel[2], rel[1]]
    twice = jnp.concatenate(turned + turned[:3], axis=0)
    return lax.dynamic_slice_in_dim(twice, ((4 - me) % 4) * n, 4 * n, axis=0)


def placed_in_order(rel, me):
    n = rel[0].shape[0]
    out = jnp.zeros((4 * n, *rel[0].shape[1:]), rel[0].dtype)
    for d, a in enumerate(rel):
        out = lax.dynamic_update_slice_in_dim(out, a, ((me - d) % 4) * n, axis=0)
    return out


def both_cores(by_x, c, rows):
    width = by_x.shape[1]
    theirs = other_core(by_x)
    mine = by_x.reshape(16, 1, rows, width)
    theirs = theirs.reshape(16, 1, rows, width)
    both = jnp.where(
        c == 0,
        jnp.concatenate([mine, theirs], axis=1),
        jnp.concatenate([theirs, mine], axis=1),
    )
    return both.reshape(32 * rows, width)


def piece(a, at, n):
    return lax.dynamic_slice_in_dim(a, at * n, n, axis=0)


def added(mine, theirs):
    return (mine.astype(F32) + theirs.astype(F32)).astype(BF)


def scattered(a, move, me, n):
    return [piece(a, me, n)] + [move(piece(a, (me + d) % 4, n), d) for d in (2, 1, 3)]


def total(terms):
    return sum(a.astype(F32) for a in terms)


def halves(v):
    high = lax.reduce_precision(v, 8, 7)
    return high.astype(BF), (v - high).astype(BF)


def normalized(values):
    centred = values - jnp.mean(values, axis=-1, keepdims=True)
    spread = jnp.mean(centred * centred, axis=-1, keepdims=True)
    scale = lax.rsqrt(spread + EPSILON)
    return centred * scale, scale


def norm_back(grad, normed, scale, gain):
    e = grad * gain
    return scale * (
        e
        - jnp.mean(e, axis=-1, keepdims=True)
        - normed * jnp.mean(e * normed, axis=-1, keepdims=True)
    )


def dot(a, b, ca, cb):
    return lax.dot_general(a, b, (((ca,), (cb,)), ((), ())), preferred_element_type=F32)


def unpack(place, msgs, sib, q_s, kt_s, vt_s, start_s, k_s, v_s):
    y, c = place[0], place[1]
    for d in range(4):
        block = lax.rem(y - d + 4, 4) * 2
        msg = msgs[d]
        q_s[d] = msg[0:64, :] * BF(0.125)
        first = msg[192:208, :].astype(F32)
        start_s[d] = first[0:1] * 64.0 + first[1:2]
        k, v = msg[64:128, :], msg[128:192, :]
        kt_s[block + c] = k.T
        vt_s[block + c] = v.T
        k_s[block + c] = k
        v_s[block + c] = v
        k, v = sib[d, 0:64, :], sib[d, 64:128, :]
        kt_s[block + 1 - c] = k.T
        vt_s[block + 1 - c] = v.T
        k_s[block + 1 - c] = k
        v_s[block + 1 - c] = v


def positions(place, axis):
    shape = (BLOCK, 1) if axis == 0 else (1, BLOCK)
    at = lax.broadcasted_iota(jnp.int32, shape, axis)
    chunk = (place[2] - (at >> 7)) & 3
    return ((chunk << 7) + (at & 127)).astype(F32)


def allowed_in(place, start, query_block, key_block, diagonal):
    key_pos = positions(place, 0)
    allowed = key_pos >= start - (key_block * BLOCK).astype(F32)
    if diagonal:
        allowed = allowed & (key_pos <= positions(place, 1))
    return allowed


def forward_kernel(
    place, m0, m1, m2, m3, sib, mixed, mixed_low, logs,
    q_s, kt_s, vt_s, start_s, k_s, v_s, peak_s, total_s, acc_s,
):
    unpack(place, (m0, m1, m2, m3), sib, q_s, kt_s, vt_s, start_s, k_s, v_s)

    def queries(d, carry):
        block = lax.rem(place[0] - d + 4, 4) * 2 + place[1]
        start = start_s[d]
        peak_s[...] = jnp.full((1, BLOCK), MASKED, F32)
        total_s[...] = jnp.zeros((1, BLOCK), F32)
        acc_s[...] = jnp.zeros((HEAD_DIM, BLOCK), F32)

        def step(key_block, diagonal):
            s = dot(kt_s[key_block], q_s[d], 1, 0)
            s = jnp.where(allowed_in(place, start, block, key_block, diagonal), s, MASKED)
            old = peak_s[...]
            peak = jnp.maximum(old, jnp.max(s, axis=0, keepdims=True))
            p = jnp.exp(s - peak)
            shrink = jnp.exp(old - peak)
            peak_s[...] = peak
            total_s[...] = total_s[...] * shrink + jnp.sum(p, axis=0, keepdims=True)
            acc_s[...] = acc_s[...] * shrink + dot(v_s[key_block], p.astype(BF), 1, 0)

        def body(key_block, carry):
            step(key_block, False)
            return carry

        low = jnp.min(start).astype(jnp.int32) // BLOCK
        lax.fori_loop(low, block, body, 0)
        step(block, True)
        out = acc_s[...] / total_s[...]
        mixed[d] = out
        mixed_low[d] = out.astype(BF)
        logs[d] = peak_s[...] + jnp.log(total_s[...])
        return carry

    lax.fori_loop(0, 4, queries, 0)


def backward_kernel(
    place, m0, m1, m2, m3, sib, mixed, logs, g0, g1, g2, g3, dq, own, away,
    q_s, kt_s, vt_s, start_s, k_s, v_s, g_s, dk_s, dv_s, acc_s,
):
    unpack(place, (m0, m1, m2, m3), sib, q_s, kt_s, vt_s, start_s, k_s, v_s)
    for d, g in enumerate((g0, g1, g2, g3)):
        g_s[d] = g[...]
    dk_s[...] = jnp.zeros(dk_s.shape, F32)
    dv_s[...] = jnp.zeros(dv_s.shape, F32)

    def queries(d, carry):
        block = lax.rem(place[0] - d + 4, 4) * 2 + place[1]
        start = start_s[d]
        log = logs[d]
        grad = g_s[d]
        q = q_s[d]
        delta = jnp.sum(grad.astype(F32) * mixed[d], axis=0, keepdims=True)
        qt = q.T
        gt = grad.T
        acc_s[...] = jnp.zeros((HEAD_DIM, BLOCK), F32)

        def step(key_block, diagonal):
            s = dot(kt_s[key_block], q, 1, 0)
            p = jnp.where(
                allowed_in(place, start, block, key_block, diagonal), jnp.exp(s - log), 0.0
            )
            dp = dot(vt_s[key_block], grad, 1, 0)
            ds = (p * (dp - delta)).astype(BF)
            dv_s[key_block] += dot(p.astype(BF), gt, 1, 0)
            dk_s[key_block] += dot(ds, qt, 1, 0)
            acc_s[...] += dot(k_s[key_block], ds, 1, 0)

        def body(key_block, carry):
            step(key_block, False)
            return carry

        low = jnp.min(start).astype(jnp.int32) // BLOCK
        lax.fori_loop(low, block, body, 0)
        step(block, True)
        dq[d] = (acc_s[...] * 0.125).astype(BF)
        return carry

    lax.fori_loop(0, 4, queries, 0)
    for d in range(4):
        block = lax.rem(place[0] - d + 4, 4) * 2
        own[d, 0:64, :] = dk_s[block + place[1]].T
        own[d, 64:128, :] = dv_s[block + place[1]].T
        away[d, 0:64, :] = dk_s[block + 1 - place[1]].T.astype(BF)
        away[d, 64:128, :] = dv_s[block + 1 - place[1]].T.astype(BF)


KV_SCRATCH = [
    pltpu.VMEM((4, HEAD_DIM, BLOCK), BF),
    pltpu.VMEM((8, BLOCK, HEAD_DIM), BF),
    pltpu.VMEM((8, BLOCK, HEAD_DIM), BF),
    pltpu.VMEM((4, 1, BLOCK), F32),
    pltpu.VMEM((8, HEAD_DIM, BLOCK), BF),
    pltpu.VMEM((8, HEAD_DIM, BLOCK), BF),
]
PARAMS = pltpu.CompilerParams(vmem_limit_bytes=48 * 1024 * 1024)


def whole_call(kernel, shapes, scratch, flops, place, *arrays):
    def whole(a):
        return pl.BlockSpec(a.shape, lambda i, rank=len(a.shape): (0,) * rank)

    outs = [jax.ShapeDtypeStruct(*shape) for shape in shapes]
    return pl.pallas_call(
        kernel,
        grid=(1,),
        out_shape=outs,
        in_specs=[pl.BlockSpec(memory_space=pltpu.SMEM)] + [whole(a) for a in arrays],
        out_specs=[whole(a) for a in outs],
        scratch_shapes=scratch,
        compiler_params=PARAMS,
        cost_estimate=pl.CostEstimate(flops=flops, bytes_accessed=8 * 2**20, transcendentals=0),
    )(place, *arrays)


def attend(place, msgs, sib):
    head = (4, HEAD_DIM, BLOCK)
    scratch = [
        pltpu.VMEM((1, BLOCK), F32),
        pltpu.VMEM((1, BLOCK), F32),
        pltpu.VMEM((HEAD_DIM, BLOCK), F32),
    ]
    shapes = ((head, F32), (head, BF), ((4, 1, BLOCK), F32))
    return whole_call(forward_kernel, shapes, KV_SCRATCH + scratch, 10**10, place, *msgs, sib)


def attend_back(place, msgs, sib, mixed, logs, grads):
    pair = (4, 2 * HEAD_DIM, BLOCK)
    scratch = [
        pltpu.VMEM((4, HEAD_DIM, BLOCK), BF),
        pltpu.VMEM((8, BLOCK, HEAD_DIM), F32),
        pltpu.VMEM((8, BLOCK, HEAD_DIM), F32),
        pltpu.VMEM((HEAD_DIM, BLOCK), F32),
    ]
    shapes = (((4, HEAD_DIM, BLOCK), BF), (pair, F32), (pair, BF))
    arrays = (*msgs, sib, mixed, logs, *grads)
    return whole_call(backward_kernel, shapes, KV_SCRATCH + scratch, 2 * 10**10, place, *arrays)


def split_cores(place, mine, away, at, width, result):
    rows = result.reshape(16, 2, 32, width)
    even, odd = rows[:, 0].reshape(512, width), rows[:, 1].reshape(512, width)
    mine[:, at : at + width] = jnp.where(place[1] == 0, even, odd).astype(BF)
    away[:, at : at + width] = jnp.where(place[1] == 0, odd, even).astype(BF)


def weights_kernel(rows_a, cols_a, rows_b, cols_b, out, turned):
    step = pl.program_id(0)

    @pl.when(step == 0)
    def _():
        turned[...] = rows_a[...].T

    @pl.when(step == 4)
    def _():
        turned[...] = rows_b[...].T

    @pl.when(step < 4)
    def _():
        out[...] = dot(turned[...], cols_a[...], 1, 0).astype(BF)

    @pl.when(step >= 4)
    def _():
        out[...] = dot(turned[...], cols_b[...], 1, 0).astype(BF)


def weight_grads(rows_a, cols_a, rows_b, cols_b):
    whole = pl.BlockSpec((512, 1024), lambda i: (0, 0))
    return pl.pallas_call(
        weights_kernel,
        grid=(8,),
        out_shape=jax.ShapeDtypeStruct((1024, 2048), BF),
        in_specs=[
            whole,
            pl.BlockSpec((512, 256), lambda i: (0, jnp.minimum(i, 3))),
            whole,
            pl.BlockSpec((512, 256), lambda i: (0, jnp.maximum(i - 4, 0))),
        ],
        out_specs=pl.BlockSpec((1024, 256), lambda i: (0, i)),
        scratch_shapes=[pltpu.VMEM((1024, 512), BF)],
        compiler_params=PARAMS,
        cost_estimate=pl.CostEstimate(flops=4 * 2**30, bytes_accessed=8 * 2**20, transcendentals=0),
    )(rows_a, cols_a, rows_b, cols_b)


def last_kernel(place, dqkv, normed, m0, m1, m2, m3, mixed, vectors, mine, away):
    weights = jnp.zeros((192, 1024), F32)
    for d in range(4):
        at = lax.rem(place[0] - d + 4, 4) * BLOCK
        weights += dot(dqkv[d], normed[pl.ds(pl.multiple_of(at, BLOCK), BLOCK), :], 1, 0)
    outs = sum(
        dot(mixed[:, 128 * d : 128 * (d + 1)], m[...], 1, 0) for d, m in enumerate((m0, m1, m2, m3))
    )
    split_cores(place, mine, away, 0, 256, outs.T)
    padding = jnp.zeros((64, 1024), F32)
    split_cores(place, mine, away, 384, 256, jnp.concatenate([weights, padding], axis=0).T)
    ones = jnp.ones((8, BLOCK), BF)
    columns = sum(dot(ones, dqkv[d], 1, 1) for d in range(4))[0:1]
    pad = jnp.zeros((1, 64), F32)
    columns = [jnp.concatenate([pad, columns[:, 64 * i : 64 * (i + 1)]], axis=1) for i in range(3)]
    row = lax.broadcasted_iota(jnp.int32, (1024, 128), 0) & 31
    small = jnp.concatenate([vectors[...].T, jnp.zeros((1024, 120), F32)], axis=1)
    for i in range(3):
        small += jnp.where(row == i, columns[i], 0.0)
    split_cores(place, mine, away, 256, 128, small)


def last_grads(place, *arrays):
    return whole_call(last_kernel, (((512, 640), BF),) * 2, [], 2**31, place, *arrays)


def rows_kernel(place, b0, b1, b2, b3, weights, own, s1, s2, s3, heads):
    for d, b in enumerate((b0, b1, b2, b3)):
        heads[pl.ds(pl.multiple_of(lax.rem(place[0] + d, 4) * 192, 64), 192), :] = b[...]
    for chunk, out in enumerate((own, s1, s2, s3)):
        rows = heads[:, 128 * chunk : 128 * (chunk + 1)].T
        out[...] = dot(rows, weights[:, :768], 1, 1).astype(out.dtype)


def row_grads(place, *arrays):
    shapes = (((128, 1024), F32),) + (((128, 1024), BF),) * 3
    return whole_call(rows_kernel, shapes, [pltpu.VMEM((768, BLOCK), BF)], 2**30, place, *arrays)


def finish_kernel(
    place, g0, g1, g2, g3, w_qkv, own, ff, qkv, w_out, columns, vectors, up, down, m_s, k_s
):
    got = (g0, g1, g2, g3)
    up[...] = ff[:, :1024].astype(F32)
    down[...] = ff[:, 1024:].astype(F32).T
    w_out[...] = total([g[:, :256] for g in got]).T
    rest = total([g[:, 256:384] for g in got])
    for d, g in enumerate(got):
        head = lax.rem(place[0] - d + 4, 4)
        m_s[head] = g[:, 384:576].astype(F32)
        k_s[head] = g[0:16, 256:384].astype(F32)
    gain, shift = own[:, 0:1], own[:, 2:3]
    gain_sum, shift_sum = jnp.zeros((32, 64), F32), jnp.zeros((32, 64), F32)
    for h in range(4):
        for i in range(3):
            at = slice(64 * h, 64 * (h + 1))
            m, k = m_s[h, :, 64 * i : 64 * (i + 1)], k_s[h, i : i + 1, 64:128]
            w = w_qkv[i, :, at].astype(F32)
            qkv[i, :, at] = gain * m + shift * k
            columns[i : i + 1, at] = k
            gain_sum += w * m
            shift_sum += w * k
    gain_sum = jnp.sum(gain_sum, axis=1, keepdims=True)
    shift_sum = jnp.sum(shift_sum, axis=1, keepdims=True)
    vectors[...] = jnp.concatenate(
        [gain_sum, rest[:, 0:1], shift_sum, rest[:, 1:5], jnp.zeros((32, 1), F32)], axis=1
    )


def finish(place, *arrays):
    shapes = ((3, 32, 256), (256, 32), (3, 256), (32, 8), (32, 1024), (1024, 32))
    scratch = [pltpu.VMEM((4, 32, 192), F32), pltpu.VMEM((4, 16, 128), F32)]
    return whole_call(
        finish_kernel, [(shape, F32) for shape in shapes], scratch, 2**28, place, *arrays
    )


def gelu_pair(v):
    root = 0.7978845608028654
    square = v * v
    t = jnp.tanh(root * v * (1.0 + 0.044715 * square))
    half = 0.5 * (1.0 + t)
    slope = half + 0.5 * v * (1.0 - t * t) * (root * (1.0 + 3 * 0.044715 * square))
    return v * half, slope


def local(
    tokens, doc_start, norm_gains, norm_biases, out_biases, w_qkv, b_qv, w_out, w_up, b_up,
    w_down, out_grad,
):
    f = lax.axis_index("fsdp")
    x, y, c = f // 8, (f // 2) % 4, f % 2
    t = lax.axis_index("tp")
    place = jnp.stack([y, c, t]).astype(jnp.int32)

    vectors = jnp.concatenate([norm_gains, norm_biases, out_biases], axis=0).reshape(1, 48)
    vectors = jnp.concatenate(halves(vectors), axis=1)
    packed = jnp.concatenate([w_out.T, jnp.pad(vectors, ((0, 15), (0, 160)))], axis=0)
    qkv_local = w_qkv.reshape(3, 32, 4, 64).transpose(1, 2, 0, 3).reshape(32, 768)
    packed = from_all(packed, along_z)
    out_columns = [p[:32] for p in packed]
    own_vectors = in_order([p[32:33, :96].astype(F32) for p in packed], t)
    own_vectors = (own_vectors[:, :48] + own_vectors[:, 48:]).reshape(4, 6, 8)
    own_vectors = own_vectors.transpose(0, 2, 1).reshape(32, 6)
    gain, shift = own_vectors[:, 0:1], own_vectors[:, 2:3]

    weights = qkv_local.astype(F32)
    bias = jnp.sum(shift * weights, axis=0).reshape(4, 3, 64)
    qv_bias = jnp.stack([b_qv[0], jnp.zeros_like(b_qv[0]), b_qv[1]], axis=1).astype(F32)
    here = (jnp.arange(4)[:, None] == f // 8) & (jnp.arange(64)[None] // 8 == f % 8)
    bias = bias + jnp.where(here[:, None], jnp.tile(qv_bias, (1, 1, 8)), 0.0)
    bias = jnp.concatenate(halves(bias.reshape(6, 128)), axis=0)
    bias = jnp.pad(bias, ((0, 20), (0, 0)))
    by_y = from_all(jnp.concatenate([(gain * weights).astype(BF), bias], axis=1), along_y)
    by_x = from_all(placed_in_order(by_y, y), along_x)

    others = jnp.stack([own_vectors[:, i] for i in (1, 3, 4, 5)], axis=1)
    others = jnp.concatenate([*halves(others), b_up.reshape(32, 1), jnp.zeros((32, 119), BF)], axis=1)
    ff_local = jnp.concatenate([w_up, w_down.T, *out_columns, others], axis=1)
    ff_all = lax.all_gather(ff_local, "fsdp", axis=0, tiled=True)
    up_all, down_all, out_all = ff_all[:, :1024], ff_all[:, 1024:2048], ff_all[:, 2048:3072]

    rows = jnp.concatenate(from_all(tokens, along_z), axis=0)
    n_one, scale_one = normalized(rows.astype(F32))
    n_one_low = n_one.astype(BF)

    attn_all = both_cores(placed_in_order(by_x, x), c, 32)
    qkv_all = attn_all[:, :768]
    bias = attn_all[:, 768:].reshape(32, 32, 128)[:, :12].astype(F32).sum(axis=0)
    qkv = dot(qkv_all, n_one_low, 0, 1) + (bias[:6] + bias[6:]).reshape(768, 1)
    qkv = qkv.astype(BF)

    first = (doc_start - x * 4096).reshape(4, 128)
    first = jnp.concatenate(
        [lax.dynamic_slice_in_dim(first, (t - d) % 4, 1, axis=0) for d in range(4)], axis=0
    ).reshape(1, BLOCK)
    first = jnp.concatenate([first // 64, first % 64, jnp.zeros((14, BLOCK), jnp.int32)], axis=0)
    first = first.astype(BF)

    def message(d):
        return jnp.concatenate([piece(qkv, (y + d) % 4, 192), first], axis=0)

    msgs = [message(0)] + [along_y(message(d), d) for d in (1, 2, 3)]
    sib = other_core(jnp.stack([m[64:192] for m in msgs]))
    out_grad, sib = lax.optimization_barrier((out_grad, sib))
    full_grad = jnp.concatenate(from_all(out_grad, along_z), axis=0)
    mixed, mixed_low, logs = attend(place, msgs, sib)
    others = ff_all[:, 3072:3200].T[:16].astype(F32)
    gain_two, shift_two, bias_one, bias_two = (others[i] + others[4 + i] for i in range(4))
    up_bias = others[8]

    back = [mixed_low[0]] + [along_y(mixed_low[d], -d) for d in (1, 2, 3)]
    mixed_own = in_order([back[0], back[3], back[2], back[1]], y)
    by_z = [mixed_own[:, 128 * d : 128 * (d + 1)] for d in range(4)]
    by_z = [by_z[0]] + [along_z(by_z[d], -d) for d in (1, 2, 3)]
    by_z, n_one_low = lax.optimization_barrier((by_z, n_one_low))
    alike = [[(x * 4 + y) * 2 + c for y in range(4)] for x in range(4) for c in range(2)]
    n_all = lax.all_gather(n_one_low, "fsdp", axis=0, tiled=True, axis_index_groups=alike)

    mixed_rel = jnp.concatenate([by_z[0], by_z[3], by_z[2], by_z[1]], axis=0)
    attn = dot(mixed_rel, out_all, 0, 1)
    middle = tokens.astype(F32) + attn + bias_one
    n_two, scale_two = normalized(middle)
    normed_two = (n_two * gain_two + shift_two).astype(BF)
    full_two = jnp.concatenate(from_all(normed_two, along_z), axis=0)

    pre_act = dot(full_two, up_all, 1, 0) + up_bias
    active, slope = gelu_pair(pre_act)
    active = active.astype(BF)
    grad_active = dot(full_grad, down_all, 1, 0)
    grad_pre = (grad_active * slope).astype(BF)
    part = dot(grad_pre, up_all, 1, 1)
    sent = part.astype(BF)
    arrived = [along_z(sent[128 * d : 128 * (d + 1)], -d) for d in (1, 2, 3)]
    ff_grads = weight_grads(full_two, grad_pre, full_grad, active)
    mlp_part = dot(active, down_all, 1, 1)
    mlp_sent = mlp_part.astype(BF)
    arrived, ff_grads, mlp_sent = lax.optimization_barrier((arrived, ff_grads, mlp_sent))
    grad_two = part[:128] + sum(a.astype(F32) for a in arrived)
    grad_bup = jnp.sum(grad_pre.astype(F32), axis=0)
    ff_grads = lax.psum_scatter(ff_grads, "fsdp", scatter_dimension=0, tiled=True)

    upstream = out_grad.astype(F32)
    grad_middle = upstream + norm_back(grad_two, n_two, scale_two, gain_two)
    middle_low = grad_middle.astype(BF)
    grad_mixed = dot(out_all, middle_low, 0, 1).astype(BF)
    by_z = [grad_mixed[256 * d : 256 * (d + 1)] for d in range(4)]
    by_z = [by_z[0]] + [along_z(by_z[d], -d) for d in (1, 2, 3)]
    grad_heads = jnp.concatenate([by_z[0], by_z[3], by_z[2], by_z[1]], axis=1)
    grads = [piece(grad_heads, y, 64)] + [
        along_y(piece(grad_heads, (y + d) % 4, 64), d) for d in (1, 2, 3)
    ]
    grads, middle_low = lax.optimization_barrier((grads, middle_low))
    full_middle = from_all(middle_low, along_z)
    dq, own, away = attend_back(place, msgs, sib, mixed, logs, grads)
    dq, own, away, full_middle, mlp_sent = lax.optimization_barrier(
        (dq, own, away, full_middle, mlp_sent)
    )
    away = other_core(away)
    mlp = [along_z(mlp_sent[128 * d : 128 * (d + 1)], -d) for d in (1, 2, 3)]

    pair = (own + away.astype(F32)).astype(BF)
    dqkv = jnp.concatenate([dq, pair], axis=1)
    back = [dqkv[0]] + [along_y(dqkv[d], -d) for d in (1, 2, 3)]

    vectors = jnp.stack(
        [
            jnp.sum(grad_two * n_two, axis=0),
            jnp.sum(grad_two, axis=0),
            jnp.sum(grad_middle, axis=0),
            jnp.sum(upstream, axis=0),
            grad_bup,
            *[jnp.zeros_like(grad_bup)] * 3,
        ]
    )
    mine, away = last_grads(place, dqkv, n_all, *full_middle, mixed_own, vectors)
    away = other_core(away)
    back, mine, away, mlp = lax.optimization_barrier((back, mine, away, mlp))
    got = scattered(added(mine, away), along_x, x, 128)
    part, *sent = row_grads(place, *back, attn_all)
    grad_one = [along_z(sent[d - 1], -d) for d in (1, 2, 3)]
    output = middle + mlp_part[:128] + total(mlp) + bias_two
    got = scattered(total(got).astype(BF), along_y, y, 32)
    out_qkv, out_wout, columns, vectors, out_wup, out_wdown = finish(
        place, got[0], got[2], got[1], got[3], w_qkv, own_vectors, ff_grads
    )
    grad_one = part + total(grad_one)
    grad_tokens = grad_middle + norm_back(grad_one, n_one[:128], scale_one[:128], 1.0)
    out_bup = vectors[:, 6:7].reshape(1, 32)
    columns = jnp.concatenate([columns[0:1], columns[2:3]], axis=0).reshape(2, 32, 8)
    out_bqv = lax.dynamic_slice_in_dim(columns, f, 1, axis=1)
    vectors = piece(vectors, t, 8) + sum(
        along_z(piece(vectors, (t + d) % 4, 8), d) for d in (1, 2, 3)
    )
    vectors = vectors.T
    return (
        output,
        grad_tokens,
        vectors[0:2],
        vectors[2:4],
        vectors[4:6],
        out_qkv,
        out_bqv,
        out_wout,
        out_wup,
        out_bup,
        out_wdown,
    )


def solution(mesh):
    by_rows = P(("fsdp", "tp"), None)
    by_features = P(None, ("fsdp", "tp"))
    weights = (
        P(None, "fsdp", "tp"),
        P(None, "tp", "fsdp"),
        P("tp", "fsdp"),
        P("fsdp", "tp"),
        P("tp", "fsdp"),
        P("tp", "fsdp"),
    )
    return jax.shard_map(
        local,
        mesh=mesh,
        in_specs=(by_rows, P("fsdp"), by_features, by_features, by_features, *weights, by_rows),
        out_specs=(by_rows, by_rows, by_features, by_features, by_features, *weights),
        check_vma=False,
    )
```

```python
import functools

import jax
import jax.numpy as jnp
from jax import lax
from jax.experimental import pallas as pl
from jax.experimental.pallas import tpu as pltpu
from jax.sharding import PartitionSpec as P

HEAD_DIM = 64
BLOCK = 512
MSG = 208
EPSILON = 1e-05
MASKED = -1e30
BF = jnp.bfloat16
F32 = jnp.float32


def along_y(a, d):
    pairs = [
        ((x * 4 + y) * 2 + c, (x * 4 + (y + d) % 4) * 2 + c)
        for x in range(4)
        for y in range(4)
        for c in range(2)
    ]
    return lax.ppermute(a, "fsdp", pairs)


def along_x(a, d):
    pairs = [
        ((x * 4 + y) * 2 + c, (((x + d) % 4) * 4 + y) * 2 + c)
        for x in range(4)
        for y in range(4)
        for c in range(2)
    ]
    return lax.ppermute(a, "fsdp", pairs)


def other_core(a):
    return lax.ppermute(a, "fsdp", [(i, i ^ 1) for i in range(32)])


def along_z(a, d):
    return lax.ppermute(a, "tp", [(i, (i + d) % 4) for i in range(4)])


def from_all(a, move):
    return [a, move(a, 1), move(a, 2), move(a, 3)]


def in_order(rel, me):
    n = rel[0].shape[0]
    turned = [rel[0], rel[3], rel[2], rel[1]]
    twice = jnp.concatenate(turned + turned[:3], axis=0)
    return lax.dynamic_slice_in_dim(twice, ((4 - me) % 4) * n, 4 * n, axis=0)


def placed_in_order(rel, me):
    n = rel[0].shape[0]
    out = jnp.zeros((4 * n, *rel[0].shape[1:]), rel[0].dtype)
    for d, a in enumerate(rel):
        out = lax.dynamic_update_slice_in_dim(out, a, ((me - d) % 4) * n, axis=0)
    return out


def both_cores(by_x, c, rows):
    width = by_x.shape[1]
    theirs = other_core(by_x)
    mine = by_x.reshape(16, 1, rows, width)
    theirs = theirs.reshape(16, 1, rows, width)
    both = jnp.where(
        c == 0,
        jnp.concatenate([mine, theirs], axis=1),
        jnp.concatenate([theirs, mine], axis=1),
    )
    return both.reshape(32 * rows, width)


def piece(a, at, n):
    return lax.dynamic_slice_in_dim(a, at * n, n, axis=0)


def added(mine, theirs):
    return (mine.astype(F32) + theirs.astype(F32)).astype(BF)


def scattered(a, move, me, n):
    return [piece(a, me, n)] + [move(piece(a, (me + d) % 4, n), d) for d in (2, 1, 3)]


def total(terms):
    return sum(a.astype(F32) for a in terms)


def halves(v):
    high = lax.reduce_precision(v, 8, 7)
    return high.astype(BF), (v - high).astype(BF)


def normalized(values):
    centred = values - jnp.mean(values, axis=-1, keepdims=True)
    spread = jnp.mean(centred * centred, axis=-1, keepdims=True)
    scale = lax.rsqrt(spread + EPSILON)
    return centred * scale, scale


def norm_back(grad, normed, scale, gain):
    e = grad * gain
    return scale * (
        e
        - jnp.mean(e, axis=-1, keepdims=True)
        - normed * jnp.mean(e * normed, axis=-1, keepdims=True)
    )


def dot(a, b, ca, cb):
    return lax.dot_general(a, b, (((ca,), (cb,)), ((), ())), preferred_element_type=F32)


def unpack(place, msgs, sib, q_s, kt_s, vt_s, start_s, k_s, v_s):
    y, c = place[0], place[1]
    for d in range(4):
        block = lax.rem(y - d + 4, 4) * 2
        msg = msgs[d]
        q_s[d] = msg[0:64, :] * BF(0.125)
        first = msg[192:208, :].astype(F32)
        start_s[d] = first[0:1] * 64.0 + first[1:2]
        k, v = msg[64:128, :], msg[128:192, :]
        kt_s[block + c] = k.T
        vt_s[block + c] = v.T
        k_s[block + c] = k
        v_s[block + c] = v
        k, v = sib[d, 0:64, :], sib[d, 64:128, :]
        kt_s[block + 1 - c] = k.T
        vt_s[block + 1 - c] = v.T
        k_s[block + 1 - c] = k
        v_s[block + 1 - c] = v


def positions(place, axis):
    shape = (BLOCK, 1) if axis == 0 else (1, BLOCK)
    at = lax.broadcasted_iota(jnp.int32, shape, axis)
    chunk = (place[2] - (at >> 7)) & 3
    return ((chunk << 7) + (at & 127)).astype(F32)


def allowed_in(place, start, key_block, mode):
    if mode == 0:
        return None
    key_pos = positions(place, 0)
    allowed = key_pos >= start - (key_block * BLOCK).astype(F32)
    if mode == 2:
        allowed = allowed & (key_pos <= positions(place, 1))
    return allowed


def over_keys(start, block, step):
    low = jnp.min(start).astype(jnp.int32) // BLOCK
    last = jnp.max(start).astype(jnp.int32)

    def body(key_block, carry):
        @pl.when(key_block * BLOCK < last)
        def _():
            step(key_block, 1)

        @pl.when(key_block * BLOCK >= last)
        def _():
            step(key_block, 0)

        return carry

    lax.fori_loop(low, block, body, 0)
    step(block, 2)


def copies(sources, targets, done):
    started = [
        pltpu.make_async_copy(source, target, done.at[i])
        for i, (source, target) in enumerate(zip(sources, targets))
    ]
    for copy in started:
        copy.start()
    return started


def forward_kernel(
    place, m0, m1, m2, m3, sib_far, mixed, mixed_low, logs,
    q_s, kt_s, vt_s, start_s, k_s, v_s, peak_s, total_s, acc_s, msgs, sib, done,
):
    near = [msgs.at[d] for d in range(4)]
    for copy in copies((m0, m1, m2, m3, sib_far), (*near, sib), done):
        copy.wait()
    unpack(place, near, sib, q_s, kt_s, vt_s, start_s, k_s, v_s)

    def queries(d, carry):
        block = lax.rem(place[0] - d + 4, 4) * 2 + place[1]
        start = start_s[d]
        peak_s[...] = jnp.full((1, BLOCK), MASKED, F32)
        total_s[...] = jnp.zeros((1, BLOCK), F32)
        acc_s[...] = jnp.zeros((HEAD_DIM, BLOCK), F32)

        def step(key_block, mode):
            allowed = allowed_in(place, start, key_block, mode)
            halves_at = [slice(0, 256), slice(256, 512)]
            scores = [dot(kt_s[key_block], q_s[d, :, at], 1, 0) for at in halves_at]
            if allowed is not None:
                scores = [
                    jnp.where(allowed[:, at], s, MASKED) for at, s in zip(halves_at, scores)
                ]
            for at, s in zip(halves_at, scores):
                old = peak_s[:, at]
                peak = jnp.maximum(old, jnp.max(s, axis=0, keepdims=True))
                p = jnp.exp(s - peak)
                shrink = jnp.exp(old - peak)
                peak_s[:, at] = peak
                total_s[:, at] = total_s[:, at] * shrink + jnp.sum(p, axis=0, keepdims=True)
                acc_s[:, at] = acc_s[:, at] * shrink + dot(v_s[key_block], p.astype(BF), 1, 0)

        over_keys(start, block, step)
        out = acc_s[...] / total_s[...]
        mixed[d] = out
        mixed_low[d] = out.astype(BF)
        logs[d] = peak_s[...] + jnp.log(total_s[...])
        return carry

    lax.fori_loop(0, 4, queries, 0)


def backward_kernel(
    place, m0, m1, m2, m3, sib_far, mixed_far, logs_far, g0, g1, g2, g3, dq, own, away,
    q_s, kt_s, vt_s, start_s, k_s, v_s, g_s, dk_s, dv_s, acc_s, msgs, sib, mixed, logs, done,
):
    started = copies(
        (m0, m1, m2, m3, sib_far, mixed_far, logs_far),
        (*[msgs.at[d] for d in range(4)], sib, mixed, logs),
        done,
    )
    for d, g in enumerate((g0, g1, g2, g3)):
        g_s[d] = g[...]
    dk_s[...] = jnp.zeros(dk_s.shape, F32)
    dv_s[...] = jnp.zeros(dv_s.shape, F32)
    for copy in started:
        copy.wait()
    unpack(place, [msgs.at[d] for d in range(4)], sib, q_s, kt_s, vt_s, start_s, k_s, v_s)

    def queries(d, carry):
        block = lax.rem(place[0] - d + 4, 4) * 2 + place[1]
        start = start_s[d]
        log = logs[d]
        grad = g_s[d]
        q = q_s[d]
        delta = jnp.sum(grad.astype(F32) * mixed[d], axis=0, keepdims=True)
        qt = q.T
        gt = grad.T
        acc_s[...] = jnp.zeros((HEAD_DIM, BLOCK), F32)

        def step(key_block, mode):
            allowed = allowed_in(place, start, key_block, mode)
            grads, probs = [], []
            for at in (slice(0, 256), slice(256, 512)):
                p = jnp.exp(dot(kt_s[key_block], q[:, at], 1, 0) - log[:, at])
                if allowed is not None:
                    p = jnp.where(allowed[:, at], p, 0.0)
                dp = dot(vt_s[key_block], grad[:, at], 1, 0)
                grads.append((p * (dp - delta[:, at])).astype(BF))
                probs.append(p.astype(BF))
            ds = jnp.concatenate(grads, axis=1)
            dv_s[key_block] += dot(jnp.concatenate(probs, axis=1), gt, 1, 0)
            dk_s[key_block] += dot(ds, qt, 1, 0)
            acc_s[...] += dot(k_s[key_block], ds, 1, 0)

        over_keys(start, block, step)
        dq[d] = (acc_s[...] * 0.125).astype(BF)
        return carry

    lax.fori_loop(0, 4, queries, 0)
    for d in range(4):
        block = lax.rem(place[0] - d + 4, 4) * 2
        own[d, 0:64, :] = dk_s[block + place[1]].T
        own[d, 64:128, :] = dv_s[block + place[1]].T
        away[d, 0:64, :] = dk_s[block + 1 - place[1]].T.astype(BF)
        away[d, 64:128, :] = dv_s[block + 1 - place[1]].T.astype(BF)


KV_SCRATCH = [
    pltpu.VMEM((4, HEAD_DIM, BLOCK), BF),
    pltpu.VMEM((8, BLOCK, HEAD_DIM), BF),
    pltpu.VMEM((8, BLOCK, HEAD_DIM), BF),
    pltpu.VMEM((4, 1, BLOCK), F32),
    pltpu.VMEM((8, HEAD_DIM, BLOCK), BF),
    pltpu.VMEM((8, HEAD_DIM, BLOCK), BF),
]
PARAMS = pltpu.CompilerParams(vmem_limit_bytes=48 * 1024 * 1024)
FETCHING = pltpu.CompilerParams(vmem_limit_bytes=60 * 1024 * 1024)


def whole_call(kernel, shapes, scratch, flops, place, *arrays, fetched=()):
    def whole(a):
        return pl.BlockSpec(a.shape, lambda i, rank=len(a.shape): (0,) * rank)

    outs = [jax.ShapeDtypeStruct(*shape) for shape in shapes]
    return pl.pallas_call(
        kernel,
        grid=(1,),
        out_shape=outs,
        in_specs=[pl.BlockSpec(memory_space=pltpu.SMEM)]
        + [
            pl.BlockSpec(memory_space=pl.ANY) if i in fetched else whole(a)
            for i, a in enumerate(arrays)
        ],
        out_specs=[whole(a) for a in outs],
        scratch_shapes=scratch,
        compiler_params=FETCHING if fetched else PARAMS,
        cost_estimate=pl.CostEstimate(flops=flops, bytes_accessed=8 * 2**20, transcendentals=0),
    )(place, *arrays)


def attend(place, msgs, sib):
    head = (4, HEAD_DIM, BLOCK)
    scratch = [
        pltpu.VMEM((1, BLOCK), F32),
        pltpu.VMEM((1, BLOCK), F32),
        pltpu.VMEM((HEAD_DIM, BLOCK), F32),
        pltpu.VMEM((4, MSG, BLOCK), BF),
        pltpu.VMEM((4, 2 * HEAD_DIM, BLOCK), BF),
        pltpu.SemaphoreType.DMA((5,)),
    ]
    shapes = ((head, F32), (head, BF), ((4, 1, BLOCK), F32))
    scratch = KV_SCRATCH + scratch
    return whole_call(
        forward_kernel, shapes, scratch, 10**10, place, *msgs, sib, fetched=range(5)
    )


def attend_back(place, msgs, sib, mixed, logs, grads):
    pair = (4, 2 * HEAD_DIM, BLOCK)
    scratch = [
        pltpu.VMEM((4, HEAD_DIM, BLOCK), BF),
        pltpu.VMEM((8, BLOCK, HEAD_DIM), F32),
        pltpu.VMEM((8, BLOCK, HEAD_DIM), F32),
        pltpu.VMEM((HEAD_DIM, BLOCK), F32),
        pltpu.VMEM((4, MSG, BLOCK), BF),
        pltpu.VMEM(pair, BF),
        pltpu.VMEM((4, HEAD_DIM, BLOCK), F32),
        pltpu.VMEM((4, 1, BLOCK), F32),
        pltpu.SemaphoreType.DMA((7,)),
    ]
    shapes = (((4, HEAD_DIM, BLOCK), BF), (pair, F32), (pair, BF))
    arrays = (*msgs, sib, mixed, logs, *grads)
    scratch = KV_SCRATCH + scratch
    return whole_call(
        backward_kernel, shapes, scratch, 2 * 10**10, place, *arrays, fetched=range(7)
    )


def split_cores(place, mine, away, at, width, result):
    rows = result.reshape(16, 2, 32, width)
    even, odd = rows[:, 0].reshape(512, width), rows[:, 1].reshape(512, width)
    mine[:, at : at + width] = jnp.where(place[1] == 0, even, odd).astype(BF)
    away[:, at : at + width] = jnp.where(place[1] == 0, odd, even).astype(BF)


def weights_kernel(place, *refs):
    normed, grad_pre, grad, active, (out, turned) = (*[refs[i : i + 4] for i in (0, 4, 8, 12)], refs[16:])
    step = pl.program_id(0)
    at = pl.ds(pl.multiple_of((step & 3) * 256, 256), 256)

    def turn(chunks):
        for d, a in enumerate(chunks):
            turned[:, 128 * d : 128 * (d + 1)] = a[...].T

    def columns(chunks):
        return dot(turned[...], jnp.concatenate([a[:, at] for a in chunks], axis=0), 1, 0)

    @pl.when(step == 0)
    def _():
        turn(normed)

    @pl.when(step == 4)
    def _():
        turn(grad)

    @pl.when(step < 4)
    def _():
        out[...] = columns(grad_pre).astype(BF)

    @pl.when(step >= 4)
    def _():
        out[...] = columns(active).astype(BF)


def weight_grads(place, normed, grad_pre, grad, active):
    chunk = pl.BlockSpec((128, 1024), lambda i: (0, 0))
    return pl.pallas_call(
        weights_kernel,
        grid=(8,),
        out_shape=jax.ShapeDtypeStruct((1024, 2048), BF),
        in_specs=[pl.BlockSpec(memory_space=pltpu.SMEM)] + [chunk] * 16,
        out_specs=pl.BlockSpec((1024, 256), lambda i: (0, i)),
        scratch_shapes=[pltpu.VMEM((1024, 512), BF)],
        compiler_params=PARAMS,
        cost_estimate=pl.CostEstimate(flops=4 * 2**30, bytes_accessed=8 * 2**20, transcendentals=0),
    )(place, *normed, *grad_pre, *grad, *active)


def down_kernel(place, g0, g1, g2, g3, down, o0, o1, o2, o3, *, side):
    for g, o in zip((g0, g1, g2, g3), (o0, o1, o2, o3)):
        o[...] = dot(g[...], down[...], 1, side).astype(o.dtype)


def with_down(place, chunks, ff_all, side, kinds):
    chunk = pl.BlockSpec((128, 1024), lambda i: (0, 0))
    return pl.pallas_call(
        functools.partial(down_kernel, side=side),
        grid=(1,),
        out_shape=[jax.ShapeDtypeStruct((128, 1024), kind) for kind in kinds],
        in_specs=[pl.BlockSpec(memory_space=pltpu.SMEM)]
        + [chunk] * 4
        + [pl.BlockSpec((1024, 1024), lambda i: (0, 1))],
        out_specs=[chunk] * 4,
        compiler_params=PARAMS,
        cost_estimate=pl.CostEstimate(flops=2**30, bytes_accessed=8 * 2**20, transcendentals=0),
    )(place, *chunks, ff_all)


def feed_kernel(place, *refs, n):
    normed, grad, (up, down, vectors), outs = refs[:n], refs[n : 2 * n], refs[2 * n : 2 * n + 3], refs[2 * n + 3 :]
    rows = jnp.concatenate([a[...] for a in normed], axis=0)
    upstream = jnp.concatenate([a[...] for a in grad], axis=0)
    value, slope = gelu_pair(dot(rows, up[...], 1, 0) + vectors[4:5])
    low = (dot(upstream, down[...], 1, 0) * slope).astype(BF)
    part = dot(low, up[...], 1, 1)
    value = value.astype(BF)
    for i in range(n):
        at = slice(128 * i, 128 * (i + 1))
        active, grad_pre, own = outs[3 * i : 3 * i + 3]
        active[...] = value[at]
        grad_pre[...] = low[at]
        own[...] = part[at].astype(own.dtype)
    outs[3 * n][...] = jnp.sum(low.astype(F32), axis=0, keepdims=True)


def feed_chunks(place, normed, grad, ff_all, vectors, kinds):
    n = len(normed)
    chunk = pl.BlockSpec((128, 1024), lambda i: (0, 0))
    shape = (128, 1024)
    outs = []
    for kind in kinds:
        outs += [jax.ShapeDtypeStruct(shape, k) for k in (BF, BF, kind)]
    *outs, columns = pl.pallas_call(
        functools.partial(feed_kernel, n=n),
        grid=(1,),
        out_shape=outs + [jax.ShapeDtypeStruct((1, 1024), F32)],
        in_specs=[pl.BlockSpec(memory_space=pltpu.SMEM)]
        + [chunk] * (2 * n)
        + [
            pl.BlockSpec((1024, 1024), lambda i: (0, 0)),
            pl.BlockSpec((1024, 1024), lambda i: (0, 1)),
            pl.BlockSpec((8, 1024), lambda i: (0, 0)),
        ],
        out_specs=[chunk] * (3 * n) + [pl.BlockSpec((1, 1024), lambda i: (0, 0))],
        compiler_params=PARAMS,
        cost_estimate=pl.CostEstimate(flops=n * 2**33, bytes_accessed=4 * 2**20, transcendentals=0),
    )(place, *normed, *grad, ff_all, ff_all, vectors)
    return [outs[3 * i : 3 * i + 3] for i in range(n)], columns


def vectors_kernel(place, block, out):
    rows = block[...].astype(F32).T
    out[...] = jnp.concatenate([rows[0:4] + rows[4:8], rows[8:9], rows[9:12]], axis=0)


def vector_rows(place, ff_all):
    return pl.pallas_call(
        vectors_kernel,
        grid=(1,),
        out_shape=jax.ShapeDtypeStruct((8, 1024), F32),
        in_specs=[
            pl.BlockSpec(memory_space=pltpu.SMEM),
            pl.BlockSpec((1024, 128), lambda i: (0, 24)),
        ],
        out_specs=pl.BlockSpec((8, 1024), lambda i: (0, 0)),
        compiler_params=PARAMS,
    )(place, ff_all)


def last_kernel(
    place, dq_far, own_far, away_far, normed, m0, m1, m2, m3, mixed_far, vectors_far,
    b0, b1, b2, b3, mine, away,
    dq, own, other, n_s, m_s, mixed, vectors, done,
):
    blocks = []
    for d in range(4):
        at = pl.multiple_of(lax.rem(place[0] - d + 4, 4) * BLOCK, BLOCK)
        blocks.append(normed.at[pl.ds(at, BLOCK), :])
    started = copies(
        (dq_far, own_far, away_far, *blocks, m0, m1, m2, m3, mixed_far, vectors_far),
        (dq, own, other, *[n_s.at[d] for d in range(4)], *[m_s.at[d] for d in range(4)], mixed, vectors),
        done,
    )
    for copy in started[:3]:
        copy.wait()
    dqkv = (b0, b1, b2, b3)
    weights = jnp.zeros((192, 1024), F32)
    for d in range(4):
        pair = (own[d] + other[d].astype(F32)).astype(BF)
        dqkv[d][...] = jnp.concatenate([dq[d], pair], axis=0)
        started[3 + d].wait()
        weights += dot(dqkv[d][...], n_s[d], 1, 0)
    for copy in started[7:]:
        copy.wait()
    outs = sum(dot(mixed[:, 128 * d : 128 * (d + 1)], m_s[d], 1, 0) for d in range(4))
    split_cores(place, mine, away, 0, 256, outs.T)
    padding = jnp.zeros((64, 1024), F32)
    split_cores(place, mine, away, 384, 256, jnp.concatenate([weights, padding], axis=0).T)
    ones = jnp.ones((8, BLOCK), BF)
    columns = sum(dot(ones, dqkv[d][...], 1, 1) for d in range(4))[0:1]
    pad = jnp.zeros((1, 64), F32)
    columns = [jnp.concatenate([pad, columns[:, 64 * i : 64 * (i + 1)]], axis=1) for i in range(3)]
    row = lax.broadcasted_iota(jnp.int32, (1024, 128), 0) & 31
    small = jnp.concatenate([vectors[...].T, jnp.zeros((1024, 120), F32)], axis=1)
    for i in range(3):
        small += jnp.where(row == i, columns[i], 0.0)
    split_cores(place, mine, away, 256, 128, small)


def last_grads(place, *arrays):
    scratch = [
        pltpu.VMEM((4, HEAD_DIM, BLOCK), BF),
        pltpu.VMEM((4, 2 * HEAD_DIM, BLOCK), F32),
        pltpu.VMEM((4, 2 * HEAD_DIM, BLOCK), BF),
        pltpu.VMEM((4, BLOCK, 1024), BF),
        pltpu.VMEM((4, 128, 1024), BF),
        pltpu.VMEM((256, BLOCK), BF),
        pltpu.VMEM((8, 1024), F32),
        pltpu.SemaphoreType.DMA((13,)),
    ]
    shapes = (((192, BLOCK), BF),) * 4 + (((512, 640), BF),) * 2
    *dqkv, mine, away = whole_call(
        last_kernel, shapes, scratch, 2**31, place, *arrays, fetched=range(10)
    )
    return dqkv, mine, away


def rows_kernel(place, b0, b1, b2, b3, weights, p1, p2, p3, own, s1, s2, s3, heads):
    for d, b in enumerate((b0, b1, b2, b3)):
        heads[pl.ds(pl.multiple_of(lax.rem(place[0] + d, 4) * 192, 64), 192), :] = b[...]
    own[...] = dot(heads[:, :128].T, weights[:, :768], 1, 1)
    for d, (p, out) in enumerate(((p1, s1), (p2, s2), (p3, s3)), 1):
        out[:128, :] = p[...]
        rows = heads[:, 128 * d : 128 * (d + 1)].T
        out[128:, :] = dot(rows, weights[:, :768], 1, 1).astype(BF)


def row_grads(place, *arrays):
    shapes = (((128, 1024), F32),) + (((256, 1024), BF),) * 3
    return whole_call(rows_kernel, shapes, [pltpu.VMEM((768, BLOCK), BF)], 2**30, place, *arrays)


def finish_kernel(
    place, g0, g1, g2, g3, w_qkv, own, ff, qkv, w_out, columns, vectors, up, down, m_s, k_s
):
    got = (g0, g1, g2, g3)
    up[...] = ff[:, :1024].astype(F32)
    down[...] = ff[:, 1024:].astype(F32)
    w_out[...] = total([g[:, :256] for g in got])
    rest = total([g[:, 256:384] for g in got])
    for d, g in enumerate(got):
        head = lax.rem(place[0] - d + 4, 4)
        m_s[head] = g[:, 384:576].astype(F32)
        k_s[head] = g[0:16, 256:384].astype(F32)
    gain, shift = own[:, 0:1], own[:, 2:3]
    gain_sum, shift_sum = jnp.zeros((32, 64), F32), jnp.zeros((32, 64), F32)
    for h in range(4):
        for i in range(3):
            at = slice(64 * h, 64 * (h + 1))
            m, k = m_s[h, :, 64 * i : 64 * (i + 1)], k_s[h, i : i + 1, 64:128]
            w = w_qkv[i, :, at].astype(F32)
            qkv[i, :, at] = gain * m + shift * k
            columns[i : i + 1, at] = k
            gain_sum += w * m
            shift_sum += w * k
    gain_sum = jnp.sum(gain_sum, axis=1, keepdims=True)
    shift_sum = jnp.sum(shift_sum, axis=1, keepdims=True)
    rows = jnp.concatenate(
        [gain_sum, rest[:, 0:1], shift_sum, rest[:, 1:5], jnp.zeros((32, 121), F32)], axis=1
    )
    vectors[...] = rows.T[:8]


def finish(place, *arrays):
    shapes = ((3, 32, 256), (32, 256), (3, 256), (8, 32), (32, 1024), (32, 1024))
    scratch = [pltpu.VMEM((4, 32, 192), F32), pltpu.VMEM((4, 16, 128), F32)]
    return whole_call(
        finish_kernel, [(shape, F32) for shape in shapes], scratch, 2**28, place, *arrays
    )


def middle_kernel(place, x0, x1, x2, x3, out, tokens, vectors, middle, normed):
    mixed = jnp.concatenate([x[...].T for x in (x0, x1, x2, x3)], axis=1)
    rows = tokens[...].astype(F32) + dot(mixed, out[...], 1, 1) + vectors[2:3]
    middle[...] = rows
    normed[...] = (normalized(rows)[0] * vectors[0:1] + vectors[1:2]).astype(BF)


def middle_back_kernel(
    place, part, a1, a2, a3, out, middle, grad, vectors, grad_middle, low, h0, h1, h2, h3, sums
):
    grad_two = part[...] + a1[...].astype(F32) + a2[...].astype(F32) + a3[...].astype(F32)
    normed, scale = normalized(middle[...])
    upstream = grad[...].astype(F32)
    rows = upstream + norm_back(grad_two, normed, scale, vectors[0:1])
    rows_low = rows.astype(BF)
    grad_middle[...] = rows
    low[...] = rows_low
    heads = dot(rows_low, out[...], 1, 0).T.astype(BF)
    for d, h in enumerate((h0, h1, h2, h3)):
        h[...] = heads[256 * d : 256 * (d + 1)]
    terms = (grad_two * normed, grad_two, rows, upstream)
    sums[...] = jnp.concatenate([jnp.sum(a, axis=0, keepdims=True) for a in terms], axis=0)


def tokens_kernel(
    place, part, a1, a2, a3, tokens, grad_middle, middle, second, vectors, grad_tokens, output
):
    terms = a1[...].astype(F32) + a2[...].astype(F32) + a3[...].astype(F32)
    normed, scale = normalized(tokens[...].astype(F32))
    grad = part[...] + terms[128:]
    grad_tokens[...] = grad_middle[...] + norm_back(grad, normed, scale, 1.0)
    output[...] = middle[...] + second[...] + terms[:128] + vectors[3:4]


def with_out(kernel, shapes, before, ff_all, after, place):
    def whole(a):
        return pl.BlockSpec(a.shape, lambda i, rank=len(a.shape): (0,) * rank)

    outs = [jax.ShapeDtypeStruct(*shape) for shape in shapes]
    return pl.pallas_call(
        kernel,
        grid=(1,),
        out_shape=outs,
        in_specs=[pl.BlockSpec(memory_space=pltpu.SMEM)]
        + [whole(a) for a in before]
        + [pl.BlockSpec((1024, 1024), lambda i: (0, 2))]
        + [whole(a) for a in after],
        out_specs=[whole(a) for a in outs],
        compiler_params=PARAMS,
        cost_estimate=pl.CostEstimate(flops=2**29, bytes_accessed=4 * 2**20, transcendentals=0),
    )(place, *before, ff_all, *after)


def gelu_pair(v):
    root = 0.7978845608028654
    square = v * v
    t = jnp.tanh(root * v * (1.0 + 0.044715 * square))
    half = 0.5 * (1.0 + t)
    slope = half + 0.5 * v * (1.0 - t * t) * (root * (1.0 + 3 * 0.044715 * square))
    return v * half, slope


def local(
    tokens, doc_start, norm_gains, norm_biases, out_biases, w_qkv, b_qv, w_out, w_up, b_up,
    w_down, out_grad,
):
    f = lax.axis_index("fsdp")
    x, y, c = f // 8, (f // 2) % 4, f % 2
    t = lax.axis_index("tp")
    place = jnp.stack([y, c, t]).astype(jnp.int32)

    vectors = jnp.concatenate([norm_gains, norm_biases, out_biases], axis=0).reshape(1, 48)
    vectors = jnp.concatenate(halves(vectors), axis=1)
    packed = jnp.concatenate([w_out.T, jnp.pad(vectors, ((0, 15), (0, 160)))], axis=0)
    qkv_local = w_qkv.reshape(3, 32, 4, 64).transpose(1, 2, 0, 3).reshape(32, 768)
    packed = from_all(packed, along_z)
    out_columns = [p[:32] for p in packed]
    own_vectors = in_order([p[32:33, :96].astype(F32) for p in packed], t)
    own_vectors = (own_vectors[:, :48] + own_vectors[:, 48:]).reshape(4, 6, 8)
    own_vectors = own_vectors.transpose(0, 2, 1).reshape(32, 6)
    gain, shift = own_vectors[:, 0:1], own_vectors[:, 2:3]

    weights = qkv_local.astype(F32)
    bias = jnp.sum(shift * weights, axis=0).reshape(4, 3, 64)
    qv_bias = jnp.stack([b_qv[0], jnp.zeros_like(b_qv[0]), b_qv[1]], axis=1).astype(F32)
    here = (jnp.arange(4)[:, None] == f // 8) & (jnp.arange(64)[None] // 8 == f % 8)
    bias = bias + jnp.where(here[:, None], jnp.tile(qv_bias, (1, 1, 8)), 0.0)
    bias = jnp.concatenate(halves(bias.reshape(6, 128)), axis=0)
    bias = jnp.pad(bias, ((0, 20), (0, 0)))
    by_y = from_all(jnp.concatenate([(gain * weights).astype(BF), bias], axis=1), along_y)
    by_x = from_all(placed_in_order(by_y, y), along_x)

    others = jnp.stack([own_vectors[:, i] for i in (1, 3, 4, 5)], axis=1)
    others = jnp.concatenate([*halves(others), b_up.reshape(32, 1), jnp.zeros((32, 119), BF)], axis=1)
    ff_local = jnp.concatenate([w_up, w_down.T, *out_columns, others], axis=1)
    ff_all = lax.all_gather(ff_local, "fsdp", axis=0, tiled=True)
    out_all = ff_all[:, 2048:3072]

    rows = from_all(tokens, along_z)
    rows, out_grad = lax.optimization_barrier((rows, out_grad))
    full_grad = from_all(out_grad, along_z)
    rows = jnp.concatenate(rows, axis=0)
    n_one, scale_one = normalized(rows.astype(F32))
    n_one_low = n_one.astype(BF)

    attn_all = both_cores(placed_in_order(by_x, x), c, 32)
    qkv_all = attn_all[:, :768]
    bias = attn_all[:, 768:].reshape(32, 32, 128)[:, :12].astype(F32).sum(axis=0)
    qkv = dot(qkv_all, n_one_low, 0, 1) + (bias[:6] + bias[6:]).reshape(768, 1)
    qkv = qkv.astype(BF)

    first = (doc_start - x * 4096).reshape(4, 128)
    first = jnp.concatenate(
        [lax.dynamic_slice_in_dim(first, (t - d) % 4, 1, axis=0) for d in range(4)], axis=0
    ).reshape(1, BLOCK)
    first = jnp.concatenate([first // 64, first % 64, jnp.zeros((14, BLOCK), jnp.int32)], axis=0)
    first = first.astype(BF)

    def message(d):
        return jnp.concatenate([piece(qkv, (y + d) % 4, 192), first], axis=0)

    msgs = [message(0)] + [along_y(message(d), d) for d in (1, 2, 3)]
    msgs, full_grad = lax.optimization_barrier((msgs, full_grad))
    sib = other_core(jnp.stack([m[64:192] for m in msgs]))
    mixed, mixed_low, logs = attend(place, msgs, sib)
    vectors = vector_rows(place, ff_all)
    vector_rows_all = vectors

    back = [mixed_low[0]] + [along_y(mixed_low[d], -d) for d in (1, 2, 3)]
    back, vectors = lax.optimization_barrier((back, vectors))
    mixed_own = in_order([back[0], back[3], back[2], back[1]], y)
    by_z = [mixed_own[:, 128 * d : 128 * (d + 1)] for d in range(4)]
    by_z = [by_z[0]] + [along_z(by_z[d], -d) for d in (1, 2, 3)]
    by_z, n_one_low, mixed_own = lax.optimization_barrier((by_z, n_one_low, mixed_own))
    alike = [[(x * 4 + y) * 2 + c for y in range(4)] for x in range(4) for c in range(2)]
    n_all = lax.all_gather(n_one_low, "fsdp", axis=0, tiled=True, axis_index_groups=alike)

    row = (128, 1024)
    before = (by_z[0], by_z[3], by_z[2], by_z[1])
    middle, normed_two = with_out(
        middle_kernel, ((row, F32), (row, BF)), before, ff_all, (tokens, vectors), place
    )
    near_one, near_three = along_z(normed_two, 1), along_z(normed_two, 3)
    far = jnp.concatenate([along_z(near_one[:64], 1), along_z(near_three[64:], 3)], axis=0)
    full_two = [normed_two, near_one, far, near_three]
    near = [0, 1, 3]
    fed, grad_bup = feed_chunks(
        place, [full_two[d] for d in near], [full_grad[d] for d in near], ff_all, vectors, [F32, BF, BF]
    )
    far, fed, grad_bup = lax.optimization_barrier((full_two[2], fed, grad_bup))
    last, more_bup = feed_chunks(place, [far], [full_grad[2]], ff_all, vectors, [BF])
    active, grad_pre, part = zip(fed[0], fed[1], last[0], fed[2])
    arrived = [along_z(part[d], -d) for d in (1, 2, 3)]
    ff_grads = weight_grads(place, full_two, grad_pre, full_grad, active)
    arrived, ff_grads, active = lax.optimization_barrier((arrived, ff_grads, active))
    mlp_part = with_down(place, active, ff_all, 1, [F32, BF, BF, BF])
    grad_bup = grad_bup + more_bup
    ff_grads = lax.psum_scatter(ff_grads, "fsdp", scatter_dimension=0, tiled=True)

    heads = ((256, 128), BF)
    grad_middle, middle_low, *grad_mixed, sums = with_out(
        middle_back_kernel,
        ((row, F32), (row, BF), heads, heads, heads, heads, ((4, 1024), F32)),
        (part[0], *arrived),
        ff_all,
        (middle, out_grad, vectors),
        place,
    )
    by_z = [grad_mixed[0]] + [along_z(grad_mixed[d], -d) for d in (1, 2, 3)]
    by_z, middle_low, mlp_part = lax.optimization_barrier((by_z, middle_low, mlp_part))
    full_middle = from_all(middle_low, along_z)
    grad_heads = jnp.concatenate([by_z[0], by_z[3], by_z[2], by_z[1]], axis=1)
    grads = [piece(grad_heads, y, 64)] + [
        along_y(piece(grad_heads, (y + d) % 4, 64), d) for d in (1, 2, 3)
    ]
    dq, own, away = attend_back(place, msgs, sib, mixed, logs, grads)
    dq, own, away, full_middle = lax.optimization_barrier((dq, own, away, full_middle))
    away = other_core(away)
    sums = jnp.concatenate([sums, grad_bup, jnp.zeros((3, 1024), F32)], axis=0)
    dqkv, mine, away = last_grads(place, dq, own, away, n_all, *full_middle, mixed_own, sums)
    away = other_core(away)
    back = [dqkv[0]] + [along_y(dqkv[d], -d) for d in (1, 2, 3)]
    back, mine, away = lax.optimization_barrier((back, mine, away))
    got = scattered(added(mine, away), along_x, x, 128)
    part, *sent = row_grads(place, *back, attn_all, *mlp_part[1:])
    grad_one = [along_z(sent[d - 1], -d) for d in (1, 2, 3)]
    got, grad_one[0], grad_one[2] = lax.optimization_barrier((got, grad_one[0], grad_one[2]))
    got = scattered(total(got).astype(BF), along_y, y, 32)
    got, grad_one = lax.optimization_barrier((got, grad_one))
    out_qkv, out_wout, columns, vectors, out_wup, out_wdown = finish(
        place, got[0], got[2], got[1], got[3], w_qkv, own_vectors, ff_grads
    )
    arrays = (part, *grad_one, tokens, grad_middle, middle, mlp_part[0], vector_rows_all)
    grad_tokens, output = whole_call(
        tokens_kernel, ((row, F32),) * 2, [], 2**28, place, *arrays
    )
    out_wdown, out_wout = out_wdown.T, out_wout.T
    out_bup = vectors[6:7]
    columns = jnp.concatenate([columns[0:1], columns[2:3]], axis=0).reshape(2, 32, 8)
    out_bqv = lax.dynamic_slice_in_dim(columns, f, 1, axis=1)
    pieces = [lax.dynamic_slice_in_dim(vectors, (t + d) % 4 * 8, 8, axis=1) for d in range(4)]
    vectors = pieces[0] + sum(along_z(pieces[d], d) for d in (1, 2, 3))
    return (
        output,
        grad_tokens,
        vectors[0:2],
        vectors[2:4],
        vectors[4:6],
        out_qkv,
        out_bqv,
        out_wout,
        out_wup,
        out_bup,
        out_wdown,
    )


def solution(mesh):
    by_rows = P(("fsdp", "tp"), None)
    by_features = P(None, ("fsdp", "tp"))
    weights = (
        P(None, "fsdp", "tp"),
        P(None, "tp", "fsdp"),
        P("tp", "fsdp"),
        P("fsdp", "tp"),
        P("tp", "fsdp"),
        P("tp", "fsdp"),
    )
    return jax.shard_map(
        local,
        mesh=mesh,
        in_specs=(by_rows, P("fsdp"), by_features, by_features, by_features, *weights, by_rows),
        out_specs=(by_rows, by_rows, by_features, by_features, by_features, *weights),
        check_vma=False,
    )
```

```python
import functools

import jax
import jax.numpy as jnp
from jax import lax
from jax.experimental import pallas as pl
from jax.experimental.pallas import tpu as pltpu
from jax.sharding import PartitionSpec as P

HEAD_DIM = 64
BLOCK = 512
MSG = 208
EPSILON = 1e-05
MASKED = -1e30
BF = jnp.bfloat16
F32 = jnp.float32


def along_y(a, d):
    pairs = [
        ((x * 4 + y) * 2 + c, (x * 4 + (y + d) % 4) * 2 + c)
        for x in range(4)
        for y in range(4)
        for c in range(2)
    ]
    return lax.ppermute(a, "fsdp", pairs)


def along_x(a, d):
    pairs = [
        ((x * 4 + y) * 2 + c, (((x + d) % 4) * 4 + y) * 2 + c)
        for x in range(4)
        for y in range(4)
        for c in range(2)
    ]
    return lax.ppermute(a, "fsdp", pairs)


def other_core(a):
    return lax.ppermute(a, "fsdp", [(i, i ^ 1) for i in range(32)])


def along_z(a, d):
    return lax.ppermute(a, "tp", [(i, (i + d) % 4) for i in range(4)])


def from_all(a, move):
    return [a, move(a, 1), move(a, 2), move(a, 3)]


def in_order(rel, me):
    n = rel[0].shape[0]
    turned = [rel[0], rel[3], rel[2], rel[1]]
    twice = jnp.concatenate(turned + turned[:3], axis=0)
    return lax.dynamic_slice_in_dim(twice, ((4 - me) % 4) * n, 4 * n, axis=0)


def placed_in_order(rel, me):
    n = rel[0].shape[0]
    out = jnp.zeros((4 * n, *rel[0].shape[1:]), rel[0].dtype)
    for d, a in enumerate(rel):
        out = lax.dynamic_update_slice_in_dim(out, a, ((me - d) % 4) * n, axis=0)
    return out


def piece(a, at, n):
    return lax.dynamic_slice_in_dim(a, at * n, n, axis=0)


def added(mine, theirs):
    return (mine.astype(F32) + theirs.astype(F32)).astype(BF)


def scattered(a, move, me, n):
    return [piece(a, me, n)] + [move(piece(a, (me + d) % 4, n), d) for d in (2, 1, 3)]


def total(terms):
    return sum(a.astype(F32) for a in terms)


def halves(v):
    high = lax.reduce_precision(v, 8, 7)
    return high.astype(BF), (v - high).astype(BF)


def normalized(values):
    centred = values - jnp.mean(values, axis=-1, keepdims=True)
    spread = jnp.mean(centred * centred, axis=-1, keepdims=True)
    scale = lax.rsqrt(spread + EPSILON)
    return centred * scale, scale


def norm_back(grad, normed, scale, gain):
    e = grad * gain
    return scale * (
        e
        - jnp.mean(e, axis=-1, keepdims=True)
        - normed * jnp.mean(e * normed, axis=-1, keepdims=True)
    )


def dot(a, b, ca, cb):
    return lax.dot_general(a, b, (((ca,), (cb,)), ((), ())), preferred_element_type=F32)


def unpack(place, msgs, sib, q_s, kt_s, vt_s, start_s, k_s, v_s):
    y, c = place[0], place[1]
    for d in range(4):
        block = lax.rem(y - d + 4, 4) * 2
        msg = msgs[d]
        q_s[d] = msg[0:64, :] * BF(0.125)
        first = msg[192:208, :].astype(F32)
        start_s[d] = first[0:1] * 64.0 + first[1:2]
        k, v = msg[64:128, :], msg[128:192, :]
        kt_s[block + c] = k.T
        vt_s[block + c] = v.T
        k_s[block + c] = k
        v_s[block + c] = v
        k, v = sib[d, 0:64, :], sib[d, 64:128, :]
        kt_s[block + 1 - c] = k.T
        vt_s[block + 1 - c] = v.T
        k_s[block + 1 - c] = k
        v_s[block + 1 - c] = v


def positions(place, axis):
    shape = (BLOCK, 1) if axis == 0 else (1, BLOCK)
    at = lax.broadcasted_iota(jnp.int32, shape, axis)
    chunk = (place[2] - (at >> 7)) & 3
    return ((chunk << 7) + (at & 127)).astype(F32)


def allowed_in(place, start, key_block, mode):
    if mode == 0:
        return None
    key_pos = positions(place, 0)
    allowed = key_pos >= start - (key_block * BLOCK).astype(F32)
    if mode == 2:
        allowed = allowed & (key_pos <= positions(place, 1))
    return allowed


def over_keys(start, block, step):
    low = jnp.min(start).astype(jnp.int32) // BLOCK
    last = jnp.max(start).astype(jnp.int32)

    def body(key_block, carry):
        @pl.when(key_block * BLOCK < last)
        def _():
            step(key_block, 1)

        @pl.when(key_block * BLOCK >= last)
        def _():
            step(key_block, 0)

        return carry

    lax.fori_loop(low, block, body, 0)
    step(block, 2)


def copies(sources, targets, done):
    started = [
        pltpu.make_async_copy(source, target, done.at[i])
        for i, (source, target) in enumerate(zip(sources, targets))
    ]
    for copy in started:
        copy.start()
    return started


def forward_kernel(
    place, m0, m1, m2, m3, sib_far, mixed, l0, l1, l2, l3, logs,
    q_s, kt_s, vt_s, start_s, k_s, v_s, peak_s, total_s, acc_s, msgs, sib, done,
):
    near = [msgs.at[d] for d in range(4)]
    for copy in copies((m0, m1, m2, m3, sib_far), (*near, sib), done):
        copy.wait()
    unpack(place, near, sib, q_s, kt_s, vt_s, start_s, k_s, v_s)

    def queries(d, carry):
        block = lax.rem(place[0] - d + 4, 4) * 2 + place[1]
        start = start_s[d]
        peak_s[...] = jnp.full((1, BLOCK), MASKED, F32)
        total_s[...] = jnp.zeros((1, BLOCK), F32)
        acc_s[...] = jnp.zeros((HEAD_DIM, BLOCK), F32)

        def step(key_block, mode):
            allowed = allowed_in(place, start, key_block, mode)
            halves_at = [slice(0, 256), slice(256, 512)]
            scores = [dot(kt_s[key_block], q_s[d, :, at], 1, 0) for at in halves_at]
            if allowed is not None:
                scores = [
                    jnp.where(allowed[:, at], s, MASKED) for at, s in zip(halves_at, scores)
                ]
            for at, s in zip(halves_at, scores):
                old = peak_s[:, at]
                peak = jnp.maximum(old, jnp.max(s, axis=0, keepdims=True))
                p = jnp.exp(s - peak)
                shrink = jnp.exp(old - peak)
                peak_s[:, at] = peak
                total_s[:, at] = total_s[:, at] * shrink + jnp.sum(p, axis=0, keepdims=True)
                acc_s[:, at] = acc_s[:, at] * shrink + dot(v_s[key_block], p.astype(BF), 1, 0)

        over_keys(start, block, step)
        out = acc_s[...] / total_s[...]
        mixed[d] = out
        logs[d] = peak_s[...] + jnp.log(total_s[...])
        return carry

    lax.fori_loop(0, 4, queries, 0)
    for d, low in enumerate((l0, l1, l2, l3)):
        low[...] = mixed[d].astype(BF)


def backward_kernel(
    place, m0, m1, m2, m3, sib_far, mixed_far, logs_far, g0, g1, g2, g3, dq, own, away,
    q_s, kt_s, vt_s, start_s, k_s, v_s, g_s, dk_s, dv_s, acc_s, msgs, sib, mixed, logs, done,
):
    started = copies(
        (m0, m1, m2, m3, sib_far, mixed_far, logs_far),
        (*[msgs.at[d] for d in range(4)], sib, mixed, logs),
        done,
    )
    for d, g in enumerate((g0, g1, g2, g3)):
        g_s[d] = g[...]
    dk_s[...] = jnp.zeros(dk_s.shape, F32)
    dv_s[...] = jnp.zeros(dv_s.shape, F32)
    for copy in started:
        copy.wait()
    unpack(place, [msgs.at[d] for d in range(4)], sib, q_s, kt_s, vt_s, start_s, k_s, v_s)

    def queries(d, carry):
        block = lax.rem(place[0] - d + 4, 4) * 2 + place[1]
        start = start_s[d]
        log = logs[d]
        grad = g_s[d]
        q = q_s[d]
        delta = jnp.sum(grad.astype(F32) * mixed[d], axis=0, keepdims=True)
        qt = q.T
        gt = grad.T
        acc_s[...] = jnp.zeros((HEAD_DIM, BLOCK), F32)

        def step(key_block, mode):
            allowed = allowed_in(place, start, key_block, mode)
            grads, probs = [], []
            for at in (slice(0, 256), slice(256, 512)):
                p = jnp.exp(dot(kt_s[key_block], q[:, at], 1, 0) - log[:, at])
                if allowed is not None:
                    p = jnp.where(allowed[:, at], p, 0.0)
                dp = dot(vt_s[key_block], grad[:, at], 1, 0)
                grads.append((p * (dp - delta[:, at])).astype(BF))
                probs.append(p.astype(BF))
            ds = jnp.concatenate(grads, axis=1)
            dv_s[key_block] += dot(jnp.concatenate(probs, axis=1), gt, 1, 0)
            dk_s[key_block] += dot(ds, qt, 1, 0)
            acc_s[...] += dot(k_s[key_block], ds, 1, 0)

        over_keys(start, block, step)
        dq[d] = (acc_s[...] * 0.125).astype(BF)
        return carry

    lax.fori_loop(0, 4, queries, 0)
    for d in range(4):
        block = lax.rem(place[0] - d + 4, 4) * 2
        own[d, 0:64, :] = dk_s[block + place[1]].T
        own[d, 64:128, :] = dv_s[block + place[1]].T
        away[d, 0:64, :] = dk_s[block + 1 - place[1]].T.astype(BF)
        away[d, 64:128, :] = dv_s[block + 1 - place[1]].T.astype(BF)


KV_SCRATCH = [
    pltpu.VMEM((4, HEAD_DIM, BLOCK), BF),
    pltpu.VMEM((8, BLOCK, HEAD_DIM), BF),
    pltpu.VMEM((8, BLOCK, HEAD_DIM), BF),
    pltpu.VMEM((4, 1, BLOCK), F32),
    pltpu.VMEM((8, HEAD_DIM, BLOCK), BF),
    pltpu.VMEM((8, HEAD_DIM, BLOCK), BF),
]
PARAMS = pltpu.CompilerParams(vmem_limit_bytes=48 * 1024 * 1024)
FETCHING = pltpu.CompilerParams(vmem_limit_bytes=60 * 1024 * 1024)


def whole_call(kernel, shapes, scratch, flops, place, *arrays, fetched=()):
    def whole(a):
        return pl.BlockSpec(a.shape, lambda i, rank=len(a.shape): (0,) * rank)

    outs = [jax.ShapeDtypeStruct(*shape) for shape in shapes]
    return pl.pallas_call(
        kernel,
        grid=(1,),
        out_shape=outs,
        in_specs=[pl.BlockSpec(memory_space=pltpu.SMEM)]
        + [
            pl.BlockSpec(memory_space=pl.ANY) if i in fetched else whole(a)
            for i, a in enumerate(arrays)
        ],
        out_specs=[whole(a) for a in outs],
        scratch_shapes=scratch,
        compiler_params=FETCHING if fetched else PARAMS,
        cost_estimate=pl.CostEstimate(flops=flops, bytes_accessed=8 * 2**20, transcendentals=0),
    )(place, *arrays)


def attend(place, msgs, sib):
    head = (4, HEAD_DIM, BLOCK)
    scratch = [
        pltpu.VMEM((1, BLOCK), F32),
        pltpu.VMEM((1, BLOCK), F32),
        pltpu.VMEM((HEAD_DIM, BLOCK), F32),
        pltpu.VMEM((4, MSG, BLOCK), BF),
        pltpu.VMEM((4, 2 * HEAD_DIM, BLOCK), BF),
        pltpu.SemaphoreType.DMA((5,)),
    ]
    shapes = ((head, F32), *[((HEAD_DIM, BLOCK), BF)] * 4, ((4, 1, BLOCK), F32))
    scratch = KV_SCRATCH + scratch
    mixed, *low, logs = whole_call(
        forward_kernel, shapes, scratch, 10**10, place, *msgs, sib, fetched=range(5)
    )
    return mixed, low, logs


def attend_back(place, msgs, sib, mixed, logs, grads):
    pair = (4, 2 * HEAD_DIM, BLOCK)
    scratch = [
        pltpu.VMEM((4, HEAD_DIM, BLOCK), BF),
        pltpu.VMEM((8, BLOCK, HEAD_DIM), F32),
        pltpu.VMEM((8, BLOCK, HEAD_DIM), F32),
        pltpu.VMEM((HEAD_DIM, BLOCK), F32),
        pltpu.VMEM((4, MSG, BLOCK), BF),
        pltpu.VMEM(pair, BF),
        pltpu.VMEM((4, HEAD_DIM, BLOCK), F32),
        pltpu.VMEM((4, 1, BLOCK), F32),
        pltpu.SemaphoreType.DMA((7,)),
    ]
    shapes = (((4, HEAD_DIM, BLOCK), BF), (pair, F32), (pair, BF))
    arrays = (*msgs, sib, mixed, logs, *grads)
    scratch = KV_SCRATCH + scratch
    return whole_call(
        backward_kernel, shapes, scratch, 2 * 10**10, place, *arrays, fetched=range(7)
    )


def split_cores(place, mine, away, at, width, result):
    rows = result.reshape(16, 2, 32, width)
    even, odd = rows[:, 0].reshape(512, width), rows[:, 1].reshape(512, width)
    mine[:, at : at + width] = jnp.where(place[1] == 0, even, odd).astype(BF)
    away[:, at : at + width] = jnp.where(place[1] == 0, odd, even).astype(BF)


def weights_kernel(place, *refs):
    normed, grad_pre, grad, active, (out, turned) = (*[refs[i : i + 4] for i in (0, 4, 8, 12)], refs[16:])
    step = pl.program_id(0)
    at = pl.ds(pl.multiple_of((step & 3) * 256, 256), 256)

    def turn(chunks):
        for d, a in enumerate(chunks):
            turned[:, 128 * d : 128 * (d + 1)] = a[...].T

    def columns(chunks):
        return dot(turned[...], jnp.concatenate([a[:, at] for a in chunks], axis=0), 1, 0)

    @pl.when(step == 0)
    def _():
        turn(normed)

    @pl.when(step == 4)
    def _():
        turn(grad)

    @pl.when(step < 4)
    def _():
        out[...] = columns(grad_pre).astype(BF)

    @pl.when(step >= 4)
    def _():
        out[...] = columns(active).astype(BF)


def weight_grads(place, normed, grad_pre, grad, active):
    chunk = pl.BlockSpec((128, 1024), lambda i: (0, 0))
    return pl.pallas_call(
        weights_kernel,
        grid=(8,),
        out_shape=jax.ShapeDtypeStruct((1024, 2048), BF),
        in_specs=[pl.BlockSpec(memory_space=pltpu.SMEM)] + [chunk] * 16,
        out_specs=pl.BlockSpec((1024, 256), lambda i: (0, i)),
        scratch_shapes=[pltpu.VMEM((1024, 512), BF)],
        compiler_params=PARAMS,
        cost_estimate=pl.CostEstimate(flops=4 * 2**30, bytes_accessed=8 * 2**20, transcendentals=0),
    )(place, *normed, *grad_pre, *grad, *active)


def down_kernel(place, g0, g1, g2, g3, down, o0, o1, o2, o3, *, side):
    for g, o in zip((g0, g1, g2, g3), (o0, o1, o2, o3)):
        o[...] = dot(g[...], down[...], 1, side).astype(o.dtype)


def with_down(place, chunks, ff_all, side, kinds):
    chunk = pl.BlockSpec((128, 1024), lambda i: (0, 0))
    return pl.pallas_call(
        functools.partial(down_kernel, side=side),
        grid=(1,),
        out_shape=[jax.ShapeDtypeStruct((128, 1024), kind) for kind in kinds],
        in_specs=[pl.BlockSpec(memory_space=pltpu.SMEM)]
        + [chunk] * 4
        + [pl.BlockSpec((1024, 1024), lambda i: (0, 1))],
        out_specs=[chunk] * 4,
        compiler_params=FETCHING,
        cost_estimate=pl.CostEstimate(flops=2**30, bytes_accessed=8 * 2**20, transcendentals=0),
    )(place, *chunks, ff_all)


def feed_kernel(place, *refs, n):
    normed, grad, (up, down, vectors), outs = refs[:n], refs[n : 2 * n], refs[2 * n : 2 * n + 3], refs[2 * n + 3 :]
    rows = jnp.concatenate([a[...] for a in normed], axis=0)
    upstream = jnp.concatenate([a[...] for a in grad], axis=0)
    value, slope = gelu_pair(dot(rows, up[...], 1, 0) + vectors[4:5])
    low = (dot(upstream, down[...], 1, 0) * slope).astype(BF)
    part = dot(low, up[...], 1, 1)
    value = value.astype(BF)
    for i in range(n):
        at = slice(128 * i, 128 * (i + 1))
        active, grad_pre, own = outs[3 * i : 3 * i + 3]
        active[...] = value[at]
        grad_pre[...] = low[at]
        own[...] = part[at].astype(own.dtype)
    outs[3 * n][...] = jnp.sum(low.astype(F32), axis=0, keepdims=True)


def feed_chunks(place, normed, grad, ff_all, vectors, kinds):
    n = len(normed)
    chunk = pl.BlockSpec((128, 1024), lambda i: (0, 0))
    shape = (128, 1024)
    outs = []
    for kind in kinds:
        outs += [jax.ShapeDtypeStruct(shape, k) for k in (BF, BF, kind)]
    *outs, columns = pl.pallas_call(
        functools.partial(feed_kernel, n=n),
        grid=(1,),
        out_shape=outs + [jax.ShapeDtypeStruct((1, 1024), F32)],
        in_specs=[pl.BlockSpec(memory_space=pltpu.SMEM)]
        + [chunk] * (2 * n)
        + [
            pl.BlockSpec((1024, 1024), lambda i: (0, 0)),
            pl.BlockSpec((1024, 1024), lambda i: (0, 1)),
            pl.BlockSpec((8, 1024), lambda i: (0, 0)),
        ],
        out_specs=[chunk] * (3 * n) + [pl.BlockSpec((1, 1024), lambda i: (0, 0))],
        compiler_params=PARAMS,
        cost_estimate=pl.CostEstimate(flops=n * 2**33, bytes_accessed=4 * 2**20, transcendentals=0),
    )(place, *normed, *grad, ff_all, ff_all, vectors)
    return [outs[3 * i : 3 * i + 3] for i in range(n)], columns


def vectors_kernel(place, block, out):
    rows = block[...].astype(F32).T
    out[...] = jnp.concatenate([rows[0:4] + rows[4:8], rows[8:9], rows[9:12]], axis=0)


def vector_rows(place, ff_all):
    return pl.pallas_call(
        vectors_kernel,
        grid=(1,),
        out_shape=jax.ShapeDtypeStruct((8, 1024), F32),
        in_specs=[
            pl.BlockSpec(memory_space=pltpu.SMEM),
            pl.BlockSpec((1024, 128), lambda i: (0, 24)),
        ],
        out_specs=pl.BlockSpec((8, 1024), lambda i: (0, 0)),
        compiler_params=PARAMS,
    )(place, ff_all)


def last_kernel(
    place, dq_far, own_far, away_far, normed, m0, m1, m2, m3, mixed_far, vectors_far,
    b0, b1, b2, b3, mine, away,
    dq, own, other, n_s, m_s, mixed, vectors, done,
):
    blocks = []
    for d in range(4):
        at = pl.multiple_of(lax.rem(place[0] - d + 4, 4) * BLOCK, BLOCK)
        blocks.append(normed.at[pl.ds(at, BLOCK), :])
    started = copies(
        (dq_far, own_far, away_far, *blocks, m0, m1, m2, m3, mixed_far, vectors_far),
        (dq, own, other, *[n_s.at[d] for d in range(4)], *[m_s.at[d] for d in range(4)], mixed, vectors),
        done,
    )
    for copy in started[:3]:
        copy.wait()
    dqkv = (b0, b1, b2, b3)
    weights = jnp.zeros((192, 1024), F32)
    for d in range(4):
        pair = (own[d] + other[d].astype(F32)).astype(BF)
        dqkv[d][...] = jnp.concatenate([dq[d], pair], axis=0)
        started[3 + d].wait()
        weights += dot(dqkv[d][...], n_s[d], 1, 0)
    for copy in started[7:]:
        copy.wait()
    outs = sum(dot(mixed[:, 128 * d : 128 * (d + 1)], m_s[d], 1, 0) for d in range(4))
    split_cores(place, mine, away, 0, 256, outs.T)
    padding = jnp.zeros((64, 1024), F32)
    split_cores(place, mine, away, 384, 256, jnp.concatenate([weights, padding], axis=0).T)
    ones = jnp.ones((8, BLOCK), BF)
    columns = sum(dot(ones, dqkv[d][...], 1, 1) for d in range(4))[0:1]
    pad = jnp.zeros((1, 64), F32)
    columns = [jnp.concatenate([pad, columns[:, 64 * i : 64 * (i + 1)]], axis=1) for i in range(3)]
    row = lax.broadcasted_iota(jnp.int32, (1024, 128), 0) & 31
    small = jnp.concatenate([vectors[...].T, jnp.zeros((1024, 120), F32)], axis=1)
    for i in range(3):
        small += jnp.where(row == i, columns[i], 0.0)
    split_cores(place, mine, away, 256, 128, small)


def last_grads(place, *arrays):
    scratch = [
        pltpu.VMEM((4, HEAD_DIM, BLOCK), BF),
        pltpu.VMEM((4, 2 * HEAD_DIM, BLOCK), F32),
        pltpu.VMEM((4, 2 * HEAD_DIM, BLOCK), BF),
        pltpu.VMEM((4, BLOCK, 1024), BF),
        pltpu.VMEM((4, 128, 1024), BF),
        pltpu.VMEM((256, BLOCK), BF),
        pltpu.VMEM((8, 1024), F32),
        pltpu.SemaphoreType.DMA((13,)),
    ]
    shapes = (((192, BLOCK), BF),) * 4 + (((512, 640), BF),) * 2
    *dqkv, mine, away = whole_call(
        last_kernel, shapes, scratch, 2**31, place, *arrays, fetched=range(10)
    )
    return dqkv, mine, away


def rows_kernel(place, b0, b1, b2, b3, far, p1, p2, p3, own, s1, s2, s3, heads, weights, done):
    sends = (s1, s2, s3)
    places = [pl.multiple_of(lax.rem(place[0] + d, 4) * 192, 64) for d in range(4)]
    started = copies(
        (far, b0, b1, b2, b3, p1, p2, p3),
        (weights, *[heads.at[pl.ds(at, 192), :] for at in places], *[s.at[pl.ds(0, 128), :] for s in sends]),
        done,
    )
    for copy in started[:5]:
        copy.wait()
    own[...] = dot(heads[:, :128].T, weights[:, :768], 1, 1)
    for d, out in enumerate(sends, 1):
        rows = heads[:, 128 * d : 128 * (d + 1)].T
        out[128:, :] = dot(rows, weights[:, :768], 1, 1).astype(BF)
    for copy in started[5:]:
        copy.wait()


def row_grads(place, *arrays):
    shapes = (((128, 1024), F32),) + (((256, 1024), BF),) * 3
    scratch = [
        pltpu.VMEM((768, BLOCK), BF),
        pltpu.VMEM((1024, 896), BF),
        pltpu.SemaphoreType.DMA((8,)),
    ]
    return whole_call(rows_kernel, shapes, scratch, 2**30, place, *arrays, fetched=range(8))


def project_kernel(place, mine, theirs, rows, first, whole, m0, m1, m2, m3, qkv):
    y, c = place[0], place[1]
    for i in range(16):
        at = slice(32 * i, 32 * (i + 1))
        whole[pl.ds(pl.multiple_of(64 * i + 32 * c, 32), 32), :] = mine[at]
        whole[pl.ds(pl.multiple_of(64 * i + 32 - 32 * c, 32), 32), :] = theirs[at]
    bias = jnp.sum(whole[:, 768:].astype(F32).reshape(32, 32, 128), axis=0)
    bias = jnp.concatenate([bias[:6] + bias[6:12], jnp.zeros((2, 128), F32)], axis=0).T
    bias = jnp.concatenate([bias[:, i : i + 1] for i in range(6)], axis=0)
    qkv[...] = (dot(whole[:, :768].T, rows[...], 1, 1) + bias).astype(BF)
    for d, m in enumerate((m0, m1, m2, m3)):
        at = pl.multiple_of(lax.rem(y + d, 4) * 192, 64)
        m[0:192, :] = qkv[pl.ds(at, 192), :]
        m[192:208, :] = first[...]


def project(place, *arrays):
    shapes = (((1024, 896), BF),) + (((MSG, BLOCK), BF),) * 4
    scratch = [pltpu.VMEM((768, BLOCK), BF)]
    whole, *msgs = whole_call(project_kernel, shapes, scratch, 2**30, place, *arrays)
    return whole, msgs


def finish_kernel(
    place, g0, g1, g2, g3, w_qkv, own, ff, qkv, w_out, columns, vectors, up, down, m_s, k_s
):
    got = (g0, g1, g2, g3)
    up[...] = ff[:, :1024].astype(F32)
    down[...] = ff[:, 1024:].astype(F32)
    w_out[...] = total([g[:, :256] for g in got])
    rest = total([g[:, 256:384] for g in got])
    for d, g in enumerate(got):
        head = lax.rem(place[0] - d + 4, 4)
        m_s[head] = g[:, 384:576].astype(F32)
        k_s[head] = g[0:16, 256:384].astype(F32)
    gain, shift = own[:, 0:1], own[:, 2:3]
    gain_sum, shift_sum = jnp.zeros((32, 64), F32), jnp.zeros((32, 64), F32)
    for h in range(4):
        for i in range(3):
            at = slice(64 * h, 64 * (h + 1))
            m, k = m_s[h, :, 64 * i : 64 * (i + 1)], k_s[h, i : i + 1, 64:128]
            w = w_qkv[i, :, at].astype(F32)
            qkv[i, :, at] = gain * m + shift * k
            columns[i : i + 1, at] = k
            gain_sum += w * m
            shift_sum += w * k
    gain_sum = jnp.sum(gain_sum, axis=1, keepdims=True)
    shift_sum = jnp.sum(shift_sum, axis=1, keepdims=True)
    rows = jnp.concatenate(
        [gain_sum, rest[:, 0:1], shift_sum, rest[:, 1:5], jnp.zeros((32, 121), F32)], axis=1
    )
    vectors[...] = rows.T[:8]


def finish(place, *arrays):
    shapes = ((3, 32, 256), (32, 256), (3, 256), (8, 32), (32, 1024), (32, 1024))
    scratch = [pltpu.VMEM((4, 32, 192), F32), pltpu.VMEM((4, 16, 128), F32)]
    return whole_call(
        finish_kernel, [(shape, F32) for shape in shapes], scratch, 2**28, place, *arrays
    )


def middle_kernel(place, x0, x1, x2, x3, out, tokens, vectors, middle, normed):
    mixed = jnp.concatenate([x[...].T for x in (x0, x1, x2, x3)], axis=1)
    rows = tokens[...].astype(F32) + dot(mixed, out[...], 1, 1) + vectors[2:3]
    middle[...] = rows
    normed[...] = (normalized(rows)[0] * vectors[0:1] + vectors[1:2]).astype(BF)


def middle_back_kernel(
    place, part, a1, a2, a3, out, middle, grad, vectors, grad_middle, low, h0, h1, h2, h3, sums
):
    grad_two = part[...] + a1[...].astype(F32) + a2[...].astype(F32) + a3[...].astype(F32)
    normed, scale = normalized(middle[...])
    upstream = grad[...].astype(F32)
    rows = upstream + norm_back(grad_two, normed, scale, vectors[0:1])
    rows_low = rows.astype(BF)
    grad_middle[...] = rows
    low[...] = rows_low
    heads = dot(rows_low, out[...], 1, 0).T.astype(BF)
    for d, h in enumerate((h0, h1, h2, h3)):
        h[...] = heads[256 * d : 256 * (d + 1)]
    terms = (grad_two * normed, grad_two, rows, upstream)
    sums[...] = jnp.concatenate([jnp.sum(a, axis=0, keepdims=True) for a in terms], axis=0)


def tokens_kernel(
    place, part, a1, a2, a3, tokens, grad_middle, middle, second, vectors, grad_tokens, output
):
    terms = a1[...].astype(F32) + a2[...].astype(F32) + a3[...].astype(F32)
    normed, scale = normalized(tokens[...].astype(F32))
    grad = part[...] + terms[128:]
    grad_tokens[...] = grad_middle[...] + norm_back(grad, normed, scale, 1.0)
    output[...] = middle[...] + second[...] + terms[:128] + vectors[3:4]


def with_out(kernel, shapes, before, ff_all, after, place):
    def whole(a):
        return pl.BlockSpec(a.shape, lambda i, rank=len(a.shape): (0,) * rank)

    outs = [jax.ShapeDtypeStruct(*shape) for shape in shapes]
    return pl.pallas_call(
        kernel,
        grid=(1,),
        out_shape=outs,
        in_specs=[pl.BlockSpec(memory_space=pltpu.SMEM)]
        + [whole(a) for a in before]
        + [pl.BlockSpec((1024, 1024), lambda i: (0, 2))]
        + [whole(a) for a in after],
        out_specs=[whole(a) for a in outs],
        compiler_params=PARAMS,
        cost_estimate=pl.CostEstimate(flops=2**29, bytes_accessed=4 * 2**20, transcendentals=0),
    )(place, *before, ff_all, *after)


def gelu_pair(v):
    root = 0.7978845608028654
    square = v * v
    t = jnp.tanh(root * v * (1.0 + 0.044715 * square))
    half = 0.5 * (1.0 + t)
    slope = half + 0.5 * v * (1.0 - t * t) * (root * (1.0 + 3 * 0.044715 * square))
    return v * half, slope


def local(
    tokens, doc_start, norm_gains, norm_biases, out_biases, w_qkv, b_qv, w_out, w_up, b_up,
    w_down, out_grad,
):
    f = lax.axis_index("fsdp")
    x, y, c = f // 8, (f // 2) % 4, f % 2
    t = lax.axis_index("tp")
    place = jnp.stack([y, c, t]).astype(jnp.int32)

    vectors = jnp.concatenate([norm_gains, norm_biases, out_biases], axis=0).reshape(1, 48)
    vectors = jnp.concatenate(halves(vectors), axis=1)
    packed = jnp.concatenate([w_out.T, jnp.pad(vectors, ((0, 15), (0, 160)))], axis=0)
    qkv_local = w_qkv.reshape(3, 32, 4, 64).transpose(1, 2, 0, 3).reshape(32, 768)
    packed = from_all(packed, along_z)
    out_columns = [p[:32] for p in packed]
    own_vectors = in_order([p[32:33, :96].astype(F32) for p in packed], t)
    own_vectors = (own_vectors[:, :48] + own_vectors[:, 48:]).reshape(4, 6, 8)
    own_vectors = own_vectors.transpose(0, 2, 1).reshape(32, 6)
    gain, shift = own_vectors[:, 0:1], own_vectors[:, 2:3]

    weights = qkv_local.astype(F32)
    bias = jnp.sum(shift * weights, axis=0).reshape(4, 3, 64)
    qv_bias = jnp.stack([b_qv[0], jnp.zeros_like(b_qv[0]), b_qv[1]], axis=1).astype(F32)
    here = (jnp.arange(4)[:, None] == f // 8) & (jnp.arange(64)[None] // 8 == f % 8)
    bias = bias + jnp.where(here[:, None], jnp.tile(qv_bias, (1, 1, 8)), 0.0)
    bias = jnp.concatenate(halves(bias.reshape(6, 128)), axis=0)
    bias = jnp.pad(bias, ((0, 20), (0, 0)))
    by_y = from_all(jnp.concatenate([(gain * weights).astype(BF), bias], axis=1), along_y)
    by_x = from_all(placed_in_order(by_y, y), along_x)

    others = jnp.stack([own_vectors[:, i] for i in (1, 3, 4, 5)], axis=1)
    others = jnp.concatenate([*halves(others), b_up.reshape(32, 1), jnp.zeros((32, 119), BF)], axis=1)
    ff_local = jnp.concatenate([w_up, w_down.T, *out_columns, others], axis=1)
    ff_all = lax.all_gather(ff_local, "fsdp", axis=0, tiled=True)
    out_all = ff_all[:, 2048:3072]

    rows = from_all(tokens, along_z)
    rows, out_grad = lax.optimization_barrier((rows, out_grad))
    full_grad = from_all(out_grad, along_z)
    rows = jnp.concatenate(rows, axis=0)
    n_one, scale_one = normalized(rows.astype(F32))
    n_one_low = n_one.astype(BF)

    first = (doc_start - x * 4096).reshape(4, 128)
    first = jnp.concatenate(
        [lax.dynamic_slice_in_dim(first, (t - d) % 4, 1, axis=0) for d in range(4)], axis=0
    ).reshape(1, BLOCK)
    first = jnp.concatenate([first // 64, first % 64, jnp.zeros((14, BLOCK), jnp.int32)], axis=0)
    first = first.astype(BF)

    by_x = placed_in_order(by_x, x)
    attn_all, msgs = project(place, by_x, other_core(by_x), n_one_low, first)
    msgs = [msgs[0]] + [along_y(msgs[d], d) for d in (1, 2, 3)]
    msgs, full_grad = lax.optimization_barrier((msgs, full_grad))
    sib = other_core(jnp.stack([m[64:192] for m in msgs]))
    mixed, mixed_low, logs = attend(place, msgs, sib)
    vectors = vector_rows(place, ff_all)
    vector_rows_all = vectors

    back = [mixed_low[0]] + [along_y(mixed_low[d], -d) for d in (1, 2, 3)]
    back, vectors = lax.optimization_barrier((back, vectors))
    mixed_own = in_order([back[0], back[3], back[2], back[1]], y)
    by_z = [mixed_own[:, 128 * d : 128 * (d + 1)] for d in range(4)]
    by_z = [by_z[0]] + [along_z(by_z[d], -d) for d in (1, 2, 3)]
    by_z, n_one_low, mixed_own = lax.optimization_barrier((by_z, n_one_low, mixed_own))
    alike = [[(x * 4 + y) * 2 + c for y in range(4)] for x in range(4) for c in range(2)]
    n_all = lax.all_gather(n_one_low, "fsdp", axis=0, tiled=True, axis_index_groups=alike)

    row = (128, 1024)
    before = (by_z[0], by_z[3], by_z[2], by_z[1])
    middle, normed_two = with_out(
        middle_kernel, ((row, F32), (row, BF)), before, ff_all, (tokens, vectors), place
    )
    near_one, near_three = along_z(normed_two, 1), along_z(normed_two, 3)
    far = jnp.concatenate([along_z(near_one[:64], 1), along_z(near_three[64:], 3)], axis=0)
    full_two = [normed_two, near_one, far, near_three]
    near = [0, 1, 3]
    fed, grad_bup = feed_chunks(
        place, [full_two[d] for d in near], [full_grad[d] for d in near], ff_all, vectors, [F32, BF, BF]
    )
    far, fed, grad_bup = lax.optimization_barrier((full_two[2], fed, grad_bup))
    last, more_bup = feed_chunks(place, [far], [full_grad[2]], ff_all, vectors, [BF])
    active, grad_pre, part = zip(fed[0], fed[1], last[0], fed[2])
    arrived = [along_z(part[d], -d) for d in (1, 2, 3)]
    ff_grads = weight_grads(place, full_two, grad_pre, full_grad, active)
    arrived, ff_grads, active = lax.optimization_barrier((arrived, ff_grads, active))
    mlp_part = with_down(place, active, ff_all, 1, [F32, BF, BF, BF])
    grad_bup = grad_bup + more_bup
    ff_grads = lax.psum_scatter(ff_grads, "fsdp", scatter_dimension=0, tiled=True)

    heads = ((256, 128), BF)
    grad_middle, middle_low, *grad_mixed, sums = with_out(
        middle_back_kernel,
        ((row, F32), (row, BF), heads, heads, heads, heads, ((4, 1024), F32)),
        (part[0], *arrived),
        ff_all,
        (middle, out_grad, vectors),
        place,
    )
    by_z = [grad_mixed[0]] + [along_z(grad_mixed[d], -d) for d in (1, 2, 3)]
    by_z, middle_low, mlp_part = lax.optimization_barrier((by_z, middle_low, mlp_part))
    full_middle = from_all(middle_low, along_z)
    grad_heads = jnp.concatenate([by_z[0], by_z[3], by_z[2], by_z[1]], axis=1)
    grads = [piece(grad_heads, y, 64)] + [
        along_y(piece(grad_heads, (y + d) % 4, 64), d) for d in (1, 2, 3)
    ]
    dq, own, away = attend_back(place, msgs, sib, mixed, logs, grads)
    dq, own, away, full_middle = lax.optimization_barrier((dq, own, away, full_middle))
    away = other_core(away)
    sums = jnp.concatenate([sums, grad_bup, jnp.zeros((3, 1024), F32)], axis=0)
    dqkv, mine, away = last_grads(place, dq, own, away, n_all, *full_middle, mixed_own, sums)
    away = other_core(away)
    back = [dqkv[0]] + [along_y(dqkv[d], -d) for d in (1, 2, 3)]
    back, mine, away = lax.optimization_barrier((back, mine, away))
    got = scattered(added(mine, away), along_x, x, 128)
    part, *sent = row_grads(place, *back, attn_all, *mlp_part[1:])
    grad_one = [along_z(sent[d - 1], -d) for d in (1, 2, 3)]
    got, grad_one[0], grad_one[2] = lax.optimization_barrier((got, grad_one[0], grad_one[2]))
    got = scattered(total(got).astype(BF), along_y, y, 32)
    got, grad_one = lax.optimization_barrier((got, grad_one))
    out_qkv, out_wout, columns, vectors, out_wup, out_wdown = finish(
        place, got[0], got[2], got[1], got[3], w_qkv, own_vectors, ff_grads
    )
    arrays = (part, *grad_one, tokens, grad_middle, middle, mlp_part[0], vector_rows_all)
    grad_tokens, output = whole_call(
        tokens_kernel, ((row, F32),) * 2, [], 2**28, place, *arrays
    )
    out_wdown, out_wout = out_wdown.T, out_wout.T
    out_bup = vectors[6:7]
    columns = jnp.concatenate([columns[0:1], columns[2:3]], axis=0).reshape(2, 32, 8)
    out_bqv = lax.dynamic_slice_in_dim(columns, f, 1, axis=1)
    pieces = [lax.dynamic_slice_in_dim(vectors, (t + d) % 4 * 8, 8, axis=1) for d in range(4)]
    vectors = pieces[0] + sum(along_z(pieces[d], d) for d in (1, 2, 3))
    return (
        output,
        grad_tokens,
        vectors[0:2],
        vectors[2:4],
        vectors[4:6],
        out_qkv,
        out_bqv,
        out_wout,
        out_wup,
        out_bup,
        out_wdown,
    )


def solution(mesh):
    by_rows = P(("fsdp", "tp"), None)
    by_features = P(None, ("fsdp", "tp"))
    weights = (
        P(None, "fsdp", "tp"),
        P(None, "tp", "fsdp"),
        P("tp", "fsdp"),
        P("fsdp", "tp"),
        P("tp", "fsdp"),
        P("tp", "fsdp"),
    )
    return jax.shard_map(
        local,
        mesh=mesh,
        in_specs=(by_rows, P("fsdp"), by_features, by_features, by_features, *weights, by_rows),
        out_specs=(by_rows, by_rows, by_features, by_features, by_features, *weights),
        check_vma=False,
    )
```

```python
import functools

import jax
import jax.numpy as jnp
from jax import lax
from jax.experimental import pallas as pl
from jax.experimental.pallas import tpu as pltpu
from jax.sharding import PartitionSpec as P

HEAD_DIM = 64
BLOCK = 512
MSG = 208
EPSILON = 1e-05
MASKED = -1e30
BF = jnp.bfloat16
F32 = jnp.float32


def along_y(a, d):
    pairs = [
        ((x * 4 + y) * 2 + c, (x * 4 + (y + d) % 4) * 2 + c)
        for x in range(4)
        for y in range(4)
        for c in range(2)
    ]
    return lax.ppermute(a, "fsdp", pairs)


def along_x(a, d):
    pairs = [
        ((x * 4 + y) * 2 + c, (((x + d) % 4) * 4 + y) * 2 + c)
        for x in range(4)
        for y in range(4)
        for c in range(2)
    ]
    return lax.ppermute(a, "fsdp", pairs)


def other_core(a):
    return lax.ppermute(a, "fsdp", [(i, i ^ 1) for i in range(32)])


def along_z(a, d):
    return lax.ppermute(a, "tp", [(i, (i + d) % 4) for i in range(4)])


def from_all(a, move):
    return [a, move(a, 1), move(a, 2), move(a, 3)]


def in_order(rel, me):
    n = rel[0].shape[0]
    turned = [rel[0], rel[3], rel[2], rel[1]]
    twice = jnp.concatenate(turned + turned[:3], axis=0)
    return lax.dynamic_slice_in_dim(twice, ((4 - me) % 4) * n, 4 * n, axis=0)


def placed_in_order(rel, me):
    n = rel[0].shape[0]
    out = jnp.zeros((4 * n, *rel[0].shape[1:]), rel[0].dtype)
    for d, a in enumerate(rel):
        out = lax.dynamic_update_slice_in_dim(out, a, ((me - d) % 4) * n, axis=0)
    return out


def piece(a, at, n):
    return lax.dynamic_slice_in_dim(a, at * n, n, axis=0)


def added(mine, theirs):
    return (mine.astype(F32) + theirs.astype(F32)).astype(BF)


def scattered(a, move, me, n):
    return [piece(a, me, n)] + [move(piece(a, (me + d) % 4, n), d) for d in (2, 1, 3)]


def total(terms):
    return sum(a.astype(F32) for a in terms)


def halves(v):
    high = lax.reduce_precision(v, 8, 7)
    return high.astype(BF), (v - high).astype(BF)


def normalized(values):
    centred = values - jnp.mean(values, axis=-1, keepdims=True)
    spread = jnp.mean(centred * centred, axis=-1, keepdims=True)
    scale = lax.rsqrt(spread + EPSILON)
    return centred * scale, scale


def norm_back(grad, normed, scale, gain):
    e = grad * gain
    return scale * (
        e
        - jnp.mean(e, axis=-1, keepdims=True)
        - normed * jnp.mean(e * normed, axis=-1, keepdims=True)
    )


def dot(a, b, ca, cb):
    return lax.dot_general(a, b, (((ca,), (cb,)), ((), ())), preferred_element_type=F32)


def unpack(place, msgs, sib, q_s, kt_s, vt_s, start_s, k_s, v_s):
    y, c = place[0], place[1]
    for d in range(4):
        block = lax.rem(y - d + 4, 4) * 2
        msg = msgs[d]
        q_s[d] = msg[0:64, :] * BF(0.125)
        first = msg[192:208, :].astype(F32)
        start_s[d] = first[0:1] * 64.0 + first[1:2]
        k, v = msg[64:128, :], msg[128:192, :]
        kt_s[block + c] = k.T
        vt_s[block + c] = v.T
        k_s[block + c] = k
        v_s[block + c] = v
        k, v = sib[d, 0:64, :], sib[d, 64:128, :]
        kt_s[block + 1 - c] = k.T
        vt_s[block + 1 - c] = v.T
        k_s[block + 1 - c] = k
        v_s[block + 1 - c] = v


def positions(place, axis):
    shape = (BLOCK, 1) if axis == 0 else (1, BLOCK)
    at = lax.broadcasted_iota(jnp.int32, shape, axis)
    chunk = (place[2] - (at >> 7)) & 3
    return ((chunk << 7) + (at & 127)).astype(F32)


def allowed_in(place, start, key_block, mode):
    if mode == 0:
        return None
    key_pos = positions(place, 0)
    allowed = key_pos >= start - (key_block * BLOCK).astype(F32)
    if mode == 2:
        allowed = allowed & (key_pos <= positions(place, 1))
    return allowed


def over_keys(start, block, step):
    low = jnp.min(start).astype(jnp.int32) // BLOCK
    last = jnp.max(start).astype(jnp.int32)

    def body(key_block, carry):
        @pl.when(key_block * BLOCK < last)
        def _():
            step(key_block, 1)

        @pl.when(key_block * BLOCK >= last)
        def _():
            step(key_block, 0)

        return carry

    lax.fori_loop(low, block, body, 0)
    step(block, 2)


def copies(sources, targets, done):
    started = [
        pltpu.make_async_copy(source, target, done.at[i])
        for i, (source, target) in enumerate(zip(sources, targets))
    ]
    for copy in started:
        copy.start()
    return started


def forward_kernel(
    place, m0, m1, m2, m3, sib_far, mixed, l0, l1, l2, l3, logs,
    q_s, kt_s, vt_s, start_s, k_s, v_s, peak_s, total_s, acc_s, msgs, sib, done,
):
    near = [msgs.at[d] for d in range(4)]
    for copy in copies((m0, m1, m2, m3, sib_far), (*near, sib), done):
        copy.wait()
    unpack(place, near, sib, q_s, kt_s, vt_s, start_s, k_s, v_s)

    def queries(d, carry):
        block = lax.rem(place[0] - d + 4, 4) * 2 + place[1]
        start = start_s[d]
        peak_s[...] = jnp.full((1, BLOCK), MASKED, F32)
        total_s[...] = jnp.zeros((1, BLOCK), F32)
        acc_s[...] = jnp.zeros((HEAD_DIM, BLOCK), F32)

        def step(key_block, mode):
            allowed = allowed_in(place, start, key_block, mode)
            halves_at = [slice(0, 256), slice(256, 512)]
            scores = [dot(kt_s[key_block], q_s[d, :, at], 1, 0) for at in halves_at]
            if allowed is not None:
                scores = [
                    jnp.where(allowed[:, at], s, MASKED) for at, s in zip(halves_at, scores)
                ]
            for at, s in zip(halves_at, scores):
                old = peak_s[:, at]
                peak = jnp.maximum(old, jnp.max(s, axis=0, keepdims=True))
                p = jnp.exp(s - peak)
                shrink = jnp.exp(old - peak)
                peak_s[:, at] = peak
                total_s[:, at] = total_s[:, at] * shrink + jnp.sum(p, axis=0, keepdims=True)
                acc_s[:, at] = acc_s[:, at] * shrink + dot(v_s[key_block], p.astype(BF), 1, 0)

        over_keys(start, block, step)
        out = acc_s[...] / total_s[...]
        mixed[d] = out
        logs[d] = peak_s[...] + jnp.log(total_s[...])
        return carry

    lax.fori_loop(0, 4, queries, 0)
    for d, low in enumerate((l0, l1, l2, l3)):
        low[...] = mixed[d].astype(BF)


def backward_kernel(
    place, m0, m1, m2, m3, sib_far, mixed_far, logs_far, g0, g1, g2, g3, dq, own, away,
    q_s, kt_s, vt_s, start_s, k_s, v_s, g_s, dk_s, dv_s, acc_s, msgs, sib, mixed, logs, done,
):
    started = copies(
        (m0, m1, m2, m3, sib_far, mixed_far, logs_far),
        (*[msgs.at[d] for d in range(4)], sib, mixed, logs),
        done,
    )
    for d, g in enumerate((g0, g1, g2, g3)):
        g_s[d] = g[...]
    dk_s[...] = jnp.zeros(dk_s.shape, F32)
    dv_s[...] = jnp.zeros(dv_s.shape, F32)
    for copy in started:
        copy.wait()
    unpack(place, [msgs.at[d] for d in range(4)], sib, q_s, kt_s, vt_s, start_s, k_s, v_s)

    def queries(d, carry):
        block = lax.rem(place[0] - d + 4, 4) * 2 + place[1]
        start = start_s[d]
        log = logs[d]
        grad = g_s[d]
        q = q_s[d]
        delta = jnp.sum(grad.astype(F32) * mixed[d], axis=0, keepdims=True)
        qt = q.T
        gt = grad.T
        acc_s[...] = jnp.zeros((HEAD_DIM, BLOCK), F32)

        def step(key_block, mode):
            allowed = allowed_in(place, start, key_block, mode)
            grads, probs = [], []
            for at in (slice(0, 256), slice(256, 512)):
                p = jnp.exp(dot(kt_s[key_block], q[:, at], 1, 0) - log[:, at])
                if allowed is not None:
                    p = jnp.where(allowed[:, at], p, 0.0)
                dp = dot(vt_s[key_block], grad[:, at], 1, 0)
                grads.append((p * (dp - delta[:, at])).astype(BF))
                probs.append(p.astype(BF))
            ds = jnp.concatenate(grads, axis=1)
            dv_s[key_block] += dot(jnp.concatenate(probs, axis=1), gt, 1, 0)
            dk_s[key_block] += dot(ds, qt, 1, 0)
            acc_s[...] += dot(k_s[key_block], ds, 1, 0)

        over_keys(start, block, step)
        dq[d] = (acc_s[...] * 0.125).astype(BF)
        return carry

    lax.fori_loop(0, 4, queries, 0)
    for d in range(4):
        block = lax.rem(place[0] - d + 4, 4) * 2
        own[d, 0:64, :] = dk_s[block + place[1]].T
        own[d, 64:128, :] = dv_s[block + place[1]].T
        away[d, 0:64, :] = dk_s[block + 1 - place[1]].T.astype(BF)
        away[d, 64:128, :] = dv_s[block + 1 - place[1]].T.astype(BF)


KV_SCRATCH = [
    pltpu.VMEM((4, HEAD_DIM, BLOCK), BF),
    pltpu.VMEM((8, BLOCK, HEAD_DIM), BF),
    pltpu.VMEM((8, BLOCK, HEAD_DIM), BF),
    pltpu.VMEM((4, 1, BLOCK), F32),
    pltpu.VMEM((8, HEAD_DIM, BLOCK), BF),
    pltpu.VMEM((8, HEAD_DIM, BLOCK), BF),
]
PARAMS = pltpu.CompilerParams(vmem_limit_bytes=48 * 1024 * 1024)
FETCHING = pltpu.CompilerParams(vmem_limit_bytes=60 * 1024 * 1024)


def whole_call(kernel, shapes, scratch, flops, place, *arrays, fetched=()):
    def whole(a):
        return pl.BlockSpec(a.shape, lambda i, rank=len(a.shape): (0,) * rank)

    outs = [jax.ShapeDtypeStruct(*shape) for shape in shapes]
    return pl.pallas_call(
        kernel,
        grid=(1,),
        out_shape=outs,
        in_specs=[pl.BlockSpec(memory_space=pltpu.SMEM)]
        + [
            pl.BlockSpec(memory_space=pl.ANY) if i in fetched else whole(a)
            for i, a in enumerate(arrays)
        ],
        out_specs=[whole(a) for a in outs],
        scratch_shapes=scratch,
        compiler_params=FETCHING if fetched else PARAMS,
        cost_estimate=pl.CostEstimate(flops=flops, bytes_accessed=8 * 2**20, transcendentals=0),
    )(place, *arrays)


def attend(place, msgs, sib):
    head = (4, HEAD_DIM, BLOCK)
    scratch = [
        pltpu.VMEM((1, BLOCK), F32),
        pltpu.VMEM((1, BLOCK), F32),
        pltpu.VMEM((HEAD_DIM, BLOCK), F32),
        pltpu.VMEM((4, MSG, BLOCK), BF),
        pltpu.VMEM((4, 2 * HEAD_DIM, BLOCK), BF),
        pltpu.SemaphoreType.DMA((5,)),
    ]
    shapes = ((head, F32), *[((HEAD_DIM, BLOCK), BF)] * 4, ((4, 1, BLOCK), F32))
    scratch = KV_SCRATCH + scratch
    mixed, *low, logs = whole_call(
        forward_kernel, shapes, scratch, 10**10, place, *msgs, sib, fetched=range(5)
    )
    return mixed, low, logs


def attend_back(place, msgs, sib, mixed, logs, grads):
    pair = (4, 2 * HEAD_DIM, BLOCK)
    scratch = [
        pltpu.VMEM((4, HEAD_DIM, BLOCK), BF),
        pltpu.VMEM((8, BLOCK, HEAD_DIM), F32),
        pltpu.VMEM((8, BLOCK, HEAD_DIM), F32),
        pltpu.VMEM((HEAD_DIM, BLOCK), F32),
        pltpu.VMEM((4, MSG, BLOCK), BF),
        pltpu.VMEM(pair, BF),
        pltpu.VMEM((4, HEAD_DIM, BLOCK), F32),
        pltpu.VMEM((4, 1, BLOCK), F32),
        pltpu.SemaphoreType.DMA((7,)),
    ]
    shapes = (((4, HEAD_DIM, BLOCK), BF), (pair, F32), (pair, BF))
    arrays = (*msgs, sib, mixed, logs, *grads)
    scratch = KV_SCRATCH + scratch
    return whole_call(
        backward_kernel, shapes, scratch, 2 * 10**10, place, *arrays, fetched=range(7)
    )


def split_cores(place, mine, away, at, width, result):
    rows = result.reshape(16, 2, 32, width)
    even, odd = rows[:, 0].reshape(512, width), rows[:, 1].reshape(512, width)
    mine[:, at : at + width] = jnp.where(place[1] == 0, even, odd).astype(BF)
    away[:, at : at + width] = jnp.where(place[1] == 0, odd, even).astype(BF)


def weights_kernel(place, *refs):
    normed, grad_pre, grad, active, (out, turned) = (*[refs[i : i + 4] for i in (0, 4, 8, 12)], refs[16:])
    step = pl.program_id(0)
    at = pl.ds(pl.multiple_of((step & 3) * 256, 256), 256)

    def turn(chunks):
        for d, a in enumerate(chunks):
            turned[:, 128 * d : 128 * (d + 1)] = a[...].T

    def columns(chunks):
        return dot(turned[...], jnp.concatenate([a[:, at] for a in chunks], axis=0), 1, 0)

    @pl.when(step == 0)
    def _():
        turn(normed)

    @pl.when(step == 4)
    def _():
        turn(grad)

    @pl.when(step < 4)
    def _():
        out[...] = columns(grad_pre).astype(BF)

    @pl.when(step >= 4)
    def _():
        out[...] = columns(active).astype(BF)


def weight_grads(place, normed, grad_pre, grad, active):
    chunk = pl.BlockSpec((128, 1024), lambda i: (0, 0))
    return pl.pallas_call(
        weights_kernel,
        grid=(8,),
        out_shape=jax.ShapeDtypeStruct((1024, 2048), BF),
        in_specs=[pl.BlockSpec(memory_space=pltpu.SMEM)] + [chunk] * 16,
        out_specs=pl.BlockSpec((1024, 256), lambda i: (0, i)),
        scratch_shapes=[pltpu.VMEM((1024, 512), BF)],
        compiler_params=PARAMS,
        cost_estimate=pl.CostEstimate(flops=4 * 2**30, bytes_accessed=8 * 2**20, transcendentals=0),
    )(place, *normed, *grad_pre, *grad, *active)


def down_kernel(place, a0, a1, a2, a3, down, low, own, after, far, before):
    own[...] = dot(a0[...], down[...], 1, 1)
    far[...] = dot(a2[...], down[...], 1, 1).astype(BF)
    for a, out in ((a3, after), (a1, before)):
        out[:128, :] = low[...]
        out[128:, :] = dot(a[...], down[...], 1, 1).astype(BF)


def with_down(place, chunks, ff_all, low):
    def rows(n):
        return pl.BlockSpec((n, 1024), lambda i: (0, 0))

    return pl.pallas_call(
        down_kernel,
        grid=(1,),
        out_shape=[
            jax.ShapeDtypeStruct((n, 1024), kind)
            for n, kind in ((128, F32), (256, BF), (128, BF), (256, BF))
        ],
        in_specs=[pl.BlockSpec(memory_space=pltpu.SMEM)]
        + [rows(128)] * 4
        + [pl.BlockSpec((1024, 1024), lambda i: (0, 1)), rows(128)],
        out_specs=[rows(128), rows(256), rows(128), rows(256)],
        compiler_params=FETCHING,
        cost_estimate=pl.CostEstimate(flops=2**30, bytes_accessed=8 * 2**20, transcendentals=0),
    )(place, *chunks, ff_all, low)


def feed_kernel(place, *refs, n):
    normed, grad, (up, down, vectors), outs = refs[:n], refs[n : 2 * n], refs[2 * n : 2 * n + 3], refs[2 * n + 3 :]
    rows = jnp.concatenate([a[...] for a in normed], axis=0)
    upstream = jnp.concatenate([a[...] for a in grad], axis=0)
    value, slope = gelu_pair(dot(rows, up[...], 1, 0) + vectors[4:5])
    low = (dot(upstream, down[...], 1, 0) * slope).astype(BF)
    part = dot(low, up[...], 1, 1)
    value = value.astype(BF)
    for i in range(n):
        at = slice(128 * i, 128 * (i + 1))
        active, grad_pre, own = outs[3 * i : 3 * i + 3]
        active[...] = value[at]
        grad_pre[...] = low[at]
        own[...] = part[at].astype(own.dtype)
    outs[3 * n][...] = jnp.sum(low.astype(F32), axis=0, keepdims=True)


def feed_chunks(place, normed, grad, ff_all, vectors, kinds):
    n = len(normed)
    chunk = pl.BlockSpec((128, 1024), lambda i: (0, 0))
    shape = (128, 1024)
    outs = []
    for kind in kinds:
        outs += [jax.ShapeDtypeStruct(shape, k) for k in (BF, BF, kind)]
    *outs, columns = pl.pallas_call(
        functools.partial(feed_kernel, n=n),
        grid=(1,),
        out_shape=outs + [jax.ShapeDtypeStruct((1, 1024), F32)],
        in_specs=[pl.BlockSpec(memory_space=pltpu.SMEM)]
        + [chunk] * (2 * n)
        + [
            pl.BlockSpec((1024, 1024), lambda i: (0, 0)),
            pl.BlockSpec((1024, 1024), lambda i: (0, 1)),
            pl.BlockSpec((8, 1024), lambda i: (0, 0)),
        ],
        out_specs=[chunk] * (3 * n) + [pl.BlockSpec((1, 1024), lambda i: (0, 0))],
        compiler_params=PARAMS,
        cost_estimate=pl.CostEstimate(flops=n * 2**33, bytes_accessed=4 * 2**20, transcendentals=0),
    )(place, *normed, *grad, ff_all, ff_all, vectors)
    return [outs[3 * i : 3 * i + 3] for i in range(n)], columns


def vectors_kernel(place, block, out):
    rows = block[...].astype(F32).T
    out[...] = jnp.concatenate([rows[0:4] + rows[4:8], rows[8:9], rows[9:12]], axis=0)


def vector_rows(place, ff_all):
    return pl.pallas_call(
        vectors_kernel,
        grid=(1,),
        out_shape=jax.ShapeDtypeStruct((8, 1024), F32),
        in_specs=[
            pl.BlockSpec(memory_space=pltpu.SMEM),
            pl.BlockSpec((1024, 128), lambda i: (0, 24)),
        ],
        out_specs=pl.BlockSpec((8, 1024), lambda i: (0, 0)),
        compiler_params=PARAMS,
    )(place, ff_all)


def last_kernel(
    place, dq_far, own_far, away_far, normed, m0, m1, m2, m3, mixed_far, vectors_far,
    b0, b1, b2, b3, mine, away,
    dq, own, other, n_s, m_s, mixed, vectors, done,
):
    blocks = []
    for d in range(4):
        at = pl.multiple_of(lax.rem(place[0] - d + 4, 4) * BLOCK, BLOCK)
        blocks.append(normed.at[pl.ds(at, BLOCK), :])
    started = copies(
        (
            *(dq_far, own_far, away_far, *blocks, m0, m1.at[pl.ds(0, 128), :], m2),
            *(m3.at[pl.ds(0, 128), :], mixed_far, vectors_far),
        ),
        (dq, own, other, *[n_s.at[d] for d in range(4)], *[m_s.at[d] for d in range(4)], mixed, vectors),
        done,
    )
    for copy in started[:3]:
        copy.wait()
    dqkv = (b0, b1, b2, b3)
    weights = jnp.zeros((192, 1024), F32)
    for d in range(4):
        pair = (own[d] + other[d].astype(F32)).astype(BF)
        dqkv[d][...] = jnp.concatenate([dq[d], pair], axis=0)
        started[3 + d].wait()
        weights += dot(dqkv[d][...], n_s[d], 1, 0)
    for copy in started[7:]:
        copy.wait()
    outs = sum(dot(mixed[:, 128 * d : 128 * (d + 1)], m_s[d], 1, 0) for d in range(4))
    split_cores(place, mine, away, 0, 256, outs.T)
    padding = jnp.zeros((64, 1024), F32)
    split_cores(place, mine, away, 384, 256, jnp.concatenate([weights, padding], axis=0).T)
    ones = jnp.ones((8, BLOCK), BF)
    columns = sum(dot(ones, dqkv[d][...], 1, 1) for d in range(4))[0:1]
    pad = jnp.zeros((1, 64), F32)
    columns = [jnp.concatenate([pad, columns[:, 64 * i : 64 * (i + 1)]], axis=1) for i in range(3)]
    row = lax.broadcasted_iota(jnp.int32, (1024, 128), 0) & 31
    small = jnp.concatenate([vectors[...].T, jnp.zeros((1024, 120), F32)], axis=1)
    for i in range(3):
        small += jnp.where(row == i, columns[i], 0.0)
    split_cores(place, mine, away, 256, 128, small)


def last_grads(place, *arrays):
    scratch = [
        pltpu.VMEM((4, HEAD_DIM, BLOCK), BF),
        pltpu.VMEM((4, 2 * HEAD_DIM, BLOCK), F32),
        pltpu.VMEM((4, 2 * HEAD_DIM, BLOCK), BF),
        pltpu.VMEM((4, BLOCK, 1024), BF),
        pltpu.VMEM((4, 128, 1024), BF),
        pltpu.VMEM((256, BLOCK), BF),
        pltpu.VMEM((8, 1024), F32),
        pltpu.SemaphoreType.DMA((13,)),
    ]
    shapes = (((192, BLOCK), BF),) * 4 + (((512, 640), BF),) * 2
    *dqkv, mine, away = whole_call(
        last_kernel, shapes, scratch, 2**31, place, *arrays, fetched=range(10)
    )
    return dqkv, mine, away


def rows_kernel(place, b0, b1, b2, b3, far, second, own, before, after, heads, weights, done):
    places = [pl.multiple_of(lax.rem(place[0] + d, 4) * 192, 64) for d in range(4)]
    started = copies(
        (far, b0, b1, b2, b3, second),
        (weights, *[heads.at[pl.ds(at, 192), :] for at in places], before.at[pl.ds(128, 128), :]),
        done,
    )
    for copy in started[:5]:
        copy.wait()
    own[...] = dot(heads[:, :128].T, weights[:, :768], 1, 1)
    for d, out, at in ((1, before, 0), (2, after, 128), (3, after, 0)):
        rows = heads[:, 128 * d : 128 * (d + 1)].T
        out[at : at + 128, :] = dot(rows, weights[:, :768], 1, 1).astype(BF)
    for copy in started[5:]:
        copy.wait()


def row_grads(place, *arrays):
    shapes = (((128, 1024), F32),) + (((256, 1024), BF),) * 2
    scratch = [
        pltpu.VMEM((768, BLOCK), BF),
        pltpu.VMEM((1024, 896), BF),
        pltpu.SemaphoreType.DMA((6,)),
    ]
    return whole_call(rows_kernel, shapes, scratch, 2**30, place, *arrays, fetched=range(6))


def project_kernel(place, mine, theirs, rows, first, whole, m0, m1, m2, m3, qkv):
    y, c = place[0], place[1]
    for i in range(16):
        at = slice(32 * i, 32 * (i + 1))
        whole[pl.ds(pl.multiple_of(64 * i + 32 * c, 32), 32), :] = mine[at]
        whole[pl.ds(pl.multiple_of(64 * i + 32 - 32 * c, 32), 32), :] = theirs[at]
    bias = jnp.sum(whole[:, 768:].astype(F32).reshape(32, 32, 128), axis=0)
    bias = jnp.concatenate([bias[:6] + bias[6:12], jnp.zeros((2, 128), F32)], axis=0).T
    bias = jnp.concatenate([bias[:, i : i + 1] for i in range(6)], axis=0)
    qkv[...] = (dot(whole[:, :768].T, rows[...], 1, 1) + bias).astype(BF)
    for d, m in enumerate((m0, m1, m2, m3)):
        at = pl.multiple_of(lax.rem(y + d, 4) * 192, 64)
        m[0:192, :] = qkv[pl.ds(at, 192), :]
        m[192:208, :] = first[...]


def project(place, *arrays):
    shapes = (((1024, 896), BF),) + (((MSG, BLOCK), BF),) * 4
    scratch = [pltpu.VMEM((768, BLOCK), BF)]
    whole, *msgs = whole_call(project_kernel, shapes, scratch, 2**30, place, *arrays)
    return whole, msgs


def finish_kernel(
    place, g0, g1, g2, g3, w_qkv, own, ff, qkv, w_out, columns, vectors, up, down, m_s, k_s
):
    got = (g0, g1, g2, g3)
    up[...] = ff[:, :1024].astype(F32)
    down[...] = ff[:, 1024:].astype(F32)
    w_out[...] = total([g[:, :256] for g in got])
    rest = total([g[:, 256:384] for g in got])
    for d, g in enumerate(got):
        head = lax.rem(place[0] - d + 4, 4)
        m_s[head] = g[:, 384:576].astype(F32)
        k_s[head] = g[0:16, 256:384].astype(F32)
    gain, shift = own[:, 0:1], own[:, 2:3]
    gain_sum, shift_sum = jnp.zeros((32, 64), F32), jnp.zeros((32, 64), F32)
    for h in range(4):
        for i in range(3):
            at = slice(64 * h, 64 * (h + 1))
            m, k = m_s[h, :, 64 * i : 64 * (i + 1)], k_s[h, i : i + 1, 64:128]
            w = w_qkv[i, :, at].astype(F32)
            qkv[i, :, at] = gain * m + shift * k
            columns[i : i + 1, at] = k
            gain_sum += w * m
            shift_sum += w * k
    gain_sum = jnp.sum(gain_sum, axis=1, keepdims=True)
    shift_sum = jnp.sum(shift_sum, axis=1, keepdims=True)
    rows = jnp.concatenate(
        [gain_sum, rest[:, 0:1], shift_sum, rest[:, 1:5], jnp.zeros((32, 121), F32)], axis=1
    )
    vectors[...] = rows.T[:8]


def finish(place, *arrays):
    shapes = ((3, 32, 256), (32, 256), (3, 256), (8, 32), (32, 1024), (32, 1024))
    scratch = [pltpu.VMEM((4, 32, 192), F32), pltpu.VMEM((4, 16, 128), F32)]
    return whole_call(
        finish_kernel, [(shape, F32) for shape in shapes], scratch, 2**28, place, *arrays
    )


def middle_kernel(place, x0, x1, x2, x3, out, tokens, vectors, middle, normed):
    mixed = jnp.concatenate([x[...].T for x in (x0, x1, x2, x3)], axis=1)
    rows = tokens[...].astype(F32) + dot(mixed, out[...], 1, 1) + vectors[2:3]
    middle[...] = rows
    normed[...] = (normalized(rows)[0] * vectors[0:1] + vectors[1:2]).astype(BF)


def middle_back_kernel(
    place, part, a1, a2, a3, out, middle, grad, vectors, grad_middle, low, h0, h1, h2, h3, sums
):
    grad_two = part[...] + a1[...].astype(F32) + a2[...].astype(F32) + a3[...].astype(F32)
    normed, scale = normalized(middle[...])
    upstream = grad[...].astype(F32)
    rows = upstream + norm_back(grad_two, normed, scale, vectors[0:1])
    rows_low = rows.astype(BF)
    grad_middle[...] = rows
    low[...] = rows_low
    heads = dot(rows_low, out[...], 1, 0).T.astype(BF)
    for d, h in enumerate((h0, h1, h2, h3)):
        h[...] = heads[256 * d : 256 * (d + 1)]
    terms = (grad_two * normed, grad_two, rows, upstream)
    sums[...] = jnp.concatenate([jnp.sum(a, axis=0, keepdims=True) for a in terms], axis=0)


def tokens_kernel(
    place, part, a1, a3, second_far, rows_far, tokens, grad_middle, middle, second, s1, s3, vectors,
    grad_tokens, output,
):
    near = a1[:128, :].astype(F32) + a3[:128, :].astype(F32)
    normed, scale = normalized(tokens[...].astype(F32))
    grad = part[...] + near + rows_far[...].astype(F32)
    grad_tokens[...] = grad_middle[...] + norm_back(grad, normed, scale, 1.0)
    near = s1[128:, :].astype(F32) + s3[128:, :].astype(F32)
    output[...] = middle[...] + second[...] + near + second_far[...].astype(F32) + vectors[3:4]


def with_out(kernel, shapes, before, ff_all, after, place):
    def whole(a):
        return pl.BlockSpec(a.shape, lambda i, rank=len(a.shape): (0,) * rank)

    outs = [jax.ShapeDtypeStruct(*shape) for shape in shapes]
    return pl.pallas_call(
        kernel,
        grid=(1,),
        out_shape=outs,
        in_specs=[pl.BlockSpec(memory_space=pltpu.SMEM)]
        + [whole(a) for a in before]
        + [pl.BlockSpec((1024, 1024), lambda i: (0, 2))]
        + [whole(a) for a in after],
        out_specs=[whole(a) for a in outs],
        compiler_params=PARAMS,
        cost_estimate=pl.CostEstimate(flops=2**29, bytes_accessed=4 * 2**20, transcendentals=0),
    )(place, *before, ff_all, *after)


def gelu_pair(v):
    root = 0.7978845608028654
    square = v * v
    t = jnp.tanh(root * v * (1.0 + 0.044715 * square))
    half = 0.5 * (1.0 + t)
    slope = half + 0.5 * v * (1.0 - t * t) * (root * (1.0 + 3 * 0.044715 * square))
    return v * half, slope


def local(
    tokens, doc_start, norm_gains, norm_biases, out_biases, w_qkv, b_qv, w_out, w_up, b_up,
    w_down, out_grad,
):
    f = lax.axis_index("fsdp")
    x, y, c = f // 8, (f // 2) % 4, f % 2
    t = lax.axis_index("tp")
    place = jnp.stack([y, c, t]).astype(jnp.int32)

    vectors = jnp.concatenate([norm_gains, norm_biases, out_biases], axis=0).reshape(1, 48)
    vectors = jnp.concatenate(halves(vectors), axis=1)
    packed = jnp.concatenate([w_out.T, jnp.pad(vectors, ((0, 15), (0, 160)))], axis=0)
    qkv_local = w_qkv.reshape(3, 32, 4, 64).transpose(1, 2, 0, 3).reshape(32, 768)
    packed = from_all(packed, along_z)
    out_columns = [p[:32] for p in packed]
    own_vectors = in_order([p[32:33, :96].astype(F32) for p in packed], t)
    own_vectors = (own_vectors[:, :48] + own_vectors[:, 48:]).reshape(4, 6, 8)
    own_vectors = own_vectors.transpose(0, 2, 1).reshape(32, 6)
    gain, shift = own_vectors[:, 0:1], own_vectors[:, 2:3]

    weights = qkv_local.astype(F32)
    bias = jnp.sum(shift * weights, axis=0).reshape(4, 3, 64)
    qv_bias = jnp.stack([b_qv[0], jnp.zeros_like(b_qv[0]), b_qv[1]], axis=1).astype(F32)
    here = (jnp.arange(4)[:, None] == f // 8) & (jnp.arange(64)[None] // 8 == f % 8)
    bias = bias + jnp.where(here[:, None], jnp.tile(qv_bias, (1, 1, 8)), 0.0)
    bias = jnp.concatenate(halves(bias.reshape(6, 128)), axis=0)
    bias = jnp.pad(bias, ((0, 20), (0, 0)))
    by_y = from_all(jnp.concatenate([(gain * weights).astype(BF), bias], axis=1), along_y)
    by_x = from_all(placed_in_order(by_y, y), along_x)

    others = jnp.stack([own_vectors[:, i] for i in (1, 3, 4, 5)], axis=1)
    others = jnp.concatenate([*halves(others), b_up.reshape(32, 1), jnp.zeros((32, 119), BF)], axis=1)
    ff_local = jnp.concatenate([w_up, w_down.T, *out_columns, others], axis=1)
    ff_all = lax.all_gather(ff_local, "fsdp", axis=0, tiled=True)
    out_all = ff_all[:, 2048:3072]

    rows = from_all(tokens, along_z)
    rows, out_grad = lax.optimization_barrier((rows, out_grad))
    full_grad = from_all(out_grad, along_z)
    rows = jnp.concatenate(rows, axis=0)
    n_one, scale_one = normalized(rows.astype(F32))
    n_one_low = n_one.astype(BF)

    first = (doc_start - x * 4096).reshape(4, 128)
    first = jnp.concatenate(
        [lax.dynamic_slice_in_dim(first, (t - d) % 4, 1, axis=0) for d in range(4)], axis=0
    ).reshape(1, BLOCK)
    first = jnp.concatenate([first // 64, first % 64, jnp.zeros((14, BLOCK), jnp.int32)], axis=0)
    first = first.astype(BF)

    by_x = placed_in_order(by_x, x)
    attn_all, msgs = project(place, by_x, other_core(by_x), n_one_low, first)
    msgs = [msgs[0]] + [along_y(msgs[d], d) for d in (1, 2, 3)]
    msgs, full_grad = lax.optimization_barrier((msgs, full_grad))
    sib = other_core(jnp.stack([m[64:192] for m in msgs]))
    mixed, mixed_low, logs = attend(place, msgs, sib)
    vectors = vector_rows(place, ff_all)
    vector_rows_all = vectors

    back = [mixed_low[0]] + [along_y(mixed_low[d], -d) for d in (1, 2, 3)]
    back, vectors = lax.optimization_barrier((back, vectors))
    mixed_own = in_order([back[0], back[3], back[2], back[1]], y)
    by_z = [mixed_own[:, 128 * d : 128 * (d + 1)] for d in range(4)]
    by_z = [by_z[0]] + [along_z(by_z[d], -d) for d in (1, 2, 3)]
    by_z, n_one_low, mixed_own = lax.optimization_barrier((by_z, n_one_low, mixed_own))
    alike = [[(x * 4 + y) * 2 + c for y in range(4)] for x in range(4) for c in range(2)]
    n_all = lax.all_gather(n_one_low, "fsdp", axis=0, tiled=True, axis_index_groups=alike)

    row = (128, 1024)
    before = (by_z[0], by_z[3], by_z[2], by_z[1])
    middle, normed_two = with_out(
        middle_kernel, ((row, F32), (row, BF)), before, ff_all, (tokens, vectors), place
    )
    near_one, near_three = along_z(normed_two, 1), along_z(normed_two, 3)
    far = jnp.concatenate([along_z(near_one[:64], 1), along_z(near_three[64:], 3)], axis=0)
    full_two = [normed_two, near_one, far, near_three]
    near = [0, 1, 3]
    fed, grad_bup = feed_chunks(
        place, [full_two[d] for d in near], [full_grad[d] for d in near], ff_all, vectors, [F32, BF, BF]
    )
    far, fed, grad_bup = lax.optimization_barrier((full_two[2], fed, grad_bup))
    last, more_bup = feed_chunks(place, [far], [full_grad[2]], ff_all, vectors, [BF])
    active, grad_pre, part = zip(fed[0], fed[1], last[0], fed[2])
    arrived = [along_z(part[d], -d) for d in (1, 2, 3)]
    ff_grads = weight_grads(place, full_two, grad_pre, full_grad, active)
    arrived, ff_grads, active = lax.optimization_barrier((arrived, ff_grads, active))
    grad_bup = grad_bup + more_bup
    ff_grads = lax.psum_scatter(ff_grads, "fsdp", scatter_dimension=0, tiled=True)

    heads = ((256, 128), BF)
    grad_middle, middle_low, *grad_mixed, sums = with_out(
        middle_back_kernel,
        ((row, F32), (row, BF), heads, heads, heads, heads, ((4, 1024), F32)),
        (part[0], *arrived),
        ff_all,
        (middle, out_grad, vectors),
        place,
    )
    by_z = [grad_mixed[0]] + [along_z(grad_mixed[d], -d) for d in (1, 2, 3)]
    second, after, second_far, before = with_down(place, active, ff_all, middle_low)
    by_z, middle_low, after, before, second_far = lax.optimization_barrier(
        (by_z, middle_low, after, before, second_far)
    )
    full_middle = [middle_low, along_z(after, 1), along_z(middle_low, 2), along_z(before, -1)]
    grad_heads = jnp.concatenate([by_z[0], by_z[3], by_z[2], by_z[1]], axis=1)
    grads = [piece(grad_heads, y, 64)] + [
        along_y(piece(grad_heads, (y + d) % 4, 64), d) for d in (1, 2, 3)
    ]
    dq, own, away = attend_back(place, msgs, sib, mixed, logs, grads)
    dq, own, away, full_middle = lax.optimization_barrier((dq, own, away, full_middle))
    away = other_core(away)
    sums = jnp.concatenate([sums, grad_bup, jnp.zeros((3, 1024), F32)], axis=0)
    dqkv, mine, away = last_grads(place, dq, own, away, n_all, *full_middle, mixed_own, sums)
    away = other_core(away)
    back = [dqkv[0]] + [along_y(dqkv[d], -d) for d in (1, 2, 3)]
    back, mine, away = lax.optimization_barrier((back, mine, away))
    got = scattered(added(mine, away), along_x, x, 128)
    part, before, after = row_grads(place, *back, attn_all, second_far)
    near = [along_z(before, -1), along_z(after, 1)]
    got, near = lax.optimization_barrier((got, near))
    far = [along_z(near[0][128:], -1), along_z(near[1][128:], 1)]
    got = scattered(total(got).astype(BF), along_y, y, 32)
    got, far = lax.optimization_barrier((got, far))
    out_qkv, out_wout, columns, vectors, out_wup, out_wdown = finish(
        place, got[0], got[2], got[1], got[3], w_qkv, own_vectors, ff_grads
    )
    arrays = (part, *near, *far, tokens, grad_middle, middle)
    arrays += (second, full_middle[1], full_middle[3], vector_rows_all)
    grad_tokens, output = whole_call(
        tokens_kernel, ((row, F32),) * 2, [], 2**28, place, *arrays
    )
    out_wdown, out_wout = out_wdown.T, out_wout.T
    out_bup = vectors[6:7]
    columns = jnp.concatenate([columns[0:1], columns[2:3]], axis=0).reshape(2, 32, 8)
    out_bqv = lax.dynamic_slice_in_dim(columns, f, 1, axis=1)
    pieces = [lax.dynamic_slice_in_dim(vectors, (t + d) % 4 * 8, 8, axis=1) for d in range(4)]
    vectors = pieces[0] + sum(along_z(pieces[d], d) for d in (1, 2, 3))
    return (
        output,
        grad_tokens,
        vectors[0:2],
        vectors[2:4],
        vectors[4:6],
        out_qkv,
        out_bqv,
        out_wout,
        out_wup,
        out_bup,
        out_wdown,
    )


def solution(mesh):
    by_rows = P(("fsdp", "tp"), None)
    by_features = P(None, ("fsdp", "tp"))
    weights = (
        P(None, "fsdp", "tp"),
        P(None, "tp", "fsdp"),
        P("tp", "fsdp"),
        P("fsdp", "tp"),
        P("tp", "fsdp"),
        P("tp", "fsdp"),
    )
    return jax.shard_map(
        local,
        mesh=mesh,
        in_specs=(by_rows, P("fsdp"), by_features, by_features, by_features, *weights, by_rows),
        out_specs=(by_rows, by_rows, by_features, by_features, by_features, *weights),
        check_vma=False,
    )
```

```python
import functools

import jax
import jax.numpy as jnp
from jax import lax
from jax.experimental import pallas as pl
from jax.experimental.pallas import tpu as pltpu
from jax.sharding import PartitionSpec as P

HEAD_DIM = 64
BLOCK = 512
MSG = 208
EPSILON = 1e-05
MASKED = -1e30
BF = jnp.bfloat16
F32 = jnp.float32


def along_y(a, d):
    pairs = [
        ((x * 4 + y) * 2 + c, (x * 4 + (y + d) % 4) * 2 + c)
        for x in range(4)
        for y in range(4)
        for c in range(2)
    ]
    return lax.ppermute(a, "fsdp", pairs)


def along_x(a, d):
    pairs = [
        ((x * 4 + y) * 2 + c, (((x + d) % 4) * 4 + y) * 2 + c)
        for x in range(4)
        for y in range(4)
        for c in range(2)
    ]
    return lax.ppermute(a, "fsdp", pairs)


def other_core(a):
    return lax.ppermute(a, "fsdp", [(i, i ^ 1) for i in range(32)])


def along_z(a, d):
    return lax.ppermute(a, "tp", [(i, (i + d) % 4) for i in range(4)])


def from_all(a, move):
    return [a, move(a, 1), move(a, 2), move(a, 3)]


def in_order(rel, me):
    n = rel[0].shape[0]
    turned = [rel[0], rel[3], rel[2], rel[1]]
    twice = jnp.concatenate(turned + turned[:3], axis=0)
    return lax.dynamic_slice_in_dim(twice, ((4 - me) % 4) * n, 4 * n, axis=0)


def placed_in_order(rel, me):
    n = rel[0].shape[0]
    out = jnp.zeros((4 * n, *rel[0].shape[1:]), rel[0].dtype)
    for d, a in enumerate(rel):
        out = lax.dynamic_update_slice_in_dim(out, a, ((me - d) % 4) * n, axis=0)
    return out


def piece(a, at, n):
    return lax.dynamic_slice_in_dim(a, at * n, n, axis=0)


def added(mine, theirs):
    return (mine.astype(F32) + theirs.astype(F32)).astype(BF)


def scattered(a, move, me, n):
    return [piece(a, me, n)] + [move(piece(a, (me + d) % 4, n), d) for d in (2, 1, 3)]


def total(terms):
    return sum(a.astype(F32) for a in terms)


def halves(v):
    high = lax.reduce_precision(v, 8, 7)
    return high.astype(BF), (v - high).astype(BF)


def normalized(values):
    centred = values - jnp.mean(values, axis=-1, keepdims=True)
    spread = jnp.mean(centred * centred, axis=-1, keepdims=True)
    scale = lax.rsqrt(spread + EPSILON)
    return centred * scale, scale


def norm_back(grad, normed, scale, gain):
    e = grad * gain
    return scale * (
        e
        - jnp.mean(e, axis=-1, keepdims=True)
        - normed * jnp.mean(e * normed, axis=-1, keepdims=True)
    )


def dot(a, b, ca, cb):
    return lax.dot_general(a, b, (((ca,), (cb,)), ((), ())), preferred_element_type=F32)


def unpack(place, msgs, sib, q_s, kt_s, vt_s, start_s, k_s, v_s):
    y, c = place[0], place[1]
    for d in range(4):
        block = lax.rem(y - d + 4, 4) * 2
        msg = msgs[d]
        q_s[d] = msg[0:64, :] * BF(0.125)
        first = msg[192:208, :].astype(F32)
        start_s[d] = first[0:1] * 64.0 + first[1:2]
        k, v = msg[64:128, :], msg[128:192, :]
        kt_s[block + c] = k.T
        vt_s[block + c] = v.T
        k_s[block + c] = k
        v_s[block + c] = v
        k, v = sib[d, 0:64, :], sib[d, 64:128, :]
        kt_s[block + 1 - c] = k.T
        vt_s[block + 1 - c] = v.T
        k_s[block + 1 - c] = k
        v_s[block + 1 - c] = v


def positions(place, axis):
    shape = (BLOCK, 1) if axis == 0 else (1, BLOCK)
    at = lax.broadcasted_iota(jnp.int32, shape, axis)
    chunk = (place[2] - (at >> 7)) & 3
    return ((chunk << 7) + (at & 127)).astype(F32)


def allowed_in(place, start, key_block, mode):
    if mode == 0:
        return None
    key_pos = positions(place, 0)
    allowed = key_pos >= start - (key_block * BLOCK).astype(F32)
    if mode == 2:
        allowed = allowed & (key_pos <= positions(place, 1))
    return allowed


def over_keys(start, block, step):
    low = jnp.min(start).astype(jnp.int32) // BLOCK
    last = jnp.max(start).astype(jnp.int32)

    def body(key_block, carry):
        @pl.when(key_block * BLOCK < last)
        def _():
            step(key_block, 1)

        @pl.when(key_block * BLOCK >= last)
        def _():
            step(key_block, 0)

        return carry

    lax.fori_loop(low, block, body, 0)
    step(block, 2)


def copies(sources, targets, done):
    started = [
        pltpu.make_async_copy(source, target, done.at[i])
        for i, (source, target) in enumerate(zip(sources, targets))
    ]
    for copy in started:
        copy.start()
    return started


def forward_kernel(
    place, m0, m1, m2, m3, sib_far, mixed, l0, l1, l2, l3, logs,
    q_s, kt_s, vt_s, start_s, k_s, v_s, peak_s, total_s, acc_s, msgs, sib, done,
):
    near = [msgs.at[d] for d in range(4)]
    for copy in copies((m0, m1, m2, m3, sib_far), (*near, sib), done):
        copy.wait()
    unpack(place, near, sib, q_s, kt_s, vt_s, start_s, k_s, v_s)

    def queries(d, carry):
        block = lax.rem(place[0] - d + 4, 4) * 2 + place[1]
        start = start_s[d]
        peak_s[...] = jnp.full((1, BLOCK), MASKED, F32)
        total_s[...] = jnp.zeros((1, BLOCK), F32)
        acc_s[...] = jnp.zeros((HEAD_DIM, BLOCK), F32)

        def step(key_block, mode):
            allowed = allowed_in(place, start, key_block, mode)
            halves_at = [slice(0, 256), slice(256, 512)]
            scores = [dot(kt_s[key_block], q_s[d, :, at], 1, 0) for at in halves_at]
            if allowed is not None:
                scores = [
                    jnp.where(allowed[:, at], s, MASKED) for at, s in zip(halves_at, scores)
                ]
            for at, s in zip(halves_at, scores):
                old = peak_s[:, at]
                peak = jnp.maximum(old, jnp.max(s, axis=0, keepdims=True))
                p = jnp.exp(s - peak)
                shrink = jnp.exp(old - peak)
                peak_s[:, at] = peak
                total_s[:, at] = total_s[:, at] * shrink + jnp.sum(p, axis=0, keepdims=True)
                acc_s[:, at] = acc_s[:, at] * shrink + dot(v_s[key_block], p.astype(BF), 1, 0)

        over_keys(start, block, step)
        out = acc_s[...] / total_s[...]
        mixed[d] = out
        logs[d] = peak_s[...] + jnp.log(total_s[...])
        return carry

    lax.fori_loop(0, 4, queries, 0)
    for d, low in enumerate((l0, l1, l2, l3)):
        low[...] = mixed[d].astype(BF)


def backward_kernel(
    place, m0, m1, m2, m3, sib_far, mixed_far, logs_far, g0, g1, g2, g3, dq, own, away,
    q_s, kt_s, vt_s, start_s, k_s, v_s, g_s, dk_s, dv_s, acc_s, msgs, sib, mixed, logs, done,
):
    started = copies(
        (m0, m1, m2, m3, sib_far, mixed_far, logs_far),
        (*[msgs.at[d] for d in range(4)], sib, mixed, logs),
        done,
    )
    for d, g in enumerate((g0, g1, g2, g3)):
        g_s[d] = g[...]
    dk_s[...] = jnp.zeros(dk_s.shape, F32)
    dv_s[...] = jnp.zeros(dv_s.shape, F32)
    for copy in started:
        copy.wait()
    unpack(place, [msgs.at[d] for d in range(4)], sib, q_s, kt_s, vt_s, start_s, k_s, v_s)

    def queries(d, carry):
        block = lax.rem(place[0] - d + 4, 4) * 2 + place[1]
        start = start_s[d]
        log = logs[d]
        grad = g_s[d]
        q = q_s[d]
        delta = jnp.sum(grad.astype(F32) * mixed[d], axis=0, keepdims=True)
        qt = q.T
        gt = grad.T
        acc_s[...] = jnp.zeros((HEAD_DIM, BLOCK), F32)

        def step(key_block, mode):
            allowed = allowed_in(place, start, key_block, mode)
            grads, probs = [], []
            for at in (slice(0, 256), slice(256, 512)):
                p = jnp.exp(dot(kt_s[key_block], q[:, at], 1, 0) - log[:, at])
                if allowed is not None:
                    p = jnp.where(allowed[:, at], p, 0.0)
                dp = dot(vt_s[key_block], grad[:, at], 1, 0)
                grads.append((p * (dp - delta[:, at])).astype(BF))
                probs.append(p.astype(BF))
            ds = jnp.concatenate(grads, axis=1)
            dv_s[key_block] += dot(jnp.concatenate(probs, axis=1), gt, 1, 0)
            dk_s[key_block] += dot(ds, qt, 1, 0)
            acc_s[...] += dot(k_s[key_block], ds, 1, 0)

        over_keys(start, block, step)
        dq[d] = (acc_s[...] * 0.125).astype(BF)
        return carry

    lax.fori_loop(0, 4, queries, 0)
    for d in range(4):
        block = lax.rem(place[0] - d + 4, 4) * 2
        own[d, 0:64, :] = dk_s[block + place[1]].T
        own[d, 64:128, :] = dv_s[block + place[1]].T
        away[d, 0:64, :] = dk_s[block + 1 - place[1]].T.astype(BF)
        away[d, 64:128, :] = dv_s[block + 1 - place[1]].T.astype(BF)


KV_SCRATCH = [
    pltpu.VMEM((4, HEAD_DIM, BLOCK), BF),
    pltpu.VMEM((8, BLOCK, HEAD_DIM), BF),
    pltpu.VMEM((8, BLOCK, HEAD_DIM), BF),
    pltpu.VMEM((4, 1, BLOCK), F32),
    pltpu.VMEM((8, HEAD_DIM, BLOCK), BF),
    pltpu.VMEM((8, HEAD_DIM, BLOCK), BF),
]
PARAMS = pltpu.CompilerParams(vmem_limit_bytes=48 * 1024 * 1024)
FETCHING = pltpu.CompilerParams(vmem_limit_bytes=60 * 1024 * 1024)


def whole_call(kernel, shapes, scratch, flops, place, *arrays, fetched=(), large=False):
    def whole(a):
        return pl.BlockSpec(a.shape, lambda i, rank=len(a.shape): (0,) * rank)

    outs = [jax.ShapeDtypeStruct(*shape) for shape in shapes]
    return pl.pallas_call(
        kernel,
        grid=(1,),
        out_shape=outs,
        in_specs=[pl.BlockSpec(memory_space=pltpu.SMEM)]
        + [
            pl.BlockSpec(memory_space=pl.ANY) if i in fetched else whole(a)
            for i, a in enumerate(arrays)
        ],
        out_specs=[whole(a) for a in outs],
        scratch_shapes=scratch,
        compiler_params=FETCHING if fetched or large else PARAMS,
        cost_estimate=pl.CostEstimate(flops=flops, bytes_accessed=8 * 2**20, transcendentals=0),
    )(place, *arrays)


def attend(place, msgs, sib):
    head = (4, HEAD_DIM, BLOCK)
    scratch = [
        pltpu.VMEM((1, BLOCK), F32),
        pltpu.VMEM((1, BLOCK), F32),
        pltpu.VMEM((HEAD_DIM, BLOCK), F32),
        pltpu.VMEM((4, MSG, BLOCK), BF),
        pltpu.VMEM((4, 2 * HEAD_DIM, BLOCK), BF),
        pltpu.SemaphoreType.DMA((5,)),
    ]
    shapes = ((head, F32), *[((HEAD_DIM, BLOCK), BF)] * 4, ((4, 1, BLOCK), F32))
    scratch = KV_SCRATCH + scratch
    mixed, *low, logs = whole_call(
        forward_kernel, shapes, scratch, 10**10, place, *msgs, sib, fetched=range(5)
    )
    return mixed, low, logs


def attend_back(place, msgs, sib, mixed, logs, grads):
    pair = (4, 2 * HEAD_DIM, BLOCK)
    scratch = [
        pltpu.VMEM((4, HEAD_DIM, BLOCK), BF),
        pltpu.VMEM((8, BLOCK, HEAD_DIM), F32),
        pltpu.VMEM((8, BLOCK, HEAD_DIM), F32),
        pltpu.VMEM((HEAD_DIM, BLOCK), F32),
        pltpu.VMEM((4, MSG, BLOCK), BF),
        pltpu.VMEM(pair, BF),
        pltpu.VMEM((4, HEAD_DIM, BLOCK), F32),
        pltpu.VMEM((4, 1, BLOCK), F32),
        pltpu.SemaphoreType.DMA((7,)),
    ]
    shapes = (((4, HEAD_DIM, BLOCK), BF), (pair, F32), (pair, BF))
    arrays = (*msgs, sib, mixed, logs, *grads)
    scratch = KV_SCRATCH + scratch
    return whole_call(
        backward_kernel, shapes, scratch, 2 * 10**10, place, *arrays, fetched=range(7)
    )


def split_cores(place, mine, away, at, width, result):
    rows = result.reshape(16, 2, 32, width)
    even, odd = rows[:, 0].reshape(512, width), rows[:, 1].reshape(512, width)
    mine[:, at : at + width] = jnp.where(place[1] == 0, even, odd).astype(BF)
    away[:, at : at + width] = jnp.where(place[1] == 0, odd, even).astype(BF)


def weights_kernel(place, *refs):
    normed, grad_pre, grad, active, (out, turned) = (*[refs[i : i + 4] for i in (0, 4, 8, 12)], refs[16:])
    step = pl.program_id(0)
    at = pl.ds(pl.multiple_of((step & 3) * 256, 256), 256)

    def turn(chunks):
        for d, a in enumerate(chunks):
            turned[:, 128 * d : 128 * (d + 1)] = a[...].T

    def columns(chunks):
        return dot(turned[...], jnp.concatenate([a[:, at] for a in chunks], axis=0), 1, 0)

    @pl.when(step == 0)
    def _():
        turn(normed)

    @pl.when(step == 4)
    def _():
        turn(grad)

    @pl.when(step < 4)
    def _():
        out[...] = columns(grad_pre).astype(BF)

    @pl.when(step >= 4)
    def _():
        out[...] = columns(active).astype(BF)


def weight_grads(place, normed, grad_pre, grad, active):
    chunk = pl.BlockSpec((128, 1024), lambda i: (0, 0))
    return pl.pallas_call(
        weights_kernel,
        grid=(8,),
        out_shape=jax.ShapeDtypeStruct((1024, 2048), BF),
        in_specs=[pl.BlockSpec(memory_space=pltpu.SMEM)] + [chunk] * 16,
        out_specs=pl.BlockSpec((1024, 256), lambda i: (0, i)),
        scratch_shapes=[pltpu.VMEM((1024, 512), BF)],
        compiler_params=PARAMS,
        cost_estimate=pl.CostEstimate(flops=4 * 2**30, bytes_accessed=8 * 2**20, transcendentals=0),
    )(place, *normed, *grad_pre, *grad, *active)


def down_kernel(place, a0, a1, a2, a3, down, low, own, after, far, before):
    own[...] = dot(a0[...], down[...], 1, 1)
    far[...] = dot(a2[...], down[...], 1, 1).astype(BF)
    for a, out in ((a3, after), (a1, before)):
        out[:128, :] = low[...]
        out[128:, :] = dot(a[...], down[...], 1, 1).astype(BF)


def with_down(place, chunks, ff_all, low):
    def rows(n):
        return pl.BlockSpec((n, 1024), lambda i: (0, 0))

    return pl.pallas_call(
        down_kernel,
        grid=(1,),
        out_shape=[
            jax.ShapeDtypeStruct((n, 1024), kind)
            for n, kind in ((128, F32), (256, BF), (128, BF), (256, BF))
        ],
        in_specs=[pl.BlockSpec(memory_space=pltpu.SMEM)]
        + [rows(128)] * 4
        + [pl.BlockSpec((1024, 1024), lambda i: (0, 1)), rows(128)],
        out_specs=[rows(128), rows(256), rows(128), rows(256)],
        compiler_params=FETCHING,
        cost_estimate=pl.CostEstimate(flops=2**30, bytes_accessed=8 * 2**20, transcendentals=0),
    )(place, *chunks, ff_all, low)


def feed_kernel(place, *refs, n):
    normed, grad, (up, down, vectors), outs = refs[:n], refs[n : 2 * n], refs[2 * n : 2 * n + 3], refs[2 * n + 3 :]
    rows = jnp.concatenate([a[...] for a in normed], axis=0)
    upstream = jnp.concatenate([a[...] for a in grad], axis=0)
    value, slope = gelu_pair(dot(rows, up[...], 1, 0) + vectors[4:5])
    low = (dot(upstream, down[...], 1, 0) * slope).astype(BF)
    part = dot(low, up[...], 1, 1)
    value = value.astype(BF)
    for i in range(n):
        at = slice(128 * i, 128 * (i + 1))
        active, grad_pre, own = outs[3 * i : 3 * i + 3]
        active[...] = value[at]
        grad_pre[...] = low[at]
        own[...] = part[at].astype(own.dtype)
    outs[3 * n][...] = jnp.sum(low.astype(F32), axis=0, keepdims=True)


def feed_chunks(place, normed, grad, ff_all, vectors, kinds):
    n = len(normed)
    chunk = pl.BlockSpec((128, 1024), lambda i: (0, 0))
    shape = (128, 1024)
    outs = []
    for kind in kinds:
        outs += [jax.ShapeDtypeStruct(shape, k) for k in (BF, BF, kind)]
    *outs, columns = pl.pallas_call(
        functools.partial(feed_kernel, n=n),
        grid=(1,),
        out_shape=outs + [jax.ShapeDtypeStruct((1, 1024), F32)],
        in_specs=[pl.BlockSpec(memory_space=pltpu.SMEM)]
        + [chunk] * (2 * n)
        + [
            pl.BlockSpec((1024, 1024), lambda i: (0, 0)),
            pl.BlockSpec((1024, 1024), lambda i: (0, 1)),
            pl.BlockSpec((8, 1024), lambda i: (0, 0)),
        ],
        out_specs=[chunk] * (3 * n) + [pl.BlockSpec((1, 1024), lambda i: (0, 0))],
        compiler_params=PARAMS,
        cost_estimate=pl.CostEstimate(flops=n * 2**33, bytes_accessed=4 * 2**20, transcendentals=0),
    )(place, *normed, *grad, ff_all, ff_all, vectors)
    return [outs[3 * i : 3 * i + 3] for i in range(n)], columns


def vectors_kernel(place, block, out):
    rows = block[...].astype(F32).T
    out[...] = jnp.concatenate([rows[0:4] + rows[4:8], rows[8:9], rows[9:12]], axis=0)


def vector_rows(place, ff_all):
    return pl.pallas_call(
        vectors_kernel,
        grid=(1,),
        out_shape=jax.ShapeDtypeStruct((8, 1024), F32),
        in_specs=[
            pl.BlockSpec(memory_space=pltpu.SMEM),
            pl.BlockSpec((1024, 128), lambda i: (0, 24)),
        ],
        out_specs=pl.BlockSpec((8, 1024), lambda i: (0, 0)),
        compiler_params=PARAMS,
    )(place, ff_all)


def last_kernel(
    place, dq_far, own_far, away_far, normed, m0, m1, m2, m3, mixed_far, vectors_far,
    b0, b1, b2, b3, mine, away,
    dq, own, other, n_s, m_s, mixed, vectors, done,
):
    blocks = []
    for d in range(4):
        at = pl.multiple_of(lax.rem(place[0] - d + 4, 4) * BLOCK, BLOCK)
        blocks.append(normed.at[pl.ds(at, BLOCK), :])
    started = copies(
        (
            *(dq_far, own_far, away_far, *blocks, m0, m1.at[pl.ds(0, 128), :], m2),
            *(m3.at[pl.ds(0, 128), :], mixed_far, vectors_far),
        ),
        (dq, own, other, *[n_s.at[d] for d in range(4)], *[m_s.at[d] for d in range(4)], mixed, vectors),
        done,
    )
    for copy in started[:3]:
        copy.wait()
    dqkv = (b0, b1, b2, b3)
    weights = jnp.zeros((192, 1024), F32)
    for d in range(4):
        pair = (own[d] + other[d].astype(F32)).astype(BF)
        dqkv[d][...] = jnp.concatenate([dq[d], pair], axis=0)
        started[3 + d].wait()
        weights += dot(dqkv[d][...], n_s[d], 1, 0)
    for copy in started[7:]:
        copy.wait()
    outs = sum(dot(mixed[:, 128 * d : 128 * (d + 1)], m_s[d], 1, 0) for d in range(4))
    split_cores(place, mine, away, 0, 256, outs.T)
    padding = jnp.zeros((64, 1024), F32)
    split_cores(place, mine, away, 384, 256, jnp.concatenate([weights, padding], axis=0).T)
    ones = jnp.ones((8, BLOCK), BF)
    columns = sum(dot(ones, dqkv[d][...], 1, 1) for d in range(4))[0:1]
    pad = jnp.zeros((1, 64), F32)
    columns = [jnp.concatenate([pad, columns[:, 64 * i : 64 * (i + 1)]], axis=1) for i in range(3)]
    row = lax.broadcasted_iota(jnp.int32, (1024, 128), 0) & 31
    small = jnp.concatenate([vectors[...].T, jnp.zeros((1024, 120), F32)], axis=1)
    for i in range(3):
        small += jnp.where(row == i, columns[i], 0.0)
    split_cores(place, mine, away, 256, 128, small)


def last_grads(place, *arrays):
    scratch = [
        pltpu.VMEM((4, HEAD_DIM, BLOCK), BF),
        pltpu.VMEM((4, 2 * HEAD_DIM, BLOCK), F32),
        pltpu.VMEM((4, 2 * HEAD_DIM, BLOCK), BF),
        pltpu.VMEM((4, BLOCK, 1024), BF),
        pltpu.VMEM((4, 128, 1024), BF),
        pltpu.VMEM((256, BLOCK), BF),
        pltpu.VMEM((8, 1024), F32),
        pltpu.SemaphoreType.DMA((13,)),
    ]
    shapes = (((192, BLOCK), BF),) * 4 + (((512, 640), BF),) * 2
    *dqkv, mine, away = whole_call(
        last_kernel, shapes, scratch, 2**31, place, *arrays, fetched=range(10)
    )
    return dqkv, mine, away


def rows_kernel(place, b0, b1, b2, b3, far, second, own, before, after, heads, weights, done):
    places = [pl.multiple_of(lax.rem(place[0] + d, 4) * 192, 64) for d in range(4)]
    started = copies(
        (far, b0, b1, b2, b3, second),
        (weights, *[heads.at[pl.ds(at, 192), :] for at in places], before.at[pl.ds(128, 128), :]),
        done,
    )
    for copy in started[:5]:
        copy.wait()
    own[...] = dot(heads[:, :128].T, weights[:, :768], 1, 1)
    for d, out, at in ((1, before, 0), (2, after, 128), (3, after, 0)):
        rows = heads[:, 128 * d : 128 * (d + 1)].T
        out[at : at + 128, :] = dot(rows, weights[:, :768], 1, 1).astype(BF)
    for copy in started[5:]:
        copy.wait()


def row_grads(place, *arrays):
    shapes = (((128, 1024), F32),) + (((256, 1024), BF),) * 2
    scratch = [
        pltpu.VMEM((768, BLOCK), BF),
        pltpu.VMEM((1024, 896), BF),
        pltpu.SemaphoreType.DMA((6,)),
    ]
    return whole_call(rows_kernel, shapes, scratch, 2**30, place, *arrays, fetched=range(6))


def project_kernel(place, mine, theirs, rows, first, whole, m0, m1, m2, m3, qkv):
    y, c = place[0], place[1]
    for i in range(16):
        at = slice(32 * i, 32 * (i + 1))
        whole[pl.ds(pl.multiple_of(64 * i + 32 * c, 32), 32), :] = mine[at]
        whole[pl.ds(pl.multiple_of(64 * i + 32 - 32 * c, 32), 32), :] = theirs[at]
    bias = jnp.sum(whole[:, 768:].astype(F32).reshape(32, 32, 128), axis=0)
    bias = jnp.concatenate([bias[:6] + bias[6:12], jnp.zeros((2, 128), F32)], axis=0).T
    bias = jnp.concatenate([bias[:, i : i + 1] for i in range(6)], axis=0)
    qkv[...] = (dot(whole[:, :768].T, rows[...], 1, 1) + bias).astype(BF)
    for d, m in enumerate((m0, m1, m2, m3)):
        at = pl.multiple_of(lax.rem(y + d, 4) * 192, 64)
        m[0:192, :] = qkv[pl.ds(at, 192), :]
        m[192:208, :] = first[...]


def project(place, *arrays):
    shapes = (((1024, 896), BF),) + (((MSG, BLOCK), BF),) * 4
    scratch = [pltpu.VMEM((768, BLOCK), BF)]
    whole, *msgs = whole_call(project_kernel, shapes, scratch, 2**30, place, *arrays)
    return whole, msgs


def finish_kernel(
    place, g0, g1, g2, g3, w_qkv, own, ff, qkv, w_out, columns, vectors, up, down, m_s, k_s
):
    got = (g0, g1, g2, g3)
    up[...] = ff[:, :1024].astype(F32)
    down[...] = ff[:, 1024:].astype(F32)
    w_out[...] = total([g[:, :256] for g in got])
    rest = total([g[:, 256:384] for g in got])
    for d, g in enumerate(got):
        head = lax.rem(place[0] - d + 4, 4)
        m_s[head] = g[:, 384:576].astype(F32)
        k_s[head] = g[0:16, 256:384].astype(F32)
    gain, shift = own[:, 0:1], own[:, 2:3]
    gain_sum, shift_sum = jnp.zeros((32, 64), F32), jnp.zeros((32, 64), F32)
    for h in range(4):
        for i in range(3):
            at = slice(64 * h, 64 * (h + 1))
            m, k = m_s[h, :, 64 * i : 64 * (i + 1)], k_s[h, i : i + 1, 64:128]
            w = w_qkv[i, :, at].astype(F32)
            qkv[i, :, at] = gain * m + shift * k
            columns[i : i + 1, at] = k
            gain_sum += w * m
            shift_sum += w * k
    gain_sum = jnp.sum(gain_sum, axis=1, keepdims=True)
    shift_sum = jnp.sum(shift_sum, axis=1, keepdims=True)
    rows = jnp.concatenate(
        [gain_sum, rest[:, 0:1], shift_sum, rest[:, 1:5], jnp.zeros((32, 121), F32)], axis=1
    )
    vectors[...] = rows.T[:8]


def finish(place, *arrays):
    shapes = ((3, 32, 256), (32, 256), (3, 256), (8, 32), (32, 1024), (32, 1024))
    scratch = [pltpu.VMEM((4, 32, 192), F32), pltpu.VMEM((4, 16, 128), F32)]
    return whole_call(
        finish_kernel, [(shape, F32) for shape in shapes], scratch, 2**28, place, *arrays
    )


def middle_kernel(place, x0, x1, x2, x3, out, tokens, vectors, middle, normed):
    mixed = jnp.concatenate([x[...].T for x in (x0, x1, x2, x3)], axis=1)
    rows = tokens[...].astype(F32) + dot(mixed, out[...], 1, 1) + vectors[2:3]
    middle[...] = rows
    normed[...] = (normalized(rows)[0] * vectors[0:1] + vectors[1:2]).astype(BF)


def middle_back_kernel(
    place, part, a1, a2, a3, out, middle, grad, vectors, grad_middle, low, h0, h1, h2, h3, sums
):
    grad_two = part[...] + a1[...].astype(F32) + a2[...].astype(F32) + a3[...].astype(F32)
    normed, scale = normalized(middle[...])
    upstream = grad[...].astype(F32)
    rows = upstream + norm_back(grad_two, normed, scale, vectors[0:1])
    rows_low = rows.astype(BF)
    grad_middle[...] = rows
    low[...] = rows_low
    heads = dot(rows_low, out[...], 1, 0).T.astype(BF)
    for d, h in enumerate((h0, h1, h2, h3)):
        h[...] = heads[256 * d : 256 * (d + 1)]
    terms = (grad_two * normed, grad_two, rows, upstream)
    sums[...] = jnp.concatenate([jnp.sum(a, axis=0, keepdims=True) for a in terms], axis=0)


def tokens_kernel(
    place, part, a1, a3, second_far, rows_far, tokens, grad_middle, middle, second, s1, s3, vectors,
    grad_tokens, output,
):
    near = a1[:128, :].astype(F32) + a3[:128, :].astype(F32)
    normed, scale = normalized(tokens[...].astype(F32))
    grad = part[...] + near + rows_far[...].astype(F32)
    grad_tokens[...] = grad_middle[...] + norm_back(grad, normed, scale, 1.0)
    near = s1[128:, :].astype(F32) + s3[128:, :].astype(F32)
    output[...] = middle[...] + second[...] + near + second_far[...].astype(F32) + vectors[3:4]


def with_out(kernel, shapes, before, ff_all, after, place):
    def whole(a):
        return pl.BlockSpec(a.shape, lambda i, rank=len(a.shape): (0,) * rank)

    outs = [jax.ShapeDtypeStruct(*shape) for shape in shapes]
    return pl.pallas_call(
        kernel,
        grid=(1,),
        out_shape=outs,
        in_specs=[pl.BlockSpec(memory_space=pltpu.SMEM)]
        + [whole(a) for a in before]
        + [pl.BlockSpec((1024, 1024), lambda i: (0, 2))]
        + [whole(a) for a in after],
        out_specs=[whole(a) for a in outs],
        compiler_params=FETCHING,
        cost_estimate=pl.CostEstimate(flops=2**29, bytes_accessed=4 * 2**20, transcendentals=0),
    )(place, *before, ff_all, *after)


def gelu_pair(v):
    root = 0.7978845608028654
    square = v * v
    t = jnp.tanh(root * v * (1.0 + 0.044715 * square))
    half = 0.5 * (1.0 + t)
    slope = half + 0.5 * v * (1.0 - t * t) * (root * (1.0 + 3 * 0.044715 * square))
    return v * half, slope


def local(
    tokens, doc_start, norm_gains, norm_biases, out_biases, w_qkv, b_qv, w_out, w_up, b_up,
    w_down, out_grad,
):
    f = lax.axis_index("fsdp")
    x, y, c = f // 8, (f // 2) % 4, f % 2
    t = lax.axis_index("tp")
    place = jnp.stack([y, c, t]).astype(jnp.int32)

    vectors = jnp.concatenate([norm_gains, norm_biases, out_biases], axis=0).reshape(1, 48)
    vectors = jnp.concatenate(halves(vectors), axis=1)
    packed = jnp.concatenate([w_out.T, jnp.pad(vectors, ((0, 15), (0, 160)))], axis=0)
    qkv_local = w_qkv.reshape(3, 32, 4, 64).transpose(1, 2, 0, 3).reshape(32, 768)
    packed = from_all(packed, along_z)
    out_columns = [p[:32] for p in packed]
    own_vectors = in_order([p[32:33, :96].astype(F32) for p in packed], t)
    own_vectors = (own_vectors[:, :48] + own_vectors[:, 48:]).reshape(4, 6, 8)
    own_vectors = own_vectors.transpose(0, 2, 1).reshape(32, 6)
    gain, shift = own_vectors[:, 0:1], own_vectors[:, 2:3]

    weights = qkv_local.astype(F32)
    bias = jnp.sum(shift * weights, axis=0).reshape(4, 3, 64)
    qv_bias = jnp.stack([b_qv[0], jnp.zeros_like(b_qv[0]), b_qv[1]], axis=1).astype(F32)
    here = (jnp.arange(4)[:, None] == f // 8) & (jnp.arange(64)[None] // 8 == f % 8)
    bias = bias + jnp.where(here[:, None], jnp.tile(qv_bias, (1, 1, 8)), 0.0)
    bias = jnp.concatenate(halves(bias.reshape(6, 128)), axis=0)
    bias = jnp.pad(bias, ((0, 20), (0, 0)))
    by_y = from_all(jnp.concatenate([(gain * weights).astype(BF), bias], axis=1), along_y)
    by_x = from_all(placed_in_order(by_y, y), along_x)

    others = jnp.stack([own_vectors[:, i] for i in (1, 3, 4, 5)], axis=1)
    others = jnp.concatenate([*halves(others), b_up.reshape(32, 1), jnp.zeros((32, 119), BF)], axis=1)
    ff_local = jnp.concatenate([w_up, w_down.T, *out_columns, others], axis=1)
    ff_all = lax.all_gather(ff_local, "fsdp", axis=0, tiled=True)
    out_all = ff_all[:, 2048:3072]

    rows = from_all(tokens, along_z)
    rows, out_grad = lax.optimization_barrier((rows, out_grad))
    full_grad = from_all(out_grad, along_z)
    rows = jnp.concatenate(rows, axis=0)
    n_one, scale_one = normalized(rows.astype(F32))
    n_one_low = n_one.astype(BF)

    first = (doc_start - x * 4096).reshape(4, 128)
    first = jnp.concatenate(
        [lax.dynamic_slice_in_dim(first, (t - d) % 4, 1, axis=0) for d in range(4)], axis=0
    ).reshape(1, BLOCK)
    first = jnp.concatenate([first // 64, first % 64, jnp.zeros((14, BLOCK), jnp.int32)], axis=0)
    first = first.astype(BF)

    by_x = placed_in_order(by_x, x)
    attn_all, msgs = project(place, by_x, other_core(by_x), n_one_low, first)
    msgs = [msgs[0]] + [along_y(msgs[d], d) for d in (1, 2, 3)]
    msgs, full_grad = lax.optimization_barrier((msgs, full_grad))
    sib = other_core(jnp.stack([m[64:192] for m in msgs]))
    mixed, mixed_low, logs = attend(place, msgs, sib)
    vectors = vector_rows(place, ff_all)
    vector_rows_all = vectors

    back = [mixed_low[0]] + [along_y(mixed_low[d], -d) for d in (1, 2, 3)]
    back, vectors = lax.optimization_barrier((back, vectors))
    mixed_own = in_order([back[0], back[3], back[2], back[1]], y)
    by_z = [mixed_own[:, 128 * d : 128 * (d + 1)] for d in range(4)]
    by_z = [by_z[0]] + [along_z(by_z[d], -d) for d in (1, 2, 3)]
    by_z, n_one_low, mixed_own = lax.optimization_barrier((by_z, n_one_low, mixed_own))
    alike = [[(x * 4 + y) * 2 + c for y in range(4)] for x in range(4) for c in range(2)]
    n_all = lax.all_gather(n_one_low, "fsdp", axis=0, tiled=True, axis_index_groups=alike)

    row = (128, 1024)
    before = (by_z[0], by_z[3], by_z[2], by_z[1])
    middle, normed_two = with_out(
        middle_kernel, ((row, F32), (row, BF)), before, ff_all, (tokens, vectors), place
    )
    near_one, near_three = along_z(normed_two, 1), along_z(normed_two, 3)
    far = jnp.concatenate([along_z(near_one[:64], 1), along_z(near_three[64:], 3)], axis=0)
    full_two = [normed_two, near_one, far, near_three]
    near = [0, 1, 3]
    fed, grad_bup = feed_chunks(
        place, [full_two[d] for d in near], [full_grad[d] for d in near], ff_all, vectors, [F32, BF, BF]
    )
    far, fed, grad_bup = lax.optimization_barrier((full_two[2], fed, grad_bup))
    last, more_bup = feed_chunks(place, [far], [full_grad[2]], ff_all, vectors, [BF])
    active, grad_pre, part = zip(fed[0], fed[1], last[0], fed[2])
    arrived = [along_z(part[d], -d) for d in (1, 2, 3)]
    ff_grads = weight_grads(place, full_two, grad_pre, full_grad, active)
    arrived, ff_grads, active = lax.optimization_barrier((arrived, ff_grads, active))
    grad_bup = grad_bup + more_bup
    ff_grads = lax.psum_scatter(ff_grads, "fsdp", scatter_dimension=0, tiled=True)

    heads = ((256, 128), BF)
    grad_middle, middle_low, *grad_mixed, sums = with_out(
        middle_back_kernel,
        ((row, F32), (row, BF), heads, heads, heads, heads, ((4, 1024), F32)),
        (part[0], *arrived),
        ff_all,
        (middle, out_grad, vectors),
        place,
    )
    by_z = [grad_mixed[0]] + [along_z(grad_mixed[d], -d) for d in (1, 2, 3)]
    second, after, second_far, before = with_down(place, active, ff_all, middle_low)
    by_z, middle_low, after, before, second_far = lax.optimization_barrier(
        (by_z, middle_low, after, before, second_far)
    )
    full_middle = [middle_low, along_z(after, 1), along_z(middle_low, 2), along_z(before, -1)]
    grad_heads = jnp.concatenate([by_z[0], by_z[3], by_z[2], by_z[1]], axis=1)
    grads = [piece(grad_heads, y, 64)] + [
        along_y(piece(grad_heads, (y + d) % 4, 64), d) for d in (1, 2, 3)
    ]
    dq, own, away = attend_back(place, msgs, sib, mixed, logs, grads)
    dq, own, away, full_middle = lax.optimization_barrier((dq, own, away, full_middle))
    away = other_core(away)
    sums = jnp.concatenate([sums, grad_bup, jnp.zeros((3, 1024), F32)], axis=0)
    dqkv, mine, away = last_grads(place, dq, own, away, n_all, *full_middle, mixed_own, sums)
    away = other_core(away)
    back = [dqkv[0]] + [along_y(dqkv[d], -d) for d in (1, 2, 3)]
    back, mine, away = lax.optimization_barrier((back, mine, away))
    got = scattered(added(mine, away), along_x, x, 128)
    part, before, after = row_grads(place, *back, attn_all, second_far)
    near = [along_z(before, -1), along_z(after, 1)]
    got, near = lax.optimization_barrier((got, near))
    far = [along_z(near[0][128:], -1), along_z(near[1][128:], 1)]
    got = scattered(total(got).astype(BF), along_y, y, 32)
    got, far = lax.optimization_barrier((got, far))
    out_qkv, out_wout, columns, vectors, out_wup, out_wdown = finish(
        place, got[0], got[2], got[1], got[3], w_qkv, own_vectors, ff_grads
    )
    arrays = (part, *near, *far, tokens, grad_middle, middle)
    arrays += (second, full_middle[1], full_middle[3], vector_rows_all)
    grad_tokens, output = whole_call(
        tokens_kernel, ((row, F32),) * 2, [], 2**28, place, *arrays, large=True
    )
    out_wdown, out_wout = out_wdown.T, out_wout.T
    out_bup = vectors[6:7]
    columns = jnp.concatenate([columns[0:1], columns[2:3]], axis=0).reshape(2, 32, 8)
    out_bqv = lax.dynamic_slice_in_dim(columns, f, 1, axis=1)
    pieces = [lax.dynamic_slice_in_dim(vectors, (t + d) % 4 * 8, 8, axis=1) for d in range(4)]
    vectors = pieces[0] + sum(along_z(pieces[d], d) for d in (1, 2, 3))
    return (
        output,
        grad_tokens,
        vectors[0:2],
        vectors[2:4],
        vectors[4:6],
        out_qkv,
        out_bqv,
        out_wout,
        out_wup,
        out_bup,
        out_wdown,
    )


def solution(mesh):
    by_rows = P(("fsdp", "tp"), None)
    by_features = P(None, ("fsdp", "tp"))
    weights = (
        P(None, "fsdp", "tp"),
        P(None, "tp", "fsdp"),
        P("tp", "fsdp"),
        P("fsdp", "tp"),
        P("tp", "fsdp"),
        P("tp", "fsdp"),
    )
    return jax.shard_map(
        local,
        mesh=mesh,
        in_specs=(by_rows, P("fsdp"), by_features, by_features, by_features, *weights, by_rows),
        out_specs=(by_rows, by_rows, by_features, by_features, by_features, *weights),
        check_vma=False,
    )
```
